32 devices in a mesh: expert: 8 (over z, x), replica: 4 (over y, core).
Axes of the slice: x: 2, y: 2, z: 4, core: 2. Of those that a mesh axis runs over, the one named last changes fastest.
Arguments:
- x_tokens: bfloat16 [4096, 2048], P(('expert', 'replica')), may hold values from -6 to 6
- d_out: bfloat16 [4096, 2048], P(('expert', 'replica')), may hold values from -3 to 3
- expert_ids: int32 [4096, 2], P(('expert', 'replica')), may hold values from 0 to 7, all different within a row; in each aligned block of 128 rows (0 to 127, 128 to 255, ...) at most 64 rows name the same one
- combine: float32 [4096, 2], P(('expert', 'replica')), may hold values from 0.1 to 1
- w_stack: bfloat16 [8, 1408, 6144], P('expert'), may hold values from -0.125 to 0.125
Outputs:
- d_tokens: bfloat16 [4096, 2048], P(('expert', 'replica'))
- g_stack: bfloat16 [8, 1408, 6144], P('expert', 'replica')
The draws below stay inside these ranges and needn't reach their ends.
Inputs may be any that keep to these rules, and one draw needn't show every extreme that they name: `expert_ids`: in the tokens of one device (aligned blocks of 128 tokens) each expert is named by at most 64 routes, and by exactly 64 in some block; a token's 2 experts differ.
All inputs are finite; a program needn't handle non-finite values.
Results may differ from the reference program's by a relative error of at most 0.013.
Values may be sent and summed in bfloat16 or wider, within the bound.
No kernel may reach another device: no remote copies, remote signals or barrier semaphores. Data moves between devices by JAX's collectives and lax.ppermute only.
A program may use at most 128 MiB of HBM per device.

```python
import math
import jax
import jax.numpy as jnp
import numpy as np
from jax import lax

D = 2048
FF = 1408
TOK_DEV = 128
TOPW = 2
EXPERTS = 8
CAP = 64
TOKENS = 4096
N_EXPERT = 8
N_REPLICA = 4


def block_scale(key, shape, cuts, least, top_value):
    gain = 1.0
    for position, blocks in cuts:
        steps = jax.random.uniform(jax.random.fold_in(jax.random.fold_in(key, 6), position), (blocks,), jnp.float32, least / len(cuts), top_value / len(cuts))
        gain = gain * jnp.repeat(jnp.exp(steps), shape[position] // blocks).reshape((-1,) + (1,) * (len(shape) - 1 - position))
    return gain


def assign_block(own_key, own, number, rows, amount, top, limit, slope):
    sequence = jax.random.permutation(own_key, amount)
    crowded, common = portions_of(amount, rows * top, limit, slope, True), portions_of(amount, rows * top, limit, slope, False)
    places = jnp.arange(amount)

    def named(tallies, rotation):
        used = int((tallies > 0).sum())
        fixed = max(1, used // 4)
        shifted = fixed + (places - fixed + rotation * (used - fixed)) % max(1, amount - fixed)
        return jnp.zeros((amount,), jnp.int32).at[sequence[jnp.where(places < fixed, places, shifted)]].set(jnp.asarray(tallies, jnp.int32))

    tallies = jnp.where(number % 4 == 0, named(crowded, number // 4), named(common, number - number // 4 - 1))
    mixed = jax.random.permutation(jax.random.fold_in(own, 3), amount)
    source_of, taker = mixed[0:amount // 2 * 2:2], mixed[1:amount // 2 * 2:2]
    room = jnp.minimum(tallies[source_of] - 1, limit - tallies[taker]) // 2
    room = jnp.where((source_of == sequence[0]) | (taker == sequence[0]) | (tallies[taker] == 0), 0, jnp.maximum(room, 0))
    shifted = jax.random.randint(jax.random.fold_in(own, 4), (amount // 2,), 0, 1 << 20) % (room + 1)
    tallies = tallies.at[source_of].add(-shifted).at[taker].add(shifted)
    items = jnp.searchsorted(jnp.cumsum(tallies), jnp.arange(rows * top), side="right").astype(jnp.int32)
    table = items.reshape(top, rows).T
    table = table[jax.random.permutation(jax.random.fold_in(own, 1), rows)]
    rotation = jax.random.randint(jax.random.fold_in(own, 2), (rows, 1), 0, top)
    return jnp.take_along_axis(table, (jnp.arange(top)[None, :] + rotation) % top, axis=1)


def portions_of(count, total, bound, lean, full):
    weights = [(1 << 20) // math.isqrt(standing ** lean) + 1 for standing in range(1, count + 1)]
    largest = bound if full else min(bound, max(-(-total // count), total * weights[0] // sum(weights)))
    least = 1 if total - largest >= count - 1 else 0
    holding, surplus = [largest] + [least] * (count - 1), total - largest - least * (count - 1)
    while surplus > 0:
        movable = [i for i in range(1, count) if holding[i] < largest] or [i for i in range(1, count) if holding[i] < bound]
        whole, budget = sum([weights[i] for i in movable]), surplus
        for i in movable:
            extra = min(bound - holding[i], max(1, budget * weights[i] // whole), surplus)
            holding[i] = holding[i] + extra
            surplus = surplus - extra
    return np.array(holding)


def noise(own_key, shape, spread, most, shards=(), kind=jnp.bfloat16):
    drawn = jax.random.normal(own_key, shape, jnp.float32) * spread
    if len(shards) > 0:
        drawn = block_scale(own_key, shape, shards, -0.22, 0.18) * drawn
    return jnp.clip(drawn, min=-most, max=most).astype(kind)


def setup_inputs(seed: int = 0) -> dict:
    seeds = jax.random.split(jax.random.key(seed), 6)
    x_tokens = noise(seeds[0], (TOKENS, D), 1.0, 6.0, ((0, 32),))
    d_out = noise(seeds[1], (TOKENS, D), 0.5, 3.0, ((0, 32),))
    expert_ids_keys = jax.random.split(jax.random.fold_in(seeds[2], 1), TOKENS // TOK_DEV)
    expert_ids_turns = jax.random.permutation(jax.random.fold_in(seeds[2], 3), TOKENS // TOK_DEV)
    expert_ids = jax.vmap(lambda own, number: assign_block(jax.random.fold_in(seeds[2], 2), own, number, TOK_DEV, EXPERTS, TOPW, CAP, 2))(expert_ids_keys, expert_ids_turns).reshape((TOKENS, TOPW))
    combine = jnp.clip(jnp.exp(math.log(1.0) - 2.3025851 * jax.random.uniform(seeds[3], (TOKENS, TOPW), jnp.float32) ** block_scale(seeds[3], (TOKENS, TOPW), ((0, 32),), -0.2, 0.2)), 0.1, 1.0)
    w_stack = noise(seeds[4], (EXPERTS, FF, 3 * D), D ** -0.5, 0.125, ((0, 8),))
    return {"x_tokens": x_tokens, "d_out": d_out, "expert_ids": expert_ids, "combine": combine, "w_stack": w_stack}


def reference(x_tokens, d_out, expert_ids, combine, w_stack):
    block_count = N_EXPERT * N_REPLICA
    route_count = TOK_DEV * TOPW
    slot_total = N_EXPERT * CAP
    route_ids = expert_ids.reshape(block_count, route_count)
    member = (route_ids[:, :, None] == jnp.arange(EXPERTS, dtype=jnp.int32)[None, None, :]).astype(jnp.int32)
    slot_rank = jnp.sum((jnp.cumsum(member, axis=1) - 1) * member, axis=2).astype(jnp.int32)
    block_index = jnp.arange(block_count, dtype=jnp.int32)[:, None]
    slot_target = ((route_ids * block_count + block_index) * CAP + slot_rank).astype(jnp.int32)
    slot_table = jnp.full((EXPERTS * block_count * CAP,), -1, jnp.int32)
    slot_table = slot_table.at[slot_target.reshape(-1)].set(jnp.arange(block_count * route_count, dtype=jnp.int32))
    slot_table = slot_table.reshape(EXPERTS, N_EXPERT, N_REPLICA, CAP).transpose(0, 2, 1, 3)
    slot_table = slot_table.reshape(EXPERTS, N_REPLICA * slot_total)
    dy_routes = (combine.reshape(-1, 1) * jnp.repeat(d_out, TOPW, axis=0).astype(jnp.float32)).astype(jnp.bfloat16)
    x_routes = jnp.repeat(x_tokens, TOPW, axis=0)

    def one_expert(dx_total, inputs):
        routes, weights = inputs
        is_valid = routes >= 0
        route_index = jnp.maximum(routes, 0).astype(jnp.int32)
        row_block = jnp.where(is_valid[:, None], x_routes[route_index], jnp.zeros((), jnp.bfloat16))
        grads_in = jnp.where(is_valid[:, None], dy_routes[route_index], jnp.zeros((), jnp.bfloat16))
        w_gate = weights[:, :D]
        w_up = weights[:, D:2 * D]
        w_down = weights[:, 2 * D:]
        gate_pre = jnp.dot(row_block, w_gate.T, preferred_element_type=jnp.float32)
        up_pre = jnp.dot(row_block, w_up.T, preferred_element_type=jnp.float32)
        d_hidden = jnp.dot(grads_in, w_down.T, preferred_element_type=jnp.float32)
        gate_sigmoid = jax.nn.sigmoid(gate_pre)
        gate_act = gate_pre * gate_sigmoid
        hidden_act = (gate_act * up_pre).astype(jnp.bfloat16)
        d_up = (d_hidden * gate_act).astype(jnp.bfloat16)
        d_gate = (d_hidden * up_pre * gate_sigmoid * (1.0 + gate_pre * (1.0 - gate_sigmoid))).astype(jnp.bfloat16)
        dx_rows = jnp.dot(d_gate, w_gate, preferred_element_type=jnp.float32) + jnp.dot(d_up, w_up, preferred_element_type=jnp.float32)
        dx_rows = jnp.where(is_valid[:, None], dx_rows, jnp.zeros((), jnp.float32))
        dx_total = dx_total.at[route_index].add(dx_rows)
        x_groups = row_block.reshape(N_REPLICA, slot_total, D).astype(jnp.float32)
        dy_groups = grads_in.reshape(N_REPLICA, slot_total, D).astype(jnp.float32)
        gate_groups = d_gate.reshape(N_REPLICA, slot_total, FF).astype(jnp.float32)
        up_groups = d_up.reshape(N_REPLICA, slot_total, FF).astype(jnp.float32)
        act_groups = hidden_act.reshape(N_REPLICA, slot_total, FF).astype(jnp.float32)
        partial_value = jnp.concatenate([
            jnp.einsum("grj,grd->gjd", gate_groups, x_groups),
            jnp.einsum("grj,grd->gjd", up_groups, x_groups),
            jnp.einsum("grj,grd->gjd", act_groups, dy_groups)], axis=2)
        rounded = lax.optimization_barrier(partial_value.astype(jnp.bfloat16)).astype(jnp.float32)
        grad_stack = jnp.sum(rounded, axis=0).astype(jnp.bfloat16)
        return dx_total, grad_stack

    dx_start = jnp.zeros((TOKENS * TOPW, D), jnp.float32)
    dx_all, g_stack = lax.scan(one_expert, dx_start, (slot_table, w_stack))
    d_tokens = jnp.sum(dx_all.reshape(TOKENS, TOPW, D), axis=1).astype(jnp.bfloat16)
    return d_tokens, g_stack
```

```python
import functools

import jax
import jax.numpy as jnp
from jax import lax
from jax.experimental import pallas as pl
from jax.experimental.pallas import tpu as pltpu
from jax.sharding import PartitionSpec as P

BF16 = jnp.bfloat16
F32 = jnp.float32
RING = (0, 1, 3, 2)
VMEM_LIMIT = 56 * 1024 * 1024


def params():
    return pltpu.CompilerParams(vmem_limit_bytes=VMEM_LIMIT)


def whole_vmem():
    return pl.BlockSpec(memory_space=pltpu.VMEM)


def smem():
    return pl.BlockSpec(memory_space=pltpu.SMEM)


def placing_of(place_ref, meta_ref, column_count, capacity):
    tokens = meta_ref.shape[1]
    base, own = place_ref[0], place_ref[1]
    id_first, id_second = meta_ref[0:1, :], meta_ref[1:2, :]
    scale_first, scale_second = meta_ref[2:3, :], meta_ref[3:4, :]
    row = lax.broadcasted_iota(jnp.int32, (16, tokens), 0)
    expert = (base + jnp.bitwise_xor(row, own)).astype(F32)
    first = id_first == expert
    member = jnp.where(first | (id_second == expert), 1.0, 0.0)
    scale = jnp.where(first, scale_first, scale_second)
    earlier = lax.broadcasted_iota(jnp.int32, (tokens, tokens), 0)
    later = lax.broadcasted_iota(jnp.int32, (tokens, tokens), 1)
    before = jnp.where(earlier < later, 1.0, 0.0).astype(BF16)
    rank = jnp.dot(member.astype(BF16), before, preferred_element_type=F32)
    rank = jnp.where(member > 0.0, rank, -1.0)
    slot = lax.broadcasted_iota(jnp.int32, (capacity, tokens), 0).astype(F32)
    hits, scales = [], []
    for d in range(column_count):
        hit = jnp.where(rank[d : d + 1, :] == slot, 1.0, 0.0)
        hits.append(hit)
        scales.append(jnp.sum(hit * scale[d : d + 1, :], axis=1, keepdims=True))
    return jnp.concatenate(hits, axis=0), jnp.concatenate(scales, axis=0)


def select_kernel(column_count, capacity, scaled, place_ref, meta_ref, rows_ref, *out_refs):
    hits, scales = placing_of(place_ref, meta_ref, column_count, capacity)
    picked = jnp.dot(hits.astype(BF16), rows_ref[...], preferred_element_type=F32)
    if scaled:
        picked = picked * scales
    picked = picked.astype(BF16)
    for d in range(column_count):
        out_refs[d][...] = picked[d * capacity : (d + 1) * capacity, :]


def select(place, meta, rows, column_count, capacity, scaled):
    tokens, width = rows.shape
    return pl.pallas_call(
        functools.partial(select_kernel, column_count, capacity, scaled),
        out_shape=[jax.ShapeDtypeStruct((capacity, width), BF16)] * column_count,
        in_specs=[smem(), whole_vmem(), whole_vmem()],
        out_specs=[whole_vmem()] * column_count,
        compiler_params=params(),
        cost_estimate=pl.CostEstimate(
            flops=2 * column_count * capacity * tokens * width,
            bytes_accessed=4 * tokens * width,
            transcendentals=0,
        ),
        name="select_scaled" if scaled else "select",
    )(place, meta, rows)


def merge_kernel(column_count, capacity, has_carry, place_ref, meta_ref, *refs):
    parts = refs[:column_count]
    out_ref = refs[-1]
    hits, _ = placing_of(place_ref, meta_ref, column_count, capacity)
    slots = jnp.concatenate([part[...] for part in parts], axis=0)
    total = lax.dot_general(
        hits.astype(BF16), slots, (((0,), (0,)), ((), ())), preferred_element_type=F32
    )
    if has_carry:
        total = total + refs[column_count][...].astype(F32)
    out_ref[...] = total.astype(BF16)


def merge(place, meta, parts, carry):
    column_count, (capacity, width) = len(parts), parts[0].shape
    tokens = meta.shape[1]
    operands = [place, meta, *parts] + ([] if carry is None else [carry])
    return pl.pallas_call(
        functools.partial(merge_kernel, column_count, capacity, carry is not None),
        out_shape=jax.ShapeDtypeStruct((tokens, width), BF16),
        in_specs=[smem()] + [whole_vmem()] * (len(operands) - 1),
        out_specs=whole_vmem(),
        compiler_params=params(),
        cost_estimate=pl.CostEstimate(
            flops=2 * column_count * capacity * tokens * width,
            bytes_accessed=6 * tokens * width,
            transcendentals=0,
        ),
        name="merge",
    )(*operands)


def expert_kernel(chunk_count, capacity, half_ref, *refs):
    x_refs, refs = refs[:chunk_count], refs[chunk_count:]
    dy_refs, refs = refs[:chunk_count], refs[chunk_count:]
    w_ref, send_ref, keep_ref, hid_ref = refs[:4]
    dx_refs, (x_all, dy_all, acc) = refs[4:-3], refs[-3:]
    step = pl.program_id(0)
    width = x_all.shape[1]
    chunk_rows = x_refs[0].shape[0]

    @pl.when(step == 0)
    def _():
        for i in range(chunk_count):
            x_all[i * chunk_rows : (i + 1) * chunk_rows, :] = x_refs[i][...]
            dy_all[i * chunk_rows : (i + 1) * chunk_rows, :] = dy_refs[i][...]

    last = (((1,), (1,)), ((), ()))
    first = (((0,), (0,)), ((), ()))
    x, dy = x_all[...], dy_all[...]
    gate = lax.dot_general(w_ref[0, :, :width], x, last, preferred_element_type=F32)
    up = lax.dot_general(w_ref[0, :, width : 2 * width], x, last, preferred_element_type=F32)
    d_hidden = lax.dot_general(w_ref[0, :, 2 * width :], dy, last, preferred_element_type=F32)
    sig = jax.nn.sigmoid(gate)
    act = gate * sig
    hid_ref[0] = (act * up).astype(BF16)
    d_up = (d_hidden * act).astype(BF16)
    d_gate = (d_hidden * up * sig * (1.0 + gate * (1.0 - sig))).astype(BF16)

    @pl.when(step == 0)
    def _():
        send_ref[0] = d_gate
        send_ref[1] = d_up

    @pl.when(step == 1)
    def _():
        keep_ref[0] = d_gate
        keep_ref[1] = d_up

    part = lax.dot_general(
        d_gate, w_ref[0, :, :width], first, preferred_element_type=F32
    ) + lax.dot_general(
        d_up, w_ref[0, :, width : 2 * width], first, preferred_element_type=F32
    )

    @pl.when(step == 0)
    def _():
        acc[...] = part

    @pl.when(step == 1)
    def _():
        total = (acc[...] + part).astype(BF16)
        for i in range(len(dx_refs)):
            dx_refs[i][...] = total[i * capacity : (i + 1) * capacity, :]


def expert(half, x_chunks, dy_chunks, w_stack, capacity):
    chunk_count = len(x_chunks)
    chunk_rows, width = x_chunks[0].shape
    rows = chunk_count * chunk_rows
    hidden = w_stack.shape[1]
    part = hidden // 2
    chunk_spec = pl.BlockSpec((chunk_rows, width), lambda j, h: (0, 0))
    pair_spec = pl.BlockSpec((2, part, rows), lambda j, h: (0, 0, 0))

    def half_of(j, h):
        return jnp.bitwise_xor(h[0], 1 - j)

    piece_count = rows // capacity
    outs = pl.pallas_call(
        functools.partial(expert_kernel, chunk_count, capacity),
        grid_spec=pltpu.PrefetchScalarGridSpec(
            num_scalar_prefetch=1,
            grid=(2,),
            in_specs=[chunk_spec] * (2 * chunk_count)
            + [pl.BlockSpec((1, part, 3 * width), lambda j, h: (0, half_of(j, h), 0))],
            out_specs=[
                pair_spec,
                pair_spec,
                pl.BlockSpec((1, part, rows), lambda j, h: (half_of(j, h), 0, 0)),
            ]
            + [pl.BlockSpec((capacity, width), lambda j, h: (0, 0))] * piece_count,
            scratch_shapes=[
                pltpu.VMEM((rows, width), BF16),
                pltpu.VMEM((rows, width), BF16),
                pltpu.VMEM((rows, width), F32),
            ],
        ),
        out_shape=[
            jax.ShapeDtypeStruct((2, part, rows), BF16),
            jax.ShapeDtypeStruct((2, part, rows), BF16),
            jax.ShapeDtypeStruct((2, part, rows), BF16),
        ]
        + [jax.ShapeDtypeStruct((capacity, width), BF16)] * piece_count,
        compiler_params=params(),
        cost_estimate=pl.CostEstimate(
            flops=10 * rows * width * hidden,
            bytes_accessed=6 * width * hidden + 6 * rows * width + 6 * rows * hidden,
            transcendentals=rows * hidden,
        ),
        name="expert",
    )(half, *x_chunks, *dy_chunks, w_stack)
    return outs[0], outs[1], outs[2], outs[3:]


def grad_kernel(act_count, row_count, add_axes, pick_ref, *refs):
    acts, refs = refs[:act_count], refs[act_count:]
    rows, refs = refs[:row_count], refs[row_count:]
    adds, out_ref = refs[: len(add_axes)], refs[-1]
    left = jnp.concatenate([ref[0] for ref in acts], axis=1)
    right = jnp.concatenate([ref[...] for ref in rows], axis=0)
    total = jnp.dot(left, right, preferred_element_type=F32)
    for ref, axes in zip(adds, add_axes):
        total = total + (ref[...] if axes == 2 else ref[0]).astype(F32)
    out_ref[...] = total.astype(BF16).reshape(out_ref.shape)


def grad(pick, leads, acts, rows, adds, out_shape, first_column, into=None, name="grad"):
    own = acts[0].shape[1] // 2
    width = rows[0].shape[1]
    tile = min(1024, width)
    tiles = width // tile
    lead_count = 1 if leads is None else leads
    stacked = len(out_shape) == 3

    def lead_of(i, pick_ref):
        return pick_ref[0] if leads is None else i

    in_specs = [
        pl.BlockSpec((1, own, act.shape[2]), lambda i, n, s: (lead_of(i, s), s[1], 0))
        for act in acts
    ] + [pl.BlockSpec((row.shape[0], tile), lambda i, n, s: (0, n)) for row in rows]
    operands = list(acts) + list(rows)
    add_axes = []
    for add in adds:
        operands.append(add)
        add_axes.append(add.ndim)
        if add.ndim == 3:
            in_specs.append(
                pl.BlockSpec((1, own, tile), lambda i, n, s: (lead_of(i, s), 0, n))
            )
        else:
            in_specs.append(pl.BlockSpec((own, tile), lambda i, n, s: (0, i * tiles + n)))
    aliases = {}
    kernel = functools.partial(grad_kernel, len(acts), len(rows), tuple(add_axes))
    if into is not None:
        operands.append(into)
        in_specs.append(pl.BlockSpec(memory_space=pl.ANY))
        aliases = {len(operands): 0}
        inner = kernel

        def kernel(pick_ref, *refs):
            inner(pick_ref, *refs[:-2], refs[-1])

    if stacked:
        out_spec = pl.BlockSpec((1, own, tile), lambda i, n, s: (i, 0, n))
    else:
        out_spec = pl.BlockSpec(
            (own, tile), lambda i, n, s: (0, first_column // tile + i * tiles + n)
        )
    depth = sum(act.shape[2] for act in acts)
    return pl.pallas_call(
        kernel,
        grid_spec=pltpu.PrefetchScalarGridSpec(
            num_scalar_prefetch=1,
            grid=(lead_count, tiles),
            in_specs=in_specs,
            out_specs=out_spec,
        ),
        out_shape=jax.ShapeDtypeStruct(out_shape, BF16),
        input_output_aliases=aliases,
        compiler_params=params(),
        cost_estimate=pl.CostEstimate(
            flops=2 * lead_count * own * depth * width,
            bytes_accessed=2 * depth * width + 2 * lead_count * own * (depth + 2 * width),
            transcendentals=0,
        ),
        name=name,
    )(pick, *operands)


def body(x_tokens, d_out, expert_ids, combine, w_stack):
    tokens, width = x_tokens.shape
    experts = lax.axis_size("expert")
    replicas = lax.axis_size("replica")
    plane_count = len(RING)
    columns = experts // plane_count
    capacity = 2 * tokens * expert_ids.shape[1] // experts
    hidden = w_stack.shape[1]
    own_rows = hidden // replicas

    position = lax.axis_index("expert")
    replica = lax.axis_index("replica")
    plane, column = position // columns, position % columns
    high, low = replica // 2, replica % 2
    place = jnp.stack([plane * columns, column]).astype(jnp.int32)
    half = high.reshape(1).astype(jnp.int32)

    follower = {RING[i]: RING[(i + 1) % plane_count] for i in range(plane_count)}
    ring_pairs = [
        (p * columns + c, follower[p] * columns + c)
        for p in range(plane_count)
        for c in range(columns)
    ]

    def along_ring(value):
        return lax.ppermute(value, "expert", ring_pairs)

    def across_columns(value, d):
        pairs = [
            (p * columns + c, p * columns + (c ^ d))
            for p in range(plane_count)
            for c in range(columns)
        ]
        return lax.ppermute(value, "expert", pairs)

    def across_replicas(value, d):
        return lax.ppermute(value, "replica", [(r, r ^ d) for r in range(replicas)])

    meta = jnp.concatenate([expert_ids.T.astype(F32), combine.T], axis=0)
    metas, x_blocks, d_blocks = [meta], [x_tokens], [d_out]
    for _ in range(plane_count - 1):
        metas.append(along_ring(metas[-1]))
        x_blocks.append(along_ring(x_blocks[-1]))
        d_blocks.append(along_ring(d_blocks[-1]))

    def chunk_of(block, meta_rows, scaled):
        picked = select(place, meta_rows, block, columns, capacity, scaled)
        arrived = [picked[0]] + [across_columns(picked[d], d) for d in range(1, columns)]
        return jnp.concatenate(arrived, axis=0)

    x_chunks, dy_chunks, x_other = [], [], []
    for s in range(plane_count):
        x_chunks.append(chunk_of(x_blocks[s], metas[s], False))
        x_other.append(across_replicas(x_chunks[s], 2))
        dy_chunks.append(chunk_of(d_blocks[s], metas[s], True))

    keeps, sends, hids, pieces = [], [], [], []
    group = 2
    for g in range(0, plane_count, group):
        send, keep, hid, dx = expert(
            half, x_chunks[g : g + group], dy_chunks[g : g + group], w_stack, capacity
        )
        keeps.append(keep)
        sends.append(across_replicas(send, 2))
        hids.append(hid)
        pieces.extend(dx)

    def dx_parts(s):
        mine = pieces[s * columns : (s + 1) * columns]
        return [mine[0]] + [across_columns(mine[d], d) for d in range(1, columns)]

    carry = None
    for s in range(1, plane_count):
        carry = along_ring(merge(place, metas[s], dx_parts(s), carry))
    d_tokens = merge(place, metas[0], dx_parts(0), carry)

    def pick(lead, rows):
        return jnp.stack([lead, rows]).astype(jnp.int32)

    down_shape = (2, own_rows, width)
    down_cores = across_replicas(
        grad(pick(high, 1 - low), 2, hids, dy_chunks, [], down_shape, 0, name="grad_down_core"), 1
    )
    down_y = across_replicas(
        grad(
            pick(1 - high, low), None, hids, dy_chunks, [down_cores], (own_rows, width), 0,
            name="grad_down_y",
        ),
        2,
    )
    acts, rows = keeps + sends, x_chunks + x_other
    x_cores = across_replicas(
        grad(pick(high, 1 - low), 2, acts, rows, [], (own_rows, 2 * width), 0, name="grad_x_core"),
        1,
    )
    g_rows = grad(
        pick(high, low), 2, acts, rows, [x_cores], (own_rows, 3 * width), 0, name="grad_x_own"
    )
    g_rows = grad(
        pick(high, low), None, hids, dy_chunks, [down_cores, down_y], (own_rows, 3 * width),
        2 * width, into=g_rows, name="grad_down_own",
    )
    return d_tokens, g_rows[None]


def solution(mesh):
    return jax.shard_map(
        body,
        mesh=mesh,
        in_specs=(
            P(("expert", "replica"), None),
            P(("expert", "replica"), None),
            P(("expert", "replica"), None),
            P(("expert", "replica"), None),
            P("expert", None, None),
        ),
        out_specs=(P(("expert", "replica"), None), P("expert", "replica", None)),
        check_vma=False,
    )
```

```python
import functools

import jax
import jax.numpy as jnp
from jax import lax
from jax.experimental import pallas as pl
from jax.experimental.pallas import tpu as pltpu
from jax.sharding import PartitionSpec as P

BF16 = jnp.bfloat16
F32 = jnp.float32
RING = (0, 1, 3, 2)
VMEM_LIMIT = 56 * 1024 * 1024


def params():
    return pltpu.CompilerParams(vmem_limit_bytes=VMEM_LIMIT)


def smem():
    return pl.BlockSpec(memory_space=pltpu.SMEM)


def small_cost():
    return pl.CostEstimate(flops=1024, bytes_accessed=1024, transcendentals=0)


def tile_of(width, most):
    return most if width % most == 0 else width


def placing_of(place_ref, meta_ref, column_count, capacity):
    tokens = meta_ref.shape[1]
    base, own = place_ref[0], place_ref[1]
    id_first, id_second = meta_ref[0:1, :], meta_ref[1:2, :]
    scale_first, scale_second = meta_ref[2:3, :], meta_ref[3:4, :]
    row = lax.broadcasted_iota(jnp.int32, (16, tokens), 0)
    expert = (base + jnp.bitwise_xor(row, own)).astype(F32)
    first = id_first == expert
    member = jnp.where(first | (id_second == expert), 1.0, 0.0)
    scale = jnp.where(first, scale_first, scale_second)
    earlier = lax.broadcasted_iota(jnp.int32, (tokens, tokens), 0)
    later = lax.broadcasted_iota(jnp.int32, (tokens, tokens), 1)
    before = jnp.where(earlier < later, 1.0, 0.0).astype(BF16)
    rank = jnp.dot(member.astype(BF16), before, preferred_element_type=F32)
    rank = jnp.where(member > 0.0, rank, -1.0)
    slot = lax.broadcasted_iota(jnp.int32, (capacity, tokens), 0).astype(F32)
    hits, scales = [], []
    for d in range(column_count):
        hit = jnp.where(rank[d : d + 1, :] == slot, 1.0, 0.0)
        hits.append(hit)
        scales.append(jnp.sum(hit * scale[d : d + 1, :], axis=1, keepdims=True))
    return jnp.concatenate(hits, axis=0), jnp.concatenate(scales, axis=0)


def select_kernel(column_count, capacity, place_ref, meta_ref, x_ref, d_ref, *refs):
    out_refs, (hits_ref, hits_all, scales_all) = refs[:column_count], refs[column_count:]

    @pl.when(pl.program_id(0) == 0)
    def _():
        hits, scales = placing_of(place_ref, meta_ref, column_count, capacity)
        hits_all[...] = hits.astype(BF16)
        hits_ref[...] = hits.astype(BF16)
        scales_all[...] = jnp.broadcast_to(scales, scales_all.shape)

    hits = hits_all[...]
    x = jnp.dot(hits, x_ref[...], preferred_element_type=F32).astype(BF16)
    dy = jnp.dot(hits, d_ref[...], preferred_element_type=F32)
    dy = (dy * scales_all[:, 0:1]).astype(BF16)
    for d in range(column_count):
        out_refs[d][0] = x[d * capacity : (d + 1) * capacity, :]
        out_refs[d][1] = dy[d * capacity : (d + 1) * capacity, :]


def select(place, meta, x, d_rows, column_count, capacity):
    tokens, width = x.shape
    tile = tile_of(width, 512)
    slot_count = column_count * capacity
    block = pl.BlockSpec((tokens, tile), lambda n: (0, n))
    outs = pl.pallas_call(
        functools.partial(select_kernel, column_count, capacity),
        grid=(width // tile,),
        out_shape=[jax.ShapeDtypeStruct((2, capacity, width), BF16)] * column_count
        + [jax.ShapeDtypeStruct((slot_count, tokens), BF16)],
        in_specs=[smem(), pl.BlockSpec(meta.shape, lambda n: (0, 0)), block, block],
        out_specs=[pl.BlockSpec((2, capacity, tile), lambda n: (0, 0, n))] * column_count
        + [pl.BlockSpec((slot_count, tokens), lambda n: (0, 0))],
        scratch_shapes=[
            pltpu.VMEM((slot_count, tokens), BF16),
            pltpu.VMEM((slot_count, 128), F32),
        ],
        compiler_params=params(),
        cost_estimate=small_cost(),
        name="select",
    )(place, meta, x, d_rows)
    return outs[:-1], outs[-1]


def merge_kernel(column_count, has_carry, hits_ref, *refs):
    slots = jnp.concatenate([part[...] for part in refs[:column_count]], axis=0)
    total = lax.dot_general(
        hits_ref[...], slots, (((0,), (0,)), ((), ())), preferred_element_type=F32
    )
    if has_carry:
        total = total + refs[column_count][...].astype(F32)
    refs[-1][...] = total.astype(BF16)


def merge(hits, parts, carry):
    column_count, (capacity, width) = len(parts), parts[0].shape
    tokens = hits.shape[1]
    tile = tile_of(width, 512)
    rows_block = pl.BlockSpec((tokens, tile), lambda n: (0, n))
    carries = [] if carry is None else [carry]
    return pl.pallas_call(
        functools.partial(merge_kernel, column_count, carry is not None),
        grid=(width // tile,),
        out_shape=jax.ShapeDtypeStruct((tokens, width), BF16),
        in_specs=[pl.BlockSpec(hits.shape, lambda n: (0, 0))]
        + [pl.BlockSpec((capacity, tile), lambda n: (0, n))] * column_count
        + [rows_block] * len(carries),
        out_specs=rows_block,
        compiler_params=params(),
        cost_estimate=small_cost(),
        name="merge",
    )(hits, *parts, *carries)


def expert_kernel(piece_count, capacity, place_ref, *refs):
    slot_refs, refs = refs[:piece_count], refs[piece_count:]
    w_ref, send_ref, keep_ref, hid_ref = refs[:4]
    dx_refs, refs = refs[4 : 4 + piece_count], refs[4 + piece_count :]
    x_all, dy_all, x_turned, dy_turned, w_pair, w_down, turned, slot_sems, w_sems = refs
    part, width = w_down.shape[1:]
    high = place_ref[2]

    slot_copies = []
    for i, ref in enumerate(slot_refs):
        rows = pl.ds(i * capacity, capacity)
        for k, target in enumerate((x_all, dy_all)):
            slot_copies.append(
                pltpu.make_async_copy(ref.at[k], target.at[rows], slot_sems.at[2 * i + k])
            )
    w_copies = []
    for t in range(2):
        rows = pl.ds(pl.multiple_of(jnp.bitwise_xor(high, 1 - t) * part, part), part)
        targets = (
            w_pair.at[pl.ds(2 * t * part, part)],
            w_pair.at[pl.ds((2 * t + 1) * part, part)],
            w_down.at[t],
        )
        for k, target in enumerate(targets):
            source = w_ref.at[0, rows, pl.ds(k * width, width)]
            w_copies.append(pltpu.make_async_copy(source, target, w_sems.at[3 * t + k]))
    for copy in slot_copies + w_copies:
        copy.start()
    for copy in slot_copies:
        copy.wait()
    x_turned[...] = x_all[...].T
    dy_turned[...] = dy_all[...].T
    for t in range(2):
        w_copies[3 * t].wait()
        w_copies[3 * t + 1].wait()
        both = jnp.dot(
            w_pair[2 * t * part : (2 * t + 2) * part, :],
            x_turned[...],
            preferred_element_type=F32,
        )
        w_copies[3 * t + 2].wait()
        d_hidden = jnp.dot(w_down[t], dy_turned[...], preferred_element_type=F32)
        gate, up = both[:part], both[part:]
        sig = jax.nn.sigmoid(gate)
        act = gate * sig
        d_up = (d_hidden * act).astype(BF16)
        d_gate = (d_hidden * up * sig * (1.0 + gate * (1.0 - sig))).astype(BF16)
        hid_ref[jnp.bitwise_xor(high, 1 - t)] = (act * up).astype(BF16)
        out_ref = (send_ref, keep_ref)[t]
        out_ref[:part, :] = d_gate
        out_ref[part:, :] = d_up
        turned[:, 2 * t * part : (2 * t + 1) * part] = d_gate.T
        turned[:, (2 * t + 1) * part : (2 * t + 2) * part] = d_up.T
    total = jnp.dot(turned[...], w_pair[...], preferred_element_type=F32).astype(BF16)
    for i in range(piece_count):
        dx_refs[i][...] = total[i * capacity : (i + 1) * capacity, :]


def expert(place, slots, w_stack):
    piece_count = len(slots)
    _, capacity, width = slots[0].shape
    rows = piece_count * capacity
    hidden = w_stack.shape[1]
    part = hidden // 2
    anywhere = pl.BlockSpec(memory_space=pl.ANY)
    inside = pl.BlockSpec(memory_space=pltpu.VMEM)
    outs = pl.pallas_call(
        functools.partial(expert_kernel, piece_count, capacity),
        in_specs=[smem()] + [anywhere] * (piece_count + 1),
        out_specs=[inside] * (3 + piece_count),
        out_shape=[
            jax.ShapeDtypeStruct((hidden, rows), BF16),
            jax.ShapeDtypeStruct((hidden, rows), BF16),
            jax.ShapeDtypeStruct((2, part, rows), BF16),
        ]
        + [jax.ShapeDtypeStruct((capacity, width), BF16)] * piece_count,
        scratch_shapes=[
            pltpu.VMEM((rows, width), BF16),
            pltpu.VMEM((rows, width), BF16),
            pltpu.VMEM((width, rows), BF16),
            pltpu.VMEM((width, rows), BF16),
            pltpu.VMEM((2 * hidden, width), BF16),
            pltpu.VMEM((2, part, width), BF16),
            pltpu.VMEM((rows, 2 * hidden), BF16),
            pltpu.SemaphoreType.DMA((2 * piece_count,)),
            pltpu.SemaphoreType.DMA((6,)),
        ],
        compiler_params=params(),
        cost_estimate=small_cost(),
        name="expert",
    )(place, *slots, w_stack)
    return outs[0], outs[1], outs[2], outs[3:]


def grad_x_kernel(act_count, place_ref, *refs):
    acts, rows = refs[:act_count], refs[act_count:-2]
    send_ref, keep_ref = refs[-2:]
    own = send_ref.shape[1]
    low = place_ref[3]
    right = jnp.concatenate(
        [ref[0] if len(ref.shape) == 3 else ref[...] for ref in rows], axis=0
    )
    lefts = []
    for who in (1 - low, low):
        for lead in range(2):
            start = pl.multiple_of((2 * lead + who) * own, own)
            lefts.append(jnp.concatenate([ref[pl.ds(start, own), :] for ref in acts], axis=1))
    total = jnp.dot(jnp.concatenate(lefts, axis=0), right, preferred_element_type=F32).astype(BF16)
    send_ref[0] = total[:own]
    send_ref[1] = total[own : 2 * own]
    keep_ref[0] = total[2 * own : 3 * own]
    keep_ref[1] = total[3 * own :]


def rows_spec(array, tile, lead):
    if array.ndim == 3:
        return pl.BlockSpec((1, array.shape[1], tile), lambda n: (lead, 0, n))
    return pl.BlockSpec((array.shape[0], tile), lambda n: (0, n))


def grad_x(place, acts, rows):
    own = acts[0].shape[0] // 4
    width = rows[0].shape[-1]
    tile = tile_of(width, 512)
    out_spec = pl.BlockSpec((2, own, tile), lambda n: (0, 0, n))
    return pl.pallas_call(
        functools.partial(grad_x_kernel, len(acts)),
        grid=(width // tile,),
        in_specs=[smem()]
        + [pl.BlockSpec(act.shape, lambda n: (0, 0)) for act in acts]
        + [rows_spec(row, tile, 0) for row in rows],
        out_specs=[out_spec, out_spec],
        out_shape=[jax.ShapeDtypeStruct((2, own, width), BF16)] * 2,
        compiler_params=params(),
        cost_estimate=small_cost(),
        name="grad_x",
    )(place, *acts, *rows)


def grad_down_kernel(act_count, other, place_ref, *refs):
    acts, rows = refs[:act_count], refs[act_count:-2]
    send_ref, keep_ref = refs[-2:]
    own = send_ref.shape[0]
    high, low = place_ref[2], place_ref[3]
    lead = 1 - high if other else high
    right = jnp.concatenate([ref[0] for ref in rows], axis=0)
    lefts = []
    for who in (1 - low, low):
        start = pl.multiple_of(who * own, own)
        lefts.append(jnp.concatenate([ref[lead, pl.ds(start, own), :] for ref in acts], axis=1))
    total = jnp.dot(jnp.concatenate(lefts, axis=0), right, preferred_element_type=F32).astype(BF16)
    send_ref[...] = total[:own]
    keep_ref[...] = total[own:]


def grad_down(place, acts, rows, other):
    own = acts[0].shape[1] // 2
    width = rows[0].shape[-1]
    tile = tile_of(width, 512)
    out_spec = pl.BlockSpec((own, tile), lambda n: (0, n))
    return pl.pallas_call(
        functools.partial(grad_down_kernel, len(acts), other),
        grid=(width // tile,),
        in_specs=[smem()]
        + [pl.BlockSpec(act.shape, lambda n: (0, 0, 0)) for act in acts]
        + [rows_spec(row, tile, 1) for row in rows],
        out_specs=[out_spec, out_spec],
        out_shape=[jax.ShapeDtypeStruct((own, width), BF16)] * 2,
        compiler_params=params(),
        cost_estimate=small_cost(),
        name="grad_down_other" if other else "grad_down_own",
    )(place, *acts, *rows)


def add_kernel(term_count, *refs):
    total = refs[0][...].astype(F32)
    for ref in refs[1:term_count]:
        total = total + ref[...].astype(F32)
    out_ref = refs[-1]
    out_ref[...] = total.astype(BF16).reshape(out_ref.shape)


def add_into(terms, columns, first, into, name):
    leads, own, width = terms[0].shape
    tile = tile_of(width, 1024)
    tiles = width // tile
    aliases, operands = {}, list(terms)
    in_specs = [pl.BlockSpec((1, own, tile), lambda i, n: (i, 0, n))] * len(terms)
    if into is not None:
        aliases = {len(operands): 0}
        operands.append(into)
        in_specs.append(pl.BlockSpec(memory_space=pl.ANY))
    return pl.pallas_call(
        functools.partial(add_kernel, len(terms)),
        grid=(leads, tiles),
        in_specs=in_specs,
        out_specs=pl.BlockSpec((own, tile), lambda i, n: (0, first // tile + i * tiles + n)),
        out_shape=jax.ShapeDtypeStruct((own, columns), BF16),
        input_output_aliases=aliases,
        compiler_params=params(),
        cost_estimate=small_cost(),
        name=name,
    )(*operands)


def body(x_tokens, d_out, expert_ids, combine, w_stack):
    tokens, width = x_tokens.shape
    experts = lax.axis_size("expert")
    replicas = lax.axis_size("replica")
    plane_count = len(RING)
    columns = experts // plane_count
    capacity = 2 * tokens * expert_ids.shape[1] // experts

    position = lax.axis_index("expert")
    replica = lax.axis_index("replica")
    plane, column = position // columns, position % columns
    high, low = replica // 2, replica % 2
    place = jnp.stack([plane * columns, column, high, low]).astype(jnp.int32)

    def along_ring(value, hops=1):
        pairs = [
            (RING[i] * columns + c, RING[(i + hops) % plane_count] * columns + c)
            for i in range(plane_count)
            for c in range(columns)
        ]
        return lax.ppermute(value, "expert", pairs)

    def across_columns(value, d):
        pairs = [
            (p * columns + c, p * columns + (c ^ d))
            for p in range(plane_count)
            for c in range(columns)
        ]
        return lax.ppermute(value, "expert", pairs)

    def across_replicas(value, d):
        return lax.ppermute(value, "replica", [(r, r ^ d) for r in range(replicas)])

    meta = jnp.concatenate([expert_ids.T.astype(F32), combine.T], axis=0)
    metas, x_blocks, d_blocks = [meta], [x_tokens], [d_out]
    for s in range(1, plane_count):
        metas.append(along_ring(meta, s))
        x_blocks.append(along_ring(x_blocks[-1]))
        d_blocks.append(along_ring(d_blocks[-1]))

    slots, hits, x_other = [], [], []
    for s in range(plane_count):
        picked, hit = select(place, metas[s], x_blocks[s], d_blocks[s], columns, capacity)
        arrived = [picked[0]] + [across_columns(picked[d], d) for d in range(1, columns)]
        slots.append(arrived)
        hits.append(hit)
        x_other.append(
            across_replicas(jnp.concatenate([piece[0] for piece in arrived], axis=0), 2)
        )

    keeps, arrivals, hids, pieces = [], [], [], []
    group = 2
    for g in range(0, plane_count, group):
        group_slots = [piece for s in range(g, g + group) for piece in slots[s]]
        send, keep, hid, dx = expert(place, group_slots, w_stack)
        keeps.append(keep)
        arrivals.append(across_replicas(send, 2))
        hids.append(hid)
        pieces.extend(dx)

    def dx_parts(s):
        mine = pieces[s * columns : (s + 1) * columns]
        return [mine[0]] + [across_columns(mine[d], d) for d in range(1, columns)]

    carry = None
    for s in range(1, plane_count):
        carry = along_ring(merge(hits[s], dx_parts(s), carry))
    d_tokens = merge(hits[0], dx_parts(0), carry)

    all_slots = [piece for arrived in slots for piece in arrived]
    send, keep = grad_down(place, hids, all_slots, True)
    across = keep.astype(F32) + across_replicas(send, 1).astype(F32)
    down_y = across_replicas(across.astype(BF16), 2)
    send, down_own = grad_down(place, hids, all_slots, False)
    down_core = across_replicas(send, 1)
    send, keep = grad_x(place, keeps + arrivals, all_slots + x_other)
    g_rows = add_into([keep, across_replicas(send, 1)], 3 * width, 0, None, "sum_x")
    down_terms = [term[None] for term in (down_own, down_core, down_y)]
    g_rows = add_into(down_terms, 3 * width, 2 * width, g_rows, "sum_down")
    return d_tokens, g_rows[None]


def solution(mesh):
    return jax.shard_map(
        body,
        mesh=mesh,
        in_specs=(
            P(("expert", "replica"), None),
            P(("expert", "replica"), None),
            P(("expert", "replica"), None),
            P(("expert", "replica"), None),
            P("expert", None, None),
        ),
        out_specs=(P(("expert", "replica"), None), P("expert", "replica", None)),
        check_vma=False,
    )
```

```python
import functools

import jax
import jax.numpy as jnp
from jax import lax
from jax.experimental import pallas as pl
from jax.experimental.pallas import tpu as pltpu
from jax.sharding import PartitionSpec as P

BF16 = jnp.bfloat16
F32 = jnp.float32
RING = (0, 1, 3, 2)
VMEM_LIMIT = 56 * 1024 * 1024


def params():
    return pltpu.CompilerParams(vmem_limit_bytes=VMEM_LIMIT)


def smem():
    return pl.BlockSpec(memory_space=pltpu.SMEM)


def anywhere():
    return pl.BlockSpec(memory_space=pl.ANY)


def inside():
    return pl.BlockSpec(memory_space=pltpu.VMEM)


def small_cost():
    return pl.CostEstimate(flops=1024, bytes_accessed=1024, transcendentals=0)


def tile_of(width, most):
    return most if width % most == 0 else width


def hold_kernel(*refs):
    pass


def hold(value, *deps):
    return pl.pallas_call(
        hold_kernel,
        in_specs=[anywhere()] * (1 + len(deps)),
        out_specs=anywhere(),
        out_shape=jax.ShapeDtypeStruct(value.shape, value.dtype),
        input_output_aliases={0: 0},
        cost_estimate=small_cost(),
        name="hold",
    )(value, *deps)


def placing_of(place_ref, meta, column_count, capacity):
    tokens = meta.shape[1]
    base, own = place_ref[0], place_ref[1]
    id_first, id_second = meta[0:1, :], meta[1:2, :]
    scale_first, scale_second = meta[2:3, :], meta[3:4, :]
    row = lax.broadcasted_iota(jnp.int32, (16, tokens), 0)
    expert = (base + jnp.bitwise_xor(row, own)).astype(F32)
    first = id_first == expert
    member = jnp.where(first | (id_second == expert), 1.0, 0.0)
    scale = jnp.where(first, scale_first, scale_second)
    earlier = lax.broadcasted_iota(jnp.int32, (tokens, tokens), 0)
    later = lax.broadcasted_iota(jnp.int32, (tokens, tokens), 1)
    before = jnp.where(earlier < later, 1.0, 0.0).astype(BF16)
    rank = jnp.dot(member.astype(BF16), before, preferred_element_type=F32)
    rank = jnp.where(member > 0.0, rank, -1.0)
    slot = lax.broadcasted_iota(jnp.int32, (capacity, tokens), 0).astype(F32)
    hits, scales = [], []
    for d in range(column_count):
        hit = jnp.where(rank[d : d + 1, :] == slot, 1.0, 0.0)
        hits.append(hit)
        scales.append(jnp.sum(hit * scale[d : d + 1, :], axis=1, keepdims=True))
    return jnp.concatenate(hits, axis=0), jnp.concatenate(scales, axis=0)


def select_x_kernel(column_count, capacity, step, place_ref, meta_ref, x_ref, *refs):
    both_ref, send_refs = refs[0], refs[1:column_count]
    hits_ref, scales_ref = refs[column_count : column_count + 2]
    hits_all = refs[-1]

    @pl.when(pl.program_id(0) == 0)
    def _():
        meta = meta_ref[place_ref[4 + step] if step else 0]
        hits, scales = placing_of(place_ref, meta, column_count, capacity)
        hits_all[...] = hits.astype(BF16)
        hits_ref[...] = hits.astype(BF16)
        scales_ref[...] = jnp.broadcast_to(scales, scales_ref.shape)

    picked = jnp.dot(hits_all[...], x_ref[...], preferred_element_type=F32).astype(BF16)
    both_ref[...] = picked
    for d in range(1, column_count):
        send_refs[d - 1][...] = picked[d * capacity : (d + 1) * capacity, :]


def select_x(place, meta, step, x, column_count, capacity, deps):
    tokens, width = x.shape
    tile = tile_of(width, 1024)
    count = column_count * capacity

    def kernel(*refs):
        select_x_kernel(column_count, capacity, step, *refs[:3], *refs[3 + len(deps) :])

    def columns(rows):
        return pl.BlockSpec((rows, tile), lambda n: (0, n))

    def fixed(shape):
        return pl.BlockSpec(shape, lambda n: (0,) * len(shape))

    outs = pl.pallas_call(
        kernel,
        grid=(width // tile,),
        in_specs=[smem(), fixed(meta.shape), columns(tokens)] + [anywhere()] * len(deps),
        out_specs=[columns(count)]
        + [columns(capacity)] * (column_count - 1)
        + [fixed((count, tokens)), fixed((count, 128))],
        out_shape=[jax.ShapeDtypeStruct((count, width), BF16)]
        + [jax.ShapeDtypeStruct((capacity, width), BF16)] * (column_count - 1)
        + [
            jax.ShapeDtypeStruct((count, tokens), BF16),
            jax.ShapeDtypeStruct((count, 128), F32),
        ],
        scratch_shapes=[pltpu.VMEM((count, tokens), BF16)],
        compiler_params=params(),
        cost_estimate=small_cost(),
        name="select_x",
    )(place, meta, x, *deps)
    return outs[0], outs[1:-2], outs[-2], outs[-1]


def select_d_kernel(column_count, capacity, hits_ref, scales_ref, d_ref, *out_refs):
    picked = jnp.dot(hits_ref[...], d_ref[...], preferred_element_type=F32)
    picked = (picked * scales_ref[:, 0:1]).astype(BF16)
    for d in range(column_count):
        out_refs[d][...] = picked[d * capacity : (d + 1) * capacity, :]


def select_d(hits, scales, d_rows, column_count, deps):
    tokens, width = d_rows.shape
    tile = tile_of(width, 1024)
    capacity = hits.shape[0] // column_count

    def kernel(*refs):
        select_d_kernel(column_count, capacity, *refs[:3], *refs[3 + len(deps) :])

    def columns(rows):
        return pl.BlockSpec((rows, tile), lambda n: (0, n))

    def fixed(shape):
        return pl.BlockSpec(shape, lambda n: (0,) * len(shape))

    return pl.pallas_call(
        kernel,
        grid=(width // tile,),
        in_specs=[fixed(hits.shape), fixed(scales.shape), columns(tokens)]
        + [anywhere()] * len(deps),
        out_specs=[columns(capacity)] * column_count,
        out_shape=[jax.ShapeDtypeStruct((capacity, width), BF16)] * column_count,
        compiler_params=params(),
        cost_estimate=small_cost(),
        name="select_d",
    )(hits, scales, d_rows, *deps)


def merge_kernel(column_count, has_carry, hits_ref, *refs):
    slots = jnp.concatenate([part[0] for part in refs[:column_count]], axis=0)
    total = lax.dot_general(
        hits_ref[...], slots, (((0,), (0,)), ((), ())), preferred_element_type=F32
    )
    if has_carry:
        total = total + refs[column_count][...].astype(F32)
    refs[-1][...] = total.astype(BF16)


def merge(hits, parts, which, carry):
    column_count, (_, capacity, width) = len(parts), parts[0].shape
    tokens = hits.shape[1]
    tile = tile_of(width, 1024)
    rows_block = pl.BlockSpec((tokens, tile), lambda n: (0, n))
    carries = [] if carry is None else [carry]
    return pl.pallas_call(
        functools.partial(merge_kernel, column_count, carry is not None),
        grid=(width // tile,),
        out_shape=jax.ShapeDtypeStruct((tokens, width), BF16),
        in_specs=[pl.BlockSpec(hits.shape, lambda n: (0, 0))]
        + [pl.BlockSpec((1, capacity, tile), lambda n: (which, 0, n))] * column_count
        + [rows_block] * len(carries),
        out_specs=rows_block,
        compiler_params=params(),
        cost_estimate=small_cost(),
        name="merge",
    )(hits, *parts, *carries)


def gate_up_kernel(piece_count, capacity, *refs):
    piece_refs, refs = refs[:piece_count], refs[piece_count:]
    w_ref, refs = refs[0], refs[-9:]
    hid_ref, act_ref, slope_ref, x_all, x_turned, w_pair, slot_sems, w_sems, _ = refs
    part = w_pair.shape[1] // 2
    width = x_all.shape[1]
    slot_copies = [
        pltpu.make_async_copy(
            ref.at[pl.ds(0, capacity)], x_all.at[pl.ds(i * capacity, capacity)], slot_sems.at[i]
        )
        for i, ref in enumerate(piece_refs)
    ]
    w_copies = [
        pltpu.make_async_copy(
            w_ref.at[0, pl.ds(t * part, part), pl.ds(k * width, width)],
            w_pair.at[t, pl.ds(k * part, part)],
            w_sems.at[2 * t + k],
        )
        for t in range(2)
        for k in range(2)
    ]
    for copy in slot_copies + w_copies:
        copy.start()
    for copy in slot_copies:
        copy.wait()
    x_turned[...] = x_all[...].T
    for t in range(2):
        w_copies[2 * t].wait()
        w_copies[2 * t + 1].wait()
        both = jnp.dot(w_pair[t], x_turned[...], preferred_element_type=F32)
        gate, up = both[:part], both[part:]
        sig = jax.nn.sigmoid(gate)
        act = gate * sig
        hid_ref[t] = (act * up).astype(BF16)
        act_ref[t * part : (t + 1) * part, :] = act
        slope_ref[t * part : (t + 1) * part, :] = up * sig * (1.0 + gate * (1.0 - sig))


def gate_up(pieces, w_stack, capacity, deps):
    width = pieces[0].shape[1]
    rows = len(pieces) * capacity
    hidden = w_stack.shape[1]
    return pl.pallas_call(
        functools.partial(gate_up_kernel, len(pieces), capacity),
        in_specs=[anywhere()] * (len(pieces) + 1 + len(deps)),
        out_specs=[inside()] * 3,
        out_shape=[
            jax.ShapeDtypeStruct((2, hidden // 2, rows), BF16),
            jax.ShapeDtypeStruct((hidden, rows), F32),
            jax.ShapeDtypeStruct((hidden, rows), F32),
        ],
        scratch_shapes=[
            pltpu.VMEM((rows, width), BF16),
            pltpu.VMEM((width, rows), BF16),
            pltpu.VMEM((2, hidden, width), BF16),
            pltpu.SemaphoreType.DMA((len(pieces),)),
            pltpu.SemaphoreType.DMA((4,)),
            pltpu.SMEM((1,), jnp.int32),
        ],
        compiler_params=params(),
        cost_estimate=small_cost(),
        name="gate_up",
    )(*pieces, w_stack, *deps)


def backward_kernel(piece_count, column_count, capacity, first_row, place_ref, *refs):
    piece_refs, refs = refs[:piece_count], refs[piece_count:]
    act_ref, slope_ref, w_ref = refs[:3]
    refs = refs[-(2 + column_count + 9) :]
    send_ref, keep_ref = refs[:2]
    dx_refs, refs = refs[2 : 2 + column_count], refs[2 + column_count :]
    dy_all, dy_turned, w_pair, w_down, act_all, slope_all, turned, slot_sems, w_sems = refs
    _, part, width = w_down.shape
    rows = dy_all.shape[0]
    high = place_ref[2]
    slot_copies = [
        pltpu.make_async_copy(
            ref, dy_all.at[pl.ds(i * capacity, capacity)], slot_sems.at[i]
        )
        for i, ref in enumerate(piece_refs)
    ]
    down_copies, factor_copies, pair_copies = [], [], []
    for t in range(2):
        units = pl.ds(pl.multiple_of(jnp.bitwise_xor(high, 1 - t) * part, part), part)
        columns = pl.ds(first_row, rows)
        down_copies.append(
            pltpu.make_async_copy(
                w_ref.at[0, units, pl.ds(2 * width, width)], w_down.at[t], w_sems.at[5 * t]
            )
        )
        for k, (ref, target) in enumerate(((act_ref, act_all), (slope_ref, slope_all))):
            factor_copies.append(
                pltpu.make_async_copy(
                    ref.at[units, columns], target.at[t], w_sems.at[5 * t + 1 + k]
                )
            )
            pair_copies.append(
                pltpu.make_async_copy(
                    w_ref.at[0, units, pl.ds(k * width, width)],
                    w_pair.at[pl.ds((2 * t + k) * part, part)],
                    w_sems.at[5 * t + 3 + k],
                )
            )
    for copy in slot_copies + down_copies + factor_copies + pair_copies:
        copy.start()
    for copy in slot_copies:
        copy.wait()
    dy_turned[...] = dy_all[...].T
    for t in range(2):
        down_copies[t].wait()
        d_hidden = jnp.dot(w_down[t], dy_turned[...], preferred_element_type=F32)
        factor_copies[2 * t].wait()
        factor_copies[2 * t + 1].wait()
        d_up = (d_hidden * act_all[t]).astype(BF16)
        d_gate = (d_hidden * slope_all[t]).astype(BF16)
        out_ref = (send_ref, keep_ref)[t]
        out_ref[:part, :] = d_gate
        out_ref[part:, :] = d_up
        turned[:, 2 * t * part : (2 * t + 1) * part] = d_gate.T
        turned[:, (2 * t + 1) * part : (2 * t + 2) * part] = d_up.T
    for copy in pair_copies:
        copy.wait()
    total = jnp.dot(turned[...], w_pair[...], preferred_element_type=F32).astype(BF16)
    for i in range(piece_count):
        dx_refs[i % column_count][i // column_count] = total[i * capacity : (i + 1) * capacity, :]


def backward(place, pieces, act, slope, w_stack, first_row, column_count, deps):
    capacity, width = pieces[0].shape
    rows = len(pieces) * capacity
    hidden = w_stack.shape[1]
    steps = len(pieces) // column_count
    outs = pl.pallas_call(
        functools.partial(backward_kernel, len(pieces), column_count, capacity, first_row),
        in_specs=[smem()] + [anywhere()] * (len(pieces) + 3 + len(deps)),
        out_specs=[inside()] * (2 + column_count),
        out_shape=[jax.ShapeDtypeStruct((hidden, rows), BF16)] * 2
        + [jax.ShapeDtypeStruct((steps, capacity, width), BF16)] * column_count,
        scratch_shapes=[
            pltpu.VMEM((rows, width), BF16),
            pltpu.VMEM((width, rows), BF16),
            pltpu.VMEM((2 * hidden, width), BF16),
            pltpu.VMEM((2, hidden // 2, width), BF16),
            pltpu.VMEM((2, hidden // 2, rows), F32),
            pltpu.VMEM((2, hidden // 2, rows), F32),
            pltpu.VMEM((rows, 2 * hidden), BF16),
            pltpu.SemaphoreType.DMA((len(pieces),)),
            pltpu.SemaphoreType.DMA((10,)),
        ],
        compiler_params=params(),
        cost_estimate=small_cost(),
        name="backward",
    )(place, *pieces, act, slope, w_stack, *deps)
    return outs[0], outs[1], outs[2:]


def row_operand(capacity, tile, entry):
    array, which = entry
    if array.ndim == 3:
        return array, pl.BlockSpec((1, capacity, tile), lambda n: (which, 0, n))
    return array, pl.BlockSpec((capacity, tile), lambda n: (0, n))


def stacked_rows(refs):
    return jnp.concatenate([ref[0] if len(ref.shape) == 3 else ref[...] for ref in refs], axis=0)


def grad_x_kernel(act_count, place_ref, *refs):
    acts, rows = refs[:act_count], refs[act_count:-2]
    send_ref, keep_ref = refs[-2:]
    own = send_ref.shape[1]
    low = place_ref[3]
    lefts = []
    for who in (1 - low, low):
        for lead in range(2):
            start = pl.multiple_of((2 * lead + who) * own, own)
            lefts.append(jnp.concatenate([ref[pl.ds(start, own), :] for ref in acts], axis=1))
    total = jnp.dot(
        jnp.concatenate(lefts, axis=0), stacked_rows(rows), preferred_element_type=F32
    ).astype(BF16)
    send_ref[0] = total[:own]
    send_ref[1] = total[own : 2 * own]
    keep_ref[0] = total[2 * own : 3 * own]
    keep_ref[1] = total[3 * own :]


def grad_x(place, acts, rows, capacity, width):
    own = acts[0].shape[0] // 4
    tile = tile_of(width, 1024)
    out_spec = pl.BlockSpec((2, own, tile), lambda n: (0, 0, n))
    arrays, specs = zip(*[row_operand(capacity, tile, entry) for entry in rows])
    return pl.pallas_call(
        functools.partial(grad_x_kernel, len(acts)),
        grid=(width // tile,),
        in_specs=[smem()]
        + [pl.BlockSpec(act.shape, lambda n: (0, 0)) for act in acts]
        + list(specs),
        out_specs=[out_spec, out_spec],
        out_shape=[jax.ShapeDtypeStruct((2, own, width), BF16)] * 2,
        compiler_params=params(),
        cost_estimate=small_cost(),
        name="grad_x",
    )(place, *acts, *arrays)


def grad_down_kernel(other, place_ref, hid_ref, *refs):
    rows, (send_ref, keep_ref) = refs[:-2], refs[-2:]
    own = send_ref.shape[0]
    high, low = place_ref[2], place_ref[3]
    lead = 1 - high if other else high
    lefts = [
        hid_ref[lead, pl.ds(pl.multiple_of(who * own, own), own), :] for who in (1 - low, low)
    ]
    total = jnp.dot(
        jnp.concatenate(lefts, axis=0), stacked_rows(rows), preferred_element_type=F32
    ).astype(BF16)
    send_ref[...] = total[:own]
    keep_ref[...] = total[own:]


def grad_down(place, hid, rows, other):
    own = hid.shape[1] // 2
    capacity, width = rows[0].shape
    tile = tile_of(width, 1024)
    out_spec = pl.BlockSpec((own, tile), lambda n: (0, n))
    arrays, specs = zip(*[row_operand(capacity, tile, (row, 0)) for row in rows])
    return pl.pallas_call(
        functools.partial(grad_down_kernel, other),
        grid=(width // tile,),
        in_specs=[smem(), pl.BlockSpec(hid.shape, lambda n: (0, 0, 0))] + list(specs),
        out_specs=[out_spec, out_spec],
        out_shape=[jax.ShapeDtypeStruct((own, width), BF16)] * 2,
        compiler_params=params(),
        cost_estimate=small_cost(),
        name="grad_down_other" if other else "grad_down_own",
    )(place, hid, *arrays)


def add_kernel(term_count, *refs):
    total = refs[0][...].astype(F32)
    for ref in refs[1:term_count]:
        total = total + ref[...].astype(F32)
    out_ref = refs[-1]
    out_ref[...] = total.astype(BF16).reshape(out_ref.shape)


def add_into(terms, columns, first, into, name):
    leads, own, width = terms[0].shape
    tile = tile_of(width, 1024)
    tiles = width // tile
    aliases, operands = {}, list(terms)
    in_specs = [pl.BlockSpec((1, own, tile), lambda i, n: (i, 0, n))] * len(terms)
    if into is not None:
        aliases = {len(operands): 0}
        operands.append(into)
        in_specs.append(pl.BlockSpec(memory_space=pl.ANY))
    return pl.pallas_call(
        functools.partial(add_kernel, len(terms)),
        grid=(leads, tiles),
        in_specs=in_specs,
        out_specs=pl.BlockSpec((own, tile), lambda i, n: (0, first // tile + i * tiles + n)),
        out_shape=jax.ShapeDtypeStruct((own, columns), BF16),
        input_output_aliases=aliases,
        compiler_params=params(),
        cost_estimate=small_cost(),
        name=name,
    )(*operands)


def body(x_tokens, d_out, expert_ids, combine, w_stack):
    tokens, width = x_tokens.shape
    experts = lax.axis_size("expert")
    replicas = lax.axis_size("replica")
    planes = len(RING)
    columns = experts // planes
    capacity = 2 * tokens * expert_ids.shape[1] // experts
    group = 2

    position = lax.axis_index("expert")
    replica = lax.axis_index("replica")
    plane, column = position // columns, position % columns
    high, low = replica // 2, replica % 2
    ring_place = plane ^ (plane >> 1)
    sources = [(ring_place - s) & (planes - 1) for s in range(planes)]
    blocks = [(source ^ (source >> 1)) * columns + column for source in sources]
    place = jnp.stack([plane * columns, column, high, low, *blocks]).astype(jnp.int32)

    def along_ring(value):
        pairs = [
            (RING[i] * columns + c, RING[(i + 1) % planes] * columns + c)
            for i in range(planes)
            for c in range(columns)
        ]
        return lax.ppermute(value, "expert", pairs)

    def across_columns(value, d):
        pairs = [
            (p * columns + c, p * columns + (c ^ d))
            for p in range(planes)
            for c in range(columns)
        ]
        return lax.ppermute(value, "expert", pairs)

    def across_replicas(value, d):
        return lax.ppermute(value, "replica", [(r, r ^ d) for r in range(replicas)])

    meta = jnp.concatenate([expert_ids.T.astype(F32), combine.T], axis=0)
    metas = lax.all_gather(meta, "expert")

    x_block = x_tokens
    hits, scales, x_pieces, y_both, y_passed = [], [], [], [], []
    for s in range(planes):
        following = along_ring(x_block) if s < planes - 1 else None
        both, sends, hit, scale = select_x(
            place, metas if s else meta[None], s, x_block, columns, capacity,
            y_both[s - 2 : s - 1] if s >= 2 else [],
        )
        x_pieces += [both] + [across_columns(send, d + 1) for d, send in enumerate(sends)]
        y_both.append(across_replicas(both, 2))
        hits.append(hit)
        scales.append(scale)
        if following is not None:
            x_block = following

    def pass_on(g):
        passed = []
        for d in range(1, columns):
            rows = jnp.stack(
                [y_both[s][d * capacity : (d + 1) * capacity] for s in range(g, g + group)]
            )
            passed.append(rows)
        return passed

    to_pass = pass_on(0)
    y_passed.append([across_columns(rows, d + 1) for d, rows in enumerate(to_pass)])
    hid, act, slope = gate_up(x_pieces, w_stack, capacity, to_pass)

    d_block = hold(d_out, x_block)
    dy_pieces, keeps, arrivals, parts = [], [], [], []
    carry = None
    for s in range(planes):
        following = along_ring(d_block) if s < planes - 1 else None
        deps = []
        if s == 2:
            to_pass = pass_on(group)
            y_passed.append([across_columns(rows, d + 1) for d, rows in enumerate(to_pass)])
            deps = to_pass + y_passed[0]
        if s == 3:
            deps = y_passed[1]
        picked = select_d(hits[s], scales[s], d_block, columns, deps)
        dy_pieces += [picked[0]] + [
            across_columns(picked[d], d) for d in range(1, columns)
        ]
        if following is not None:
            d_block = following
        if s % group == group - 1:
            deps = []
            if s == planes - 1:
                send, keep = grad_down(place, hid, dy_pieces, True)
                down_send, down_own = grad_down(place, hid, dy_pieces, False)
                across = keep.astype(F32) + across_replicas(send, 1).astype(F32)
                across = across.astype(BF16)
                down_y = across_replicas(across, 2)
                down_core = across_replicas(down_send, 1)
                carry = merge(hits[1], parts[0], 1, None)
                deps = [across, down_core, carry, arrivals[0]]
                carry = along_ring(carry)
            first_row = (s + 1 - group) * columns * capacity
            send, keep, dx = backward(
                place, dy_pieces[-group * columns :], act, slope, w_stack, first_row, columns, deps
            )
            keeps.append(keep)
            arrivals.append(across_replicas(send, 2))
            parts.append([dx[0]] + [across_columns(dx[d], d) for d in range(1, columns)])

    for s in range(2, planes):
        carry = along_ring(merge(hits[s], parts[s // group], s % group, carry))
    d_tokens = merge(hits[0], parts[0], 0, carry)

    rows = [(piece, 0) for piece in x_pieces]
    for s in range(planes):
        rows += [(y_both[s], 0)] + [(passed, s % group) for passed in y_passed[s // group]]
    send, keep = grad_x(place, keeps + arrivals, rows, capacity, width)
    g_rows = add_into([keep, across_replicas(send, 1)], 3 * width, 0, None, "sum_x")
    down_terms = [term[None] for term in (down_own, down_core, down_y)]
    g_rows = add_into(down_terms, 3 * width, 2 * width, g_rows, "sum_down")
    return d_tokens, g_rows[None]


def solution(mesh):
    return jax.shard_map(
        body,
        mesh=mesh,
        in_specs=(
            P(("expert", "replica"), None),
            P(("expert", "replica"), None),
            P(("expert", "replica"), None),
            P(("expert", "replica"), None),
            P("expert", None, None),
        ),
        out_specs=(P(("expert", "replica"), None), P("expert", "replica", None)),
        check_vma=False,
    )
```

```python
import functools

import jax
import jax.numpy as jnp
from jax import lax
from jax.experimental import pallas as pl
from jax.experimental.pallas import tpu as pltpu
from jax.sharding import PartitionSpec as P

BF16 = jnp.bfloat16
F32 = jnp.float32
RING = (0, 1, 3, 2)
VMEM_LIMIT = 56 * 1024 * 1024


def params():
    return pltpu.CompilerParams(vmem_limit_bytes=VMEM_LIMIT)


def smem():
    return pl.BlockSpec(memory_space=pltpu.SMEM)


def anywhere():
    return pl.BlockSpec(memory_space=pl.ANY)


def inside():
    return pl.BlockSpec(memory_space=pltpu.VMEM)


def small_cost():
    return pl.CostEstimate(flops=1024, bytes_accessed=1024, transcendentals=0)


def tile_of(width, most):
    return most if width % most == 0 else width


class Order:
    def __init__(self):
        self.last = []

    def call(self, kernel, specs, operands, deps=(), **options):
        extra = list(deps) + self.last
        count = len(operands)

        def body_of(*refs):
            kernel(*refs[:count], *refs[count + len(extra) :])

        outs = pl.pallas_call(
            body_of,
            in_specs=list(specs) + [anywhere()] * len(extra),
            compiler_params=params(),
            cost_estimate=small_cost(),
            **options,
        )(*operands, *extra)
        self.last = [outs[-1] if isinstance(outs, (list, tuple)) else outs]
        return outs


def columns_spec(rows, tile):
    return pl.BlockSpec((rows, tile), lambda n: (0, n))


def fixed_spec(shape):
    return pl.BlockSpec(shape, lambda n: (0,) * len(shape))


def placing_of(place_ref, meta, column_count, capacity):
    tokens = meta.shape[1]
    base, own = place_ref[0], place_ref[1]
    id_first, id_second = meta[0:1, :], meta[1:2, :]
    scale_first, scale_second = meta[2:3, :], meta[3:4, :]
    row = lax.broadcasted_iota(jnp.int32, (16, tokens), 0)
    expert = (base + jnp.bitwise_xor(row, own)).astype(F32)
    first = id_first == expert
    member = jnp.where(first | (id_second == expert), 1.0, 0.0)
    scale = jnp.where(first, scale_first, scale_second)
    earlier = lax.broadcasted_iota(jnp.int32, (tokens, tokens), 0)
    later = lax.broadcasted_iota(jnp.int32, (tokens, tokens), 1)
    before = jnp.where(earlier < later, 1.0, 0.0).astype(BF16)
    rank = jnp.dot(member.astype(BF16), before, preferred_element_type=F32)
    rank = jnp.where(member > 0.0, rank, -1.0)
    slot = lax.broadcasted_iota(jnp.int32, (capacity, tokens), 0).astype(F32)
    hits, scales = [], []
    for d in range(column_count):
        hit = jnp.where(rank[d : d + 1, :] == slot, 1.0, 0.0)
        hits.append(hit)
        scales.append(jnp.sum(hit * scale[d : d + 1, :], axis=1, keepdims=True))
    return jnp.concatenate(hits, axis=0), jnp.concatenate(scales, axis=0)


def select_x_kernel(column_count, capacity, place_ref, meta_ref, x_ref, *refs):
    both_ref, send_refs = refs[0], refs[1:column_count]
    scales_ref, hits_ref, hits_all = refs[column_count:]

    @pl.when(pl.program_id(0) == 0)
    def _():
        hits, scales = placing_of(place_ref, meta_ref, column_count, capacity)
        hits_all[...] = hits.astype(BF16)
        hits_ref[...] = hits.astype(BF16)
        scales_ref[...] = jnp.broadcast_to(scales, scales_ref.shape)

    picked = jnp.dot(hits_all[...], x_ref[...], preferred_element_type=F32).astype(BF16)
    both_ref[...] = picked
    for d in range(1, column_count):
        send_refs[d - 1][...] = picked[d * capacity : (d + 1) * capacity, :]


def select_x(order, place, meta, x, column_count, capacity, deps):
    tokens, width = x.shape
    tile = tile_of(width, 1024)
    count = column_count * capacity
    outs = order.call(
        functools.partial(select_x_kernel, column_count, capacity),
        [smem(), fixed_spec(meta.shape), columns_spec(tokens, tile)],
        [place, meta, x],
        deps,
        grid=(width // tile,),
        out_specs=[columns_spec(count, tile)]
        + [columns_spec(capacity, tile)] * (column_count - 1)
        + [fixed_spec((count, 128)), fixed_spec((count, tokens))],
        out_shape=[jax.ShapeDtypeStruct((count, width), BF16)]
        + [jax.ShapeDtypeStruct((capacity, width), BF16)] * (column_count - 1)
        + [
            jax.ShapeDtypeStruct((count, 128), F32),
            jax.ShapeDtypeStruct((count, tokens), BF16),
        ],
        scratch_shapes=[pltpu.VMEM((count, tokens), BF16)],
        name="select_x",
    )
    return outs[0], outs[1:-2], outs[-2], outs[-1]


def select_d_kernel(column_count, capacity, hits_ref, scales_ref, d_ref, *out_refs):
    rows = d_ref[...]
    picked = jnp.dot(hits_ref[...], rows, preferred_element_type=F32)
    picked = (picked * scales_ref[:, 0:1]).astype(BF16)
    for d in range(column_count):
        out_refs[d][...] = picked[d * capacity : (d + 1) * capacity, :]
    if len(out_refs) > column_count:
        out_refs[-1][...] = rows


def select_d(order, hits, scales, d_rows, column_count, again, deps):
    tokens, width = d_rows.shape
    tile = tile_of(width, 1024)
    capacity = hits.shape[0] // column_count
    heights = [capacity] * column_count + [tokens] * again
    return order.call(
        functools.partial(select_d_kernel, column_count, capacity),
        [fixed_spec(hits.shape), fixed_spec(scales.shape), columns_spec(tokens, tile)],
        [hits, scales, d_rows],
        deps,
        grid=(width // tile,),
        out_specs=[columns_spec(height, tile) for height in heights],
        out_shape=[jax.ShapeDtypeStruct((height, width), BF16) for height in heights],
        name="select_d",
    )


def merge_kernel(column_count, has_carry, hits_ref, *refs):
    slots = jnp.concatenate([part[0] for part in refs[:column_count]], axis=0)
    total = lax.dot_general(
        hits_ref[...], slots, (((0,), (0,)), ((), ())), preferred_element_type=F32
    )
    if has_carry:
        total = total + refs[column_count][...].astype(F32)
    refs[-1][...] = total.astype(BF16)


def merge(order, hits, parts, which, carry, deps=()):
    column_count, (_, capacity, width) = len(parts), parts[0].shape
    tokens = hits.shape[1]
    tile = tile_of(width, 1024)
    carries = [] if carry is None else [carry]
    return order.call(
        functools.partial(merge_kernel, column_count, carry is not None),
        [fixed_spec(hits.shape)]
        + [pl.BlockSpec((1, capacity, tile), lambda n: (which, 0, n))] * column_count
        + [columns_spec(tokens, tile)] * len(carries),
        [hits, *parts, *carries],
        deps,
        grid=(width // tile,),
        out_shape=jax.ShapeDtypeStruct((tokens, width), BF16),
        out_specs=columns_spec(tokens, tile),
        name="merge",
    )


def start_rows(refs, target, capacity, sems):
    copies = [
        pltpu.make_async_copy(
            ref.at[pl.ds(0, capacity)], target.at[pl.ds(i * capacity, capacity)], sems.at[i]
        )
        for i, ref in enumerate(refs)
    ]
    for copy in copies:
        copy.start()
    return copies


def start_weights(w_ref, units, part, target, sem):
    width = target.shape[-1]
    copy = pltpu.make_async_copy(w_ref.at[0, units, pl.ds(part * width, width)], target, sem)
    copy.start()
    return copy


def units_of(place_ref, step, half):
    return pl.ds(pl.multiple_of(jnp.bitwise_xor(place_ref[2], 1 - step) * half, half), half)


def give_dx(turned, w_pair, dx_refs, capacity):
    total = jnp.dot(turned[...], w_pair[...], preferred_element_type=F32).astype(BF16)
    for i in range(total.shape[0] // capacity):
        dx_refs[i % len(dx_refs)][i // len(dx_refs)] = total[i * capacity : (i + 1) * capacity, :]


def give_factors(step, half, d_gate, d_up, out_ref, turned):
    out_ref[:half, :] = d_gate
    out_ref[half:, :] = d_up
    turned[:, 2 * step * half : (2 * step + 1) * half] = d_gate.T
    turned[:, (2 * step + 1) * half : (2 * step + 2) * half] = d_up.T


def expert_kernel(count, columns, capacity, place_ref, *refs):
    x_refs, dy_refs, w_ref = refs[:count], refs[count : 2 * count], refs[2 * count]
    refs = refs[2 * count + 1 :]
    hid_ref, dx_refs, (send_ref, keep_ref), refs = (
        refs[0], refs[1 : 1 + columns], refs[1 + columns : 3 + columns], refs[3 + columns :]
    )
    x_all, dy_all, x_turned, dy_turned, w_pair, w_down, turned, sems, w_sems = refs
    half = w_down.shape[1]
    rows = start_rows(x_refs, x_all, capacity, sems)
    rows += start_rows(dy_refs, dy_all, capacity, sems.at[pl.ds(count, count)])
    weights = []
    for t in range(2):
        units = units_of(place_ref, t, half)
        for k in range(2):
            target = w_pair.at[pl.ds((2 * t + k) * half, half)]
            weights.append(start_weights(w_ref, units, k, target, w_sems.at[3 * t + k]))
        weights.append(start_weights(w_ref, units, 2, w_down.at[t], w_sems.at[3 * t + 2]))
    for copy in rows:
        copy.wait()
    x_turned[...] = x_all[...].T
    dy_turned[...] = dy_all[...].T
    for t in range(2):
        weights[3 * t].wait()
        weights[3 * t + 1].wait()
        pair = w_pair[2 * t * half : (2 * t + 2) * half, :]
        both = jnp.dot(pair, x_turned[...], preferred_element_type=F32)
        weights[3 * t + 2].wait()
        d_hidden = jnp.dot(w_down[t], dy_turned[...], preferred_element_type=F32)
        gate, up = both[:half], both[half:]
        sig = jax.nn.sigmoid(gate)
        act = gate * sig
        d_up = (d_hidden * act).astype(BF16)
        d_gate = (d_hidden * up * sig * (1.0 + gate * (1.0 - sig))).astype(BF16)
        hid_ref[jnp.bitwise_xor(place_ref[2], 1 - t)] = (act * up).astype(BF16)
        give_factors(t, half, d_gate, d_up, (send_ref, keep_ref)[t], turned)
    give_dx(turned, w_pair, dx_refs, capacity)


def expert(order, place, x_pieces, dy_pieces, w_stack, column_count, deps):
    count = len(x_pieces)
    capacity, width = dy_pieces[0].shape
    rows, hidden = count * capacity, w_stack.shape[1]
    outs = order.call(
        functools.partial(expert_kernel, count, column_count, capacity),
        [smem()] + [anywhere()] * (2 * count + 1),
        [place, *x_pieces, *dy_pieces, w_stack],
        deps,
        out_specs=[inside()] * (3 + column_count),
        out_shape=[jax.ShapeDtypeStruct((2, hidden // 2, rows), BF16)]
        + [jax.ShapeDtypeStruct((count // column_count, capacity, width), BF16)] * column_count
        + [jax.ShapeDtypeStruct((hidden, rows), BF16)] * 2,
        scratch_shapes=[
            pltpu.VMEM((rows, width), BF16),
            pltpu.VMEM((rows, width), BF16),
            pltpu.VMEM((width, rows), BF16),
            pltpu.VMEM((width, rows), BF16),
            pltpu.VMEM((2 * hidden, width), BF16),
            pltpu.VMEM((2, hidden // 2, width), BF16),
            pltpu.VMEM((rows, 2 * hidden), BF16),
            pltpu.SemaphoreType.DMA((2 * count,)),
            pltpu.SemaphoreType.DMA((6,)),
        ],
        name="expert",
    )
    return outs[0], outs[1:-2], outs[-2], outs[-1]


def gate_up_kernel(count, capacity, *refs):
    x_refs, w_ref, refs = refs[:count], refs[count], refs[count + 1 :]
    hid_ref, act_ref, slope_ref, x_all, x_turned, w_pair, sems, w_sems = refs
    half = w_pair.shape[1] // 2
    rows = start_rows(x_refs, x_all, capacity, sems)
    weights = []
    for t in range(2):
        for k in range(2):
            target = w_pair.at[t, pl.ds(k * half, half)]
            units = pl.ds(t * half, half)
            weights.append(start_weights(w_ref, units, k, target, w_sems.at[2 * t + k]))
    for copy in rows:
        copy.wait()
    x_turned[...] = x_all[...].T
    for t in range(2):
        weights[2 * t].wait()
        weights[2 * t + 1].wait()
        both = jnp.dot(w_pair[t], x_turned[...], preferred_element_type=F32)
        gate, up = both[:half], both[half:]
        sig = jax.nn.sigmoid(gate)
        act = gate * sig
        hid_ref[t] = (act * up).astype(BF16)
        act_ref[t] = act
        slope_ref[t] = up * sig * (1.0 + gate * (1.0 - sig))


def gate_up(order, pieces, w_stack, capacity, deps):
    width = pieces[0].shape[1]
    rows, hidden = len(pieces) * capacity, w_stack.shape[1]
    return order.call(
        functools.partial(gate_up_kernel, len(pieces), capacity),
        [anywhere()] * (len(pieces) + 1),
        [*pieces, w_stack],
        deps,
        out_specs=[inside()] * 3,
        out_shape=[
            jax.ShapeDtypeStruct((2, hidden // 2, rows), BF16),
            jax.ShapeDtypeStruct((2, hidden // 2, rows), F32),
            jax.ShapeDtypeStruct((2, hidden // 2, rows), F32),
        ],
        scratch_shapes=[
            pltpu.VMEM((rows, width), BF16),
            pltpu.VMEM((width, rows), BF16),
            pltpu.VMEM((2, hidden, width), BF16),
            pltpu.SemaphoreType.DMA((len(pieces),)),
            pltpu.SemaphoreType.DMA((4,)),
        ],
        name="gate_up",
    )


def backward_kernel(count, columns, capacity, place_ref, *refs):
    dy_refs, (act_ref, slope_ref, w_ref), refs = (
        refs[:count], refs[count : count + 3], refs[count + 3 :]
    )
    dx_refs, (send_ref, keep_ref), refs = refs[:columns], refs[columns : columns + 2], refs[columns + 2 :]
    dy_all, dy_turned, w_pair, w_down, act_all, slope_all, turned, sems, w_sems = refs
    half = w_down.shape[1]
    rows = start_rows(dy_refs, dy_all, capacity, sems)
    downs, factors, pairs = [], [], []
    for t in range(2):
        units = units_of(place_ref, t, half)
        downs.append(start_weights(w_ref, units, 2, w_down.at[t], w_sems.at[5 * t]))
        which = jnp.bitwise_xor(place_ref[2], 1 - t)
        for k, (ref, target) in enumerate(((act_ref, act_all), (slope_ref, slope_all))):
            copy = pltpu.make_async_copy(ref.at[which], target.at[t], w_sems.at[5 * t + 1 + k])
            copy.start()
            factors.append(copy)
    for t in range(2):
        for k in range(2):
            target = w_pair.at[pl.ds((2 * t + k) * half, half)]
            sem = w_sems.at[5 * t + 3 + k]
            pairs.append(start_weights(w_ref, units_of(place_ref, t, half), k, target, sem))
    for copy in rows:
        copy.wait()
    dy_turned[...] = dy_all[...].T
    for t in range(2):
        downs[t].wait()
        d_hidden = jnp.dot(w_down[t], dy_turned[...], preferred_element_type=F32)
        factors[2 * t].wait()
        factors[2 * t + 1].wait()
        d_up = (d_hidden * act_all[t]).astype(BF16)
        d_gate = (d_hidden * slope_all[t]).astype(BF16)
        give_factors(t, half, d_gate, d_up, (send_ref, keep_ref)[t], turned)
    for copy in pairs:
        copy.wait()
    give_dx(turned, w_pair, dx_refs, capacity)


def backward(order, place, pieces, act, slope, w_stack, column_count, deps):
    count = len(pieces)
    capacity, width = pieces[0].shape
    rows, hidden = count * capacity, w_stack.shape[1]
    outs = order.call(
        functools.partial(backward_kernel, count, column_count, capacity),
        [smem()] + [anywhere()] * (count + 3),
        [place, *pieces, act, slope, w_stack],
        deps,
        out_specs=[inside()] * (2 + column_count),
        out_shape=[jax.ShapeDtypeStruct((count // column_count, capacity, width), BF16)]
        * column_count
        + [jax.ShapeDtypeStruct((hidden, rows), BF16)] * 2,
        scratch_shapes=[
            pltpu.VMEM((rows, width), BF16),
            pltpu.VMEM((width, rows), BF16),
            pltpu.VMEM((2 * hidden, width), BF16),
            pltpu.VMEM((2, hidden // 2, width), BF16),
            pltpu.VMEM((2, hidden // 2, rows), F32),
            pltpu.VMEM((2, hidden // 2, rows), F32),
            pltpu.VMEM((rows, 2 * hidden), BF16),
            pltpu.SemaphoreType.DMA((count,)),
            pltpu.SemaphoreType.DMA((10,)),
        ],
        name="backward",
    )
    return outs[:-2], outs[-2], outs[-1]


def row_operand(capacity, tile, entry):
    array, which = entry
    if array.ndim == 3:
        return array, pl.BlockSpec((1, capacity, tile), lambda n: (which, 0, n))
    return array, pl.BlockSpec((capacity, tile), lambda n: (0, n))


def stacked_rows(refs):
    return jnp.concatenate([ref[0] if len(ref.shape) == 3 else ref[...] for ref in refs], axis=0)


def grad_x_kernel(act_count, place_ref, *refs):
    acts, rows = refs[:act_count], refs[act_count:-2]
    send_ref, keep_ref = refs[-2:]
    own = send_ref.shape[1]
    low = place_ref[3]
    lefts = []
    for who in (1 - low, low):
        for lead in range(2):
            start = pl.multiple_of((2 * lead + who) * own, own)
            lefts.append(jnp.concatenate([ref[pl.ds(start, own), :] for ref in acts], axis=1))
    total = jnp.dot(
        jnp.concatenate(lefts, axis=0), stacked_rows(rows), preferred_element_type=F32
    ).astype(BF16)
    send_ref[0] = total[:own]
    send_ref[1] = total[own : 2 * own]
    keep_ref[0] = total[2 * own : 3 * own]
    keep_ref[1] = total[3 * own :]


def grad_x(order, place, acts, rows, capacity, width):
    own = acts[0].shape[0] // 4
    tile = tile_of(width, 512)
    arrays, specs = zip(*[row_operand(capacity, tile, entry) for entry in rows])
    return order.call(
        functools.partial(grad_x_kernel, len(acts)),
        [smem()] + [fixed_spec(act.shape) for act in acts] + list(specs),
        [place, *acts, *arrays],
        grid=(width // tile,),
        out_specs=[pl.BlockSpec((2, own, tile), lambda n: (0, 0, n))] * 2,
        out_shape=[jax.ShapeDtypeStruct((2, own, width), BF16)] * 2,
        name="grad_x",
    )


def grad_down_kernel(hid_count, other, place_ref, *refs):
    hids, rows, (send_ref, keep_ref) = refs[:hid_count], refs[hid_count:-2], refs[-2:]
    own = send_ref.shape[0]
    high, low = place_ref[2], place_ref[3]
    lead = 1 - high if other else high
    lefts = []
    for who in (1 - low, low):
        start = pl.multiple_of(who * own, own)
        lefts.append(jnp.concatenate([ref[lead, pl.ds(start, own), :] for ref in hids], axis=1))
    total = jnp.dot(
        jnp.concatenate(lefts, axis=0), stacked_rows(rows), preferred_element_type=F32
    ).astype(BF16)
    send_ref[...] = total[:own]
    keep_ref[...] = total[own:]


def grad_down(order, place, hids, rows, other):
    own = hids[0].shape[1] // 2
    capacity, width = rows[0].shape
    tile = tile_of(width, 1024)
    arrays, specs = zip(*[row_operand(capacity, tile, (row, 0)) for row in rows])
    return order.call(
        functools.partial(grad_down_kernel, len(hids), other),
        [smem()] + [fixed_spec(hid.shape) for hid in hids] + list(specs),
        [place, *hids, *arrays],
        grid=(width // tile,),
        out_specs=[columns_spec(own, tile)] * 2,
        out_shape=[jax.ShapeDtypeStruct((own, width), BF16)] * 2,
        name="grad_down_other" if other else "grad_down_own",
    )


def add_kernel(term_count, *refs):
    total = refs[0][...].astype(F32)
    for ref in refs[1:term_count]:
        total = total + ref[...].astype(F32)
    out_ref = refs[-1]
    out_ref[...] = total.astype(BF16).reshape(out_ref.shape)


def add_into(order, terms, columns, first, into, name):
    leads, own, width = terms[0].shape
    tile = tile_of(width, 1024)
    tiles = width // tile
    aliases, operands = {}, list(terms)
    in_specs = [pl.BlockSpec((1, own, tile), lambda i, n: (i, 0, n))] * len(terms)
    if into is not None:
        aliases = {len(operands): 0}
        operands.append(into)
        in_specs.append(anywhere())
    return order.call(
        functools.partial(add_kernel, len(terms)),
        in_specs,
        operands,
        grid=(leads, tiles),
        out_specs=pl.BlockSpec((own, tile), lambda i, n: (0, first // tile + i * tiles + n)),
        out_shape=jax.ShapeDtypeStruct((own, columns), BF16),
        input_output_aliases=aliases,
        name=name,
    )


def body(x_tokens, d_out, expert_ids, combine, w_stack):
    tokens, width = x_tokens.shape
    experts = lax.axis_size("expert")
    replicas = lax.axis_size("replica")
    planes = len(RING)
    columns = experts // planes
    capacity = 2 * tokens * expert_ids.shape[1] // experts

    position = lax.axis_index("expert")
    replica = lax.axis_index("replica")
    plane, column = position // columns, position % columns
    high, low = replica // 2, replica % 2
    place = jnp.stack([plane * columns, column, high, low]).astype(jnp.int32)

    def along_ring(value, hops=1):
        pairs = [
            (RING[i] * columns + c, RING[(i + hops) % planes] * columns + c)
            for i in range(planes)
            for c in range(columns)
        ]
        return lax.ppermute(value, "expert", pairs)

    def across_columns(value, d):
        pairs = [
            (p * columns + c, p * columns + (c ^ d))
            for p in range(planes)
            for c in range(columns)
        ]
        return lax.ppermute(value, "expert", pairs)

    def across_replicas(value, d):
        return lax.ppermute(value, "replica", [(r, r ^ d) for r in range(replicas)])

    def exchange(values):
        return [across_columns(value, d + 1) for d, value in enumerate(values)]

    order = Order()
    meta = jnp.concatenate([expert_ids.T.astype(F32), combine.T], axis=0)
    metas = [meta] + [along_ring(meta, s) for s in range(1, planes)]
    hits, scales, x_pieces, y_both, dy_pieces = [], [], [], [], []

    def take_x(s, block, deps):
        both, sends, scale, hit = select_x(order, place, metas[s], block, columns, capacity, deps)
        x_pieces.append([both] + exchange(sends))
        y_both.append(across_replicas(both, 2))
        hits.append(hit)
        scales.append(scale)

    def take_d(s, block, deps, again=False):
        picked = select_d(order, hits[s], scales[s], block, columns, again, deps)
        dy_pieces.append([picked[0]] + exchange(picked[1:columns]))
        return picked[-1]

    def pass_on(steps):
        return [
            jnp.stack([y_both[s][d * capacity : (d + 1) * capacity] for s in steps])
            for d in range(1, columns)
        ]

    x_1 = along_ring(x_tokens)
    take_x(0, x_tokens, [])
    x_2 = along_ring(x_1)
    d_0 = take_d(0, d_out, [x_1], again=True)
    d_1 = along_ring(d_0)
    take_x(1, x_1, metas[1:] + x_pieces[0][1:])
    x_3 = along_ring(x_2)
    d_2 = along_ring(d_1)
    take_x(2, x_2, [d_1, y_both[0]] + dy_pieces[0][1:])
    take_d(1, d_1, [])
    to_pass = pass_on((0, 1))
    y_passed = [exchange(to_pass)]
    first_x, first_dy = x_pieces[0] + x_pieces[1], dy_pieces[0] + dy_pieces[1]
    hid_a, dx_a, send, keep_a = expert(
        order, place, first_x, first_dy, w_stack, columns, to_pass
    )
    arrived_a = across_replicas(send, 2)
    parts_a = [dx_a[0]] + exchange(dx_a[1:])
    d_3 = along_ring(d_2)
    take_x(3, x_3, [d_2, y_both[2]] + y_passed[0])
    take_d(2, d_2, [])
    carry = along_ring(merge(order, hits[1], parts_a, 1, None))
    last_x = x_pieces[2] + x_pieces[3]
    hid_b, act, slope = gate_up(order, last_x, w_stack, capacity, [arrived_a])
    take_d(3, d_3, [])
    to_pass = pass_on((2, 3))
    y_passed.append(exchange(to_pass))
    last_dy = dy_pieces[2] + dy_pieces[3]

    hids, all_dy = [hid_a, hid_b], first_dy + last_dy
    send, keep = grad_down(order, place, hids, all_dy, True)
    across = (keep.astype(F32) + across_replicas(send, 1).astype(F32)).astype(BF16)
    down_y = across_replicas(across, 2)
    send, down_own = grad_down(order, place, hids, all_dy, False)
    down_core = across_replicas(send, 1)
    dx_b, send, keep_b = backward(
        order, place, last_dy, act, slope, w_stack, columns, [across, carry, *to_pass]
    )
    arrived_b = across_replicas(send, 2)
    parts_b = [dx_b[0]] + exchange(dx_b[1:])
    carry = along_ring(merge(order, hits[2], parts_b, 0, carry, [down_core] + y_passed[1]))

    rows = [(piece, 0) for pieces in x_pieces for piece in pieces]
    for s in range(planes):
        rows += [(y_both[s], 0)] + [(passed, s % 2) for passed in y_passed[s // 2]]
    acts = [keep_a, keep_b, arrived_a, arrived_b]
    send, keep = grad_x(order, place, acts, rows, capacity, width)
    x_core = across_replicas(send, 1)
    carry = along_ring(merge(order, hits[3], parts_b, 1, carry))
    g_rows = add_into(order, [keep, x_core], 3 * width, 0, None, "sum_x")
    d_tokens = merge(order, hits[0], parts_a, 0, carry)
    down_terms = [term[None] for term in (down_own, down_core, down_y)]
    g_rows = add_into(order, down_terms, 3 * width, 2 * width, g_rows, "sum_down")
    return d_tokens, g_rows[None]


def solution(mesh):
    return jax.shard_map(
        body,
        mesh=mesh,
        in_specs=(
            P(("expert", "replica"), None),
            P(("expert", "replica"), None),
            P(("expert", "replica"), None),
            P(("expert", "replica"), None),
            P("expert", None, None),
        ),
        out_specs=(P(("expert", "replica"), None), P("expert", "replica", None)),
        check_vma=False,
    )
```

```python
import functools

import jax
import jax.numpy as jnp
from jax import lax
from jax.experimental import pallas as pl
from jax.experimental.pallas import tpu as pltpu
from jax.sharding import PartitionSpec as P

BF16 = jnp.bfloat16
F32 = jnp.float32
RING = (0, 1, 3, 2)
VMEM_LIMIT = 44 * 1024 * 1024


def params():
    return pltpu.CompilerParams(vmem_limit_bytes=VMEM_LIMIT)


def smem():
    return pl.BlockSpec(memory_space=pltpu.SMEM)


def anywhere():
    return pl.BlockSpec(memory_space=pl.ANY)


def inside():
    return pl.BlockSpec(memory_space=pltpu.VMEM)


def small_cost():
    return pl.CostEstimate(flops=1024, bytes_accessed=1024, transcendentals=0)


def tile_of(width, most):
    return most if width % most == 0 else width


class Order:
    def __init__(self):
        self.last = []

    def call(self, kernel, specs, operands, deps=(), **options):
        extra = list(deps) + self.last
        count = len(operands)

        def body_of(*refs):
            kernel(*refs[:count], *refs[count + len(extra) :])

        outs = pl.pallas_call(
            body_of,
            in_specs=list(specs) + [anywhere()] * len(extra),
            compiler_params=params(),
            cost_estimate=small_cost(),
            **options,
        )(*operands, *extra)
        self.last = [outs[-1] if isinstance(outs, (list, tuple)) else outs]
        return outs


def columns_spec(rows, tile):
    return pl.BlockSpec((rows, tile), lambda n: (0, n))


def fixed_spec(shape):
    return pl.BlockSpec(shape, lambda n: (0,) * len(shape))


def placing_of(base, own, meta, expert_count, capacity):
    tokens = meta.shape[1]
    id_first, id_second = meta[0:1, :], meta[1:2, :]
    scale_first, scale_second = meta[2:3, :], meta[3:4, :]
    row = lax.broadcasted_iota(jnp.int32, (max(16, expert_count), tokens), 0)
    expert = (base + jnp.bitwise_xor(row, own)).astype(F32)
    first = id_first == expert
    member = jnp.where(first | (id_second == expert), 1.0, 0.0)
    scale = jnp.where(first, scale_first, scale_second)
    earlier = lax.broadcasted_iota(jnp.int32, (tokens, tokens), 0)
    later = lax.broadcasted_iota(jnp.int32, (tokens, tokens), 1)
    before = jnp.where(earlier < later, 1.0, 0.0).astype(BF16)
    rank = jnp.dot(member.astype(BF16), before, preferred_element_type=F32)
    rank = jnp.where(member > 0.0, rank, -1.0)
    slot = lax.broadcasted_iota(jnp.int32, (capacity, tokens), 0).astype(F32)
    hits, scales = [], []
    for d in range(expert_count):
        hit = jnp.where(rank[d : d + 1, :] == slot, 1.0, 0.0)
        hits.append(hit)
        scales.append(jnp.sum(hit * scale[d : d + 1, :], axis=1, keepdims=True))
    return jnp.concatenate(hits, axis=0), jnp.concatenate(scales, axis=0)


def rounded(value):
    return value.astype(BF16).astype(F32)


def meta_columns(meta):
    scale = meta[2:4, :]
    top = rounded(scale)
    middle = rounded(scale - top)
    rest = scale - top - middle
    filler = jnp.zeros((120, meta.shape[1]), F32)
    return jnp.concatenate([meta[0:2, :], top, middle, rest, filler], axis=0).T.astype(BF16)


def meta_rows(columns):
    rows = columns.astype(F32).T
    scale = rows[2:4, :] + rows[4:6, :] + rows[6:8, :]
    return jnp.concatenate([rows[0:2, :], scale], axis=0)


def first_kernel(columns, capacity, place_ref, meta_ref, x_ref, *refs):
    x_out, keep_ref, send_refs = refs[0], refs[1], refs[2 : columns + 1]
    scales_ref, hits_ref = refs[columns + 1 :]
    width = x_ref.shape[1]
    meta = meta_ref[...]
    x = x_ref[...]
    x_out[:, :width] = x
    x_out[:, width:] = meta_columns(meta)
    hits, scales = placing_of(place_ref[0], place_ref[1], meta, columns, capacity)
    hits = hits.astype(BF16)
    hits_ref[...] = hits
    scales_ref[...] = jnp.broadcast_to(scales, scales_ref.shape)
    picked = jnp.dot(hits, x, preferred_element_type=F32).astype(BF16)
    keep_ref[...] = picked[:capacity, :]
    for d in range(1, columns):
        send_refs[d - 1][...] = picked[d * capacity : (d + 1) * capacity, :]


def select_first(order, place, meta, x, columns, capacity):
    tokens, width = x.shape
    count = columns * capacity
    outs = order.call(
        functools.partial(first_kernel, columns, capacity),
        [smem(), inside(), inside()],
        [place, meta, x],
        out_specs=[inside()] * (columns + 3),
        out_shape=[jax.ShapeDtypeStruct((tokens, width + 128), BF16)]
        + [jax.ShapeDtypeStruct((capacity, width), BF16)] * columns
        + [
            jax.ShapeDtypeStruct((count, 128), F32),
            jax.ShapeDtypeStruct((count, tokens), BF16),
        ],
        name="select_first",
    )
    return outs[0], outs[1:-2], outs[-2], outs[-1]


def both_kernel(columns, capacity, again, place_ref, x_ref, old_scales, old_hits, d_ref, *refs):
    keep_x, keep_d, refs = refs[0], refs[1], refs[2:]
    pair_refs, send_refs, refs = refs[: columns - 1], refs[columns - 1 : 2 * columns - 2], refs[2 * columns - 2 :]
    scales_ref, hits_ref = refs[-2:]
    width = d_ref.shape[1]
    rows = d_ref[...]
    if again:
        refs[0][...] = rows
    meta = meta_rows(x_ref[:, width:])
    hits, scales = placing_of(place_ref[0], place_ref[1], meta, columns, capacity)
    hits = hits.astype(BF16)
    hits_ref[...] = hits
    scales_ref[...] = jnp.broadcast_to(scales, scales_ref.shape)
    x = jnp.dot(hits, x_ref[:, :width], preferred_element_type=F32).astype(BF16)
    dy = jnp.dot(old_hits[...], rows, preferred_element_type=F32)
    dy = (dy * old_scales[:, 0:1]).astype(BF16)
    keep_x[...] = x[:capacity, :]
    keep_d[...] = dy[:capacity, :]
    for d in range(1, columns):
        part = slice(d * capacity, (d + 1) * capacity)
        pair_refs[d - 1][0] = x[part, :]
        pair_refs[d - 1][1] = dy[part, :]
        send_refs[d - 1][...] = x[part, :]


def select_both(order, place, x, scales, hits, d_rows, columns, again, deps):
    tokens, width = d_rows.shape
    count = hits.shape[0]
    capacity = count // columns
    shapes = [(capacity, width)] * 2
    shapes += [(2, capacity, width)] * (columns - 1) + [(capacity, width)] * (columns - 1)
    shapes += [(tokens, width)] * again
    outs = order.call(
        functools.partial(both_kernel, columns, capacity, again),
        [smem()] + [inside()] * 4,
        [place, x, scales, hits, d_rows],
        deps,
        out_specs=[inside()] * (len(shapes) + 2),
        out_shape=[jax.ShapeDtypeStruct(shape, BF16) for shape in shapes]
        + [
            jax.ShapeDtypeStruct((count, 128), F32),
            jax.ShapeDtypeStruct((count, tokens), BF16),
        ],
        name="select_both",
    )
    pairs, sends = outs[2 : columns + 1], outs[columns + 1 : 2 * columns]
    return outs[0], outs[1], pairs, sends, outs[-3], outs[-2], outs[-1]


def last_kernel(columns, scales_ref, hits_ref, d_ref, *out_refs):
    capacity = out_refs[0].shape[0]
    picked = jnp.dot(hits_ref[...], d_ref[...], preferred_element_type=F32)
    picked = (picked * scales_ref[:, 0:1]).astype(BF16)
    for d in range(columns):
        out_refs[d][...] = picked[d * capacity : (d + 1) * capacity, :]


def select_last(order, scales, hits, d_rows, columns, deps):
    width = d_rows.shape[1]
    capacity = hits.shape[0] // columns
    return order.call(
        functools.partial(last_kernel, columns),
        [inside()] * 3,
        [scales, hits, d_rows],
        deps,
        out_specs=[inside()] * columns,
        out_shape=[jax.ShapeDtypeStruct((capacity, width), BF16)] * columns,
        name="select_last",
    )


def place_all_kernel(experts, capacity, meta_ref, hits_ref):
    hits, _ = placing_of(0, 0, meta_ref[...], experts, capacity)
    hits_ref[...] = hits.astype(BF16)


def place_all(order, meta, experts, capacity):
    return order.call(
        functools.partial(place_all_kernel, experts, capacity),
        [inside()],
        [meta],
        out_specs=inside(),
        out_shape=jax.ShapeDtypeStruct((experts * capacity, meta.shape[1]), BF16),
        name="place_all",
    )


def merge_kernel(hits_ref, slots_ref, out_ref):
    out_ref[...] = lax.dot_general(
        hits_ref[...], slots_ref[...], (((0,), (0,)), ((), ())), preferred_element_type=F32
    ).astype(BF16)


def merge(order, hits, slots):
    count, tokens = hits.shape
    width = slots.shape[1]
    tile = tile_of(width, 1024)
    return order.call(
        merge_kernel,
        [fixed_spec(hits.shape), columns_spec(count, tile)],
        [hits, slots],
        grid=(width // tile,),
        out_shape=jax.ShapeDtypeStruct((tokens, width), BF16),
        out_specs=columns_spec(tokens, tile),
        name="merge",
    )


def start_rows(refs, target, sems):
    capacity = target.shape[0] // len(refs)
    copies = []
    for i, (ref, which) in enumerate(refs):
        source = ref if which is None else ref.at[which]
        rows = target.at[pl.ds(i * capacity, capacity)]
        copies.append(pltpu.make_async_copy(source, rows, sems.at[i]))
    for copy in copies:
        copy.start()
    return copies


def split_pieces(pieces):
    return [array for array, _ in pieces], [which for _, which in pieces]


def start_weights(w_ref, units, part, target, sem):
    width = target.shape[-1]
    copy = pltpu.make_async_copy(w_ref.at[0, units, pl.ds(part * width, width)], target, sem)
    copy.start()
    return copy


def gate_up_kernel(whiches, *refs):
    count = len(whiches)
    x_refs, w_ref, refs = refs[:count], refs[count], refs[count + 1 :]
    hid_ref, act_ref, slope_ref, x_all, x_turned, w_pair, sems, w_sems = refs
    half = hid_ref.shape[1]
    rows = start_rows(list(zip(x_refs, whiches)), x_all, sems)
    weights = []
    for t in range(2):
        for k in range(2):
            units = pl.ds(t * half, half)
            weights.append(start_weights(w_ref, units, k, w_pair.at[t, k], w_sems.at[2 * t + k]))
    for copy in rows:
        copy.wait()
    x_turned[...] = x_all[...].T
    for t in range(2):
        weights[2 * t].wait()
        gate = jnp.dot(w_pair[t, 0], x_turned[...], preferred_element_type=F32)
        weights[2 * t + 1].wait()
        up = jnp.dot(w_pair[t, 1], x_turned[...], preferred_element_type=F32)
        sig = jax.nn.sigmoid(gate)
        act = gate * sig
        hid_ref[t] = (act * up).astype(BF16)
        act_ref[t] = act
        slope_ref[t] = up * sig * (1.0 + gate * (1.0 - sig))


def gate_up(order, pieces, w_stack, capacity, deps=()):
    arrays, whiches = split_pieces(pieces)
    width = arrays[0].shape[-1]
    rows, hidden = len(pieces) * capacity, w_stack.shape[1]
    return order.call(
        functools.partial(gate_up_kernel, whiches),
        [anywhere()] * (len(pieces) + 1),
        [*arrays, w_stack],
        deps,
        out_specs=[inside()] * 3,
        out_shape=[
            jax.ShapeDtypeStruct((2, hidden // 2, rows), BF16),
            jax.ShapeDtypeStruct((2, hidden // 2, rows), F32),
            jax.ShapeDtypeStruct((2, hidden // 2, rows), F32),
        ],
        scratch_shapes=[
            pltpu.VMEM((rows, width), BF16),
            pltpu.VMEM((width, rows), BF16),
            pltpu.VMEM((2, 2, hidden // 2, width), BF16),
            pltpu.SemaphoreType.DMA((len(pieces),)),
            pltpu.SemaphoreType.DMA((4,)),
        ],
        name="gate_up",
    )


def backward_kernel(whiches, columns, first_step, place_ref, *refs):
    count = len(whiches)
    dy_refs, (act_ref, slope_ref, w_ref), refs = refs[:count], refs[count : count + 3], refs[count + 3 :]
    dx_ref, send_ref, keep_ref, dy_all, dy_turned, total, w_all, sems, w_sems, out_sems = refs[-10:]
    half = act_ref.shape[1]
    capacity = dx_ref.shape[1]
    rows = start_rows(list(zip(dy_refs, whiches)), dy_all, sems)
    halves = [jnp.bitwise_xor(place_ref[2], 1 - t) for t in range(2)]
    weights = []
    for t, which in enumerate(halves):
        units = pl.ds(pl.multiple_of(which * half, half), half)
        for k in (2, 0, 1):
            weights.append(start_weights(w_ref, units, k, w_all.at[t, k], w_sems.at[3 * t + k]))
    for copy in rows:
        copy.wait()
    dy_turned[...] = dy_all[...].T
    sums = None
    for t, which in enumerate(halves):
        weights[3 * t].wait()
        d_hidden = jnp.dot(w_all[t, 2], dy_turned[...], preferred_element_type=F32)
        d_up = (d_hidden * act_ref[which]).astype(BF16)
        d_gate = (d_hidden * slope_ref[which]).astype(BF16)
        out_ref = (send_ref, keep_ref)[t]
        out_ref[:half, :] = d_gate
        out_ref[half:, :] = d_up
        for k, factor in enumerate((d_gate, d_up)):
            weights[3 * t + 1 + k].wait()
            part = jnp.dot(factor.T, w_all[t, k], preferred_element_type=F32)
            sums = part if sums is None else sums + part
    total[...] = sums.astype(BF16)
    copies = []
    for i in range(count):
        block = place_ref[4 + first_step + i // columns] + jnp.bitwise_xor(
            place_ref[1], i % columns
        )
        copies.append(
            pltpu.make_async_copy(
                total.at[pl.ds(i * capacity, capacity)], dx_ref.at[block], out_sems.at[i]
            )
        )
    for copy in copies:
        copy.start()
    for copy in copies:
        copy.wait()


def backward(order, place, pieces, act, slope, w_stack, columns, first_step, dx, shape, deps):
    arrays, whiches = split_pieces(pieces)
    count = len(pieces)
    capacity, width = shape[1:]
    rows, hidden = count * capacity, w_stack.shape[1]
    operands = [place, *arrays, act, slope, w_stack]
    specs = [smem()] + [anywhere()] * count + [inside()] * 2 + [anywhere()]
    aliases = {}
    if dx is not None:
        aliases = {len(operands): 0}
        operands.append(dx)
        specs.append(anywhere())
    return order.call(
        functools.partial(backward_kernel, whiches, columns, first_step),
        specs,
        operands,
        deps,
        out_specs=[anywhere(), inside(), inside()],
        out_shape=[jax.ShapeDtypeStruct(shape, BF16)]
        + [jax.ShapeDtypeStruct((hidden, rows), BF16)] * 2,
        scratch_shapes=[
            pltpu.VMEM((rows, width), BF16),
            pltpu.VMEM((width, rows), BF16),
            pltpu.VMEM((rows, width), BF16),
            pltpu.VMEM((2, 3, hidden // 2, width), BF16),
            pltpu.SemaphoreType.DMA((count,)),
            pltpu.SemaphoreType.DMA((6,)),
            pltpu.SemaphoreType.DMA((count,)),
        ],
        input_output_aliases=aliases,
        name="backward",
    )


def row_operand(capacity, tile, entry):
    array, which = entry
    if array.ndim == 3:
        return array, pl.BlockSpec((1, capacity, tile), lambda n: (which, 0, n))
    return array, pl.BlockSpec((capacity, tile), lambda n: (0, n))


def stacked_rows(refs):
    return jnp.concatenate([ref[0] if len(ref.shape) == 3 else ref[...] for ref in refs], axis=0)


def grad_x_kernel(act_count, place_ref, *refs):
    acts, rows = refs[:act_count], refs[act_count:-2]
    send_ref, keep_ref = refs[-2:]
    own = send_ref.shape[1]
    low = place_ref[3]
    lefts = []
    for who in (1 - low, low):
        for lead in range(2):
            start = pl.multiple_of((2 * lead + who) * own, own)
            lefts.append(jnp.concatenate([ref[pl.ds(start, own), :] for ref in acts], axis=1))
    total = jnp.dot(
        jnp.concatenate(lefts, axis=0), stacked_rows(rows), preferred_element_type=F32
    ).astype(BF16)
    send_ref[0] = total[:own]
    send_ref[1] = total[own : 2 * own]
    keep_ref[0] = total[2 * own : 3 * own]
    keep_ref[1] = total[3 * own :]


def grad_x(order, place, acts, rows, capacity, width, deps):
    own = acts[0].shape[0] // 4
    tile = tile_of(width, 512)
    arrays, specs = zip(*[row_operand(capacity, tile, entry) for entry in rows])
    return order.call(
        functools.partial(grad_x_kernel, len(acts)),
        [smem()] + [fixed_spec(act.shape) for act in acts] + list(specs),
        [place, *acts, *arrays],
        deps,
        grid=(width // tile,),
        out_specs=[pl.BlockSpec((2, own, tile), lambda n: (0, 0, n))] * 2,
        out_shape=[jax.ShapeDtypeStruct((2, own, width), BF16)] * 2,
        name="grad_x",
    )


def grad_down_kernel(hid_count, place_ref, *refs):
    hids, rows, out_refs = refs[:hid_count], refs[hid_count:-4], refs[-4:]
    own = out_refs[0].shape[0]
    high, low = place_ref[2], place_ref[3]
    lefts = []
    for lead in (1 - high, high):
        for who in (1 - low, low):
            start = pl.multiple_of(who * own, own)
            lefts.append(
                jnp.concatenate([ref[lead, pl.ds(start, own), :] for ref in hids], axis=1)
            )
    total = jnp.dot(
        jnp.concatenate(lefts, axis=0), stacked_rows(rows), preferred_element_type=F32
    ).astype(BF16)
    for i in range(4):
        out_refs[i][...] = total[i * own : (i + 1) * own]


def grad_down(order, place, hids, rows, capacity, width, deps):
    own = hids[0].shape[1] // 2
    tile = tile_of(width, 1024)
    arrays, specs = zip(*[row_operand(capacity, tile, row) for row in rows])
    return order.call(
        functools.partial(grad_down_kernel, len(hids)),
        [smem()] + [fixed_spec(hid.shape) for hid in hids] + list(specs),
        [place, *hids, *arrays],
        deps,
        grid=(width // tile,),
        out_specs=[columns_spec(own, tile)] * 4,
        out_shape=[jax.ShapeDtypeStruct((own, width), BF16)] * 4,
        name="grad_down",
    )


def add_kernel(term_count, *refs):
    total = refs[0][...].astype(F32)
    for ref in refs[1:term_count]:
        total = total + ref[...].astype(F32)
    out_ref = refs[-1]
    out_ref[...] = total.astype(BF16).reshape(out_ref.shape)


def add_into(order, terms, columns, first, into, name):
    leads, own, width = terms[0].shape
    tile = tile_of(width, 1024)
    tiles = width // tile
    aliases, operands = {}, list(terms)
    in_specs = [pl.BlockSpec((1, own, tile), lambda i, n: (i, 0, n))] * len(terms)
    if into is not None:
        aliases = {len(operands): 0}
        operands.append(into)
        in_specs.append(anywhere())
    return order.call(
        functools.partial(add_kernel, len(terms)),
        in_specs,
        operands,
        grid=(leads, tiles),
        out_specs=pl.BlockSpec((own, tile), lambda i, n: (0, first // tile + i * tiles + n)),
        out_shape=jax.ShapeDtypeStruct((own, columns), BF16),
        input_output_aliases=aliases,
        name=name,
    )


def body(x_tokens, d_out, expert_ids, combine, w_stack):
    tokens, width = x_tokens.shape
    experts = lax.axis_size("expert")
    replicas = lax.axis_size("replica")
    planes = len(RING)
    columns = experts // planes
    capacity = 2 * tokens * expert_ids.shape[1] // experts

    position = lax.axis_index("expert")
    replica = lax.axis_index("replica")
    plane, column = position // columns, position % columns
    high, low = replica // 2, replica % 2
    ring_place = plane ^ (plane >> 1)
    sources = [(ring_place - s) & (planes - 1) for s in range(planes)]
    firsts = [(source ^ (source >> 1)) * columns for source in sources]
    place = jnp.stack([plane * columns, column, high, low, *firsts]).astype(jnp.int32)

    def along_ring(value):
        pairs = [
            (RING[i] * columns + c, RING[(i + 1) % planes] * columns + c)
            for i in range(planes)
            for c in range(columns)
        ]
        return lax.ppermute(value, "expert", pairs)

    def across(value, d, r):
        pairs = [
            ((p * columns + c) * replicas + k, (p * columns + (c ^ d)) * replicas + (k ^ r))
            for p in range(planes)
            for c in range(columns)
            for k in range(replicas)
        ]
        return lax.ppermute(value, ("expert", "replica"), pairs)

    def exchange(values, r):
        return [across(value, d + 1, r) for d, value in enumerate(values)]

    order = Order()
    meta = jnp.concatenate([expert_ids.T.astype(F32), combine.T], axis=0)

    x_0, picked, scales, hits = select_first(order, place, meta, x_tokens, columns, capacity)
    x_1 = along_ring(x_0)
    x_pieces = [(picked[0], None)] + [(value, None) for value in exchange(picked[1:], 0)]
    x_other = [(across(picked[0], 0, 2), None)] + [(v, None) for v in exchange(picked[1:], 2)]
    dy_pieces = []
    all_hits = place_all(order, meta, experts, capacity)
    x_block, d_block = x_1, d_out
    hids, acts_kept, acts_come = [], [], []
    dx = None
    dx_shape = (experts, capacity, width)
    factors = None
    for s in range(1, planes):
        x_next = along_ring(x_block) if s < planes - 1 else None
        waits = {
            1: [value for value, _ in x_pieces[1:]],
            2: [value for value, _ in x_other[:columns]],
            3: [value for value, _ in x_other[: 2 * columns]],
        }[s]
        d_next = along_ring(d_block) if s > 1 else None
        keep_x, keep_d, pairs, sends, again, scales, hits = select_both(
            order, place, x_block, scales, hits, d_block, columns, s == 1, waits
        )
        if s == 1:
            d_next = along_ring(again)
        come = exchange(pairs, 0)
        x_pieces += [(keep_x, None)] + [(value, 0) for value in come]
        dy_pieces += [(keep_d, None)] + [(value, 1) for value in come]
        x_other += [(across(keep_x, 0, 2), None)] + [(v, None) for v in exchange(sends, 2)]
        x_block, d_block = x_next, d_next
        if s == 1:
            hid, *factors = gate_up(order, x_pieces[: 2 * columns], w_stack, capacity)
            hids.append(hid)
        if s == 2:
            dx, send, keep = backward(
                order, place, dy_pieces[: 2 * columns], *factors, w_stack, columns, 0, None,
                dx_shape, [],
            )
            acts_kept.append(keep)
            acts_come.append(across(send, 0, 2))
    picked = select_last(order, scales, hits, d_block, columns, [])
    dy_pieces += [(picked[0], None)] + [(value, None) for value in exchange(picked[1:], 0)]
    hid, *factors = gate_up(
        order, x_pieces[2 * columns :], w_stack, capacity,
        [acts_come[0]] + [value for value, _ in x_other[2 * columns : 3 * columns]],
    )
    hids.append(hid)
    send_other, keep_other, send_own, down_own = grad_down(
        order, place, hids, dy_pieces, capacity, width,
        [value for value, _ in x_other[3 * columns :]],
    )
    dx, send, keep = backward(
        order, place, dy_pieces[2 * columns :], *factors, w_stack, columns, 2, dx, dx_shape,
        [],
    )
    acts_kept.append(keep)
    acts_come.append(across(send, 0, 2))
    returned = lax.all_to_all(dx, "expert", split_axis=0, concat_axis=0, tiled=True)
    summed = keep_other.astype(F32) + across(send_other, 0, 1).astype(F32)
    summed = summed.astype(BF16)
    down_y = across(summed, 0, 2)
    down_core = across(send_own, 0, 1)

    send, keep = grad_x(
        order, place, acts_kept + acts_come, x_pieces + x_other, capacity, width, [summed]
    )
    down_terms = [term[None] for term in (down_own, down_core, down_y)]
    g_rows = add_into(order, down_terms, 3 * width, 2 * width, None, "sum_down")
    g_rows = add_into(order, [keep, across(send, 0, 1)], 3 * width, 0, g_rows, "sum_x")
    d_tokens = merge(order, all_hits, returned.reshape(experts * capacity, width))
    return d_tokens, g_rows[None]


def solution(mesh):
    return jax.shard_map(
        body,
        mesh=mesh,
        in_specs=(
            P(("expert", "replica"), None),
            P(("expert", "replica"), None),
            P(("expert", "replica"), None),
            P(("expert", "replica"), None),
            P("expert", None, None),
        ),
        out_specs=(P(("expert", "replica"), None), P("expert", "replica", None)),
        check_vma=False,
    )
```

```python
import functools

import jax
import jax.numpy as jnp
from jax import lax
from jax.experimental import pallas as pl
from jax.experimental.pallas import tpu as pltpu
from jax.sharding import PartitionSpec as P

BF16 = jnp.bfloat16
F32 = jnp.float32
RING = (0, 1, 3, 2)
VMEM_LIMIT = 44 * 1024 * 1024


def params():
    return pltpu.CompilerParams(vmem_limit_bytes=VMEM_LIMIT)


def smem():
    return pl.BlockSpec(memory_space=pltpu.SMEM)


def anywhere():
    return pl.BlockSpec(memory_space=pl.ANY)


def inside():
    return pl.BlockSpec(memory_space=pltpu.VMEM)


def small_cost():
    return pl.CostEstimate(flops=1024, bytes_accessed=1024, transcendentals=0)


def tile_of(width, most):
    return most if width % most == 0 else width


class Order:
    def __init__(self):
        self.last = []

    def call(self, kernel, specs, operands, deps=(), cost=None, **options):
        extra = list(deps) + self.last
        count = len(operands)

        def body_of(*refs):
            kernel(*refs[:count], *refs[count + len(extra) :])

        outs = pl.pallas_call(
            body_of,
            in_specs=list(specs) + [anywhere()] * len(extra),
            compiler_params=params(),
            cost_estimate=cost or small_cost(),
            **options,
        )(*operands, *extra)
        self.last = [outs[-1] if isinstance(outs, (list, tuple)) else outs]
        return outs


def placing_of(base, own, meta, expert_count, capacity):
    tokens = meta.shape[1]
    id_first, id_second = meta[0:1, :], meta[1:2, :]
    scale_first, scale_second = meta[2:3, :], meta[3:4, :]
    row = lax.broadcasted_iota(jnp.int32, (max(16, expert_count), tokens), 0)
    expert = (base + jnp.bitwise_xor(row, own)).astype(F32)
    first = id_first == expert
    member = jnp.where(first | (id_second == expert), 1.0, 0.0)
    scale = jnp.where(first, scale_first, scale_second)
    earlier = lax.broadcasted_iota(jnp.int32, (tokens, tokens), 0)
    later = lax.broadcasted_iota(jnp.int32, (tokens, tokens), 1)
    before = jnp.where(earlier < later, 1.0, 0.0).astype(BF16)
    rank = jnp.dot(member.astype(BF16), before, preferred_element_type=F32)
    rank = jnp.where(member > 0.0, rank, -1.0)
    slot = lax.broadcasted_iota(jnp.int32, (capacity, tokens), 0).astype(F32)
    hits, scales = [], []
    for d in range(expert_count):
        hit = jnp.where(rank[d : d + 1, :] == slot, 1.0, 0.0)
        hits.append(hit)
        scales.append(jnp.sum(hit * scale[d : d + 1, :], axis=1, keepdims=True))
    return jnp.concatenate(hits, axis=0), jnp.concatenate(scales, axis=0)


def rounded(value):
    return value.astype(BF16).astype(F32)


def meta_columns(meta):
    scale = meta[2:4, :]
    top = rounded(scale)
    middle = rounded(scale - top)
    rest = scale - top - middle
    filler = jnp.zeros((120, meta.shape[1]), F32)
    return jnp.concatenate([meta[0:2, :], top, middle, rest, filler], axis=0).T.astype(BF16)


def meta_rows(columns):
    rows = columns.astype(F32).T
    scale = rows[2:4, :] + rows[4:6, :] + rows[6:8, :]
    return jnp.concatenate([rows[0:2, :], scale], axis=0)


def first_kernel(columns, capacity, place_ref, meta_ref, x_ref, *refs):
    x_out, keep_ref, send_refs = refs[0], refs[1], refs[2 : columns + 1]
    scales_ref, hits_ref = refs[columns + 1 :]
    width = x_ref.shape[1]
    meta = meta_ref[...]
    x = x_ref[...]
    x_out[:, :width] = x
    x_out[:, width:] = meta_columns(meta)
    hits, scales = placing_of(place_ref[0], place_ref[1], meta, columns, capacity)
    hits = hits.astype(BF16)
    hits_ref[...] = hits
    scales_ref[...] = jnp.broadcast_to(scales, scales_ref.shape)
    picked = jnp.dot(hits, x, preferred_element_type=F32).astype(BF16)
    keep_ref[...] = picked[:capacity, :]
    for d in range(1, columns):
        send_refs[d - 1][...] = picked[d * capacity : (d + 1) * capacity, :]


def select_first(order, place, meta, x, columns, capacity):
    tokens, width = x.shape
    count = columns * capacity
    outs = order.call(
        functools.partial(first_kernel, columns, capacity),
        [smem(), inside(), inside()],
        [place, meta, x],
        out_specs=[inside()] * (columns + 3),
        out_shape=[jax.ShapeDtypeStruct((tokens, width + 128), BF16)]
        + [jax.ShapeDtypeStruct((capacity, width), BF16)] * columns
        + [
            jax.ShapeDtypeStruct((count, 128), F32),
            jax.ShapeDtypeStruct((count, tokens), BF16),
        ],
        name="select_first",
    )
    return outs[0], outs[1:-2], outs[-2], outs[-1]


def both_kernel(columns, capacity, again, place_ref, x_ref, old_scales, old_hits, d_ref, *refs):
    keep_x, keep_d, refs = refs[0], refs[1], refs[2:]
    pair_refs, send_refs, refs = refs[: columns - 1], refs[columns - 1 : 2 * columns - 2], refs[2 * columns - 2 :]
    scales_ref, hits_ref = refs[-2:]
    width = d_ref.shape[1]
    rows = d_ref[...]
    if again:
        refs[0][...] = rows
    meta = meta_rows(x_ref[:, width:])
    hits, scales = placing_of(place_ref[0], place_ref[1], meta, columns, capacity)
    hits = hits.astype(BF16)
    hits_ref[...] = hits
    scales_ref[...] = jnp.broadcast_to(scales, scales_ref.shape)
    x = jnp.dot(hits, x_ref[:, :width], preferred_element_type=F32).astype(BF16)
    dy = jnp.dot(old_hits[...], rows, preferred_element_type=F32)
    dy = (dy * old_scales[:, 0:1]).astype(BF16)
    keep_x[...] = x[:capacity, :]
    keep_d[...] = dy[:capacity, :]
    for d in range(1, columns):
        part = slice(d * capacity, (d + 1) * capacity)
        pair_refs[d - 1][0] = x[part, :]
        pair_refs[d - 1][1] = dy[part, :]
        send_refs[d - 1][...] = x[part, :]


def select_both(order, place, x, scales, hits, d_rows, columns, again, deps):
    tokens, width = d_rows.shape
    count = hits.shape[0]
    capacity = count // columns
    shapes = [(capacity, width)] * 2
    shapes += [(2, capacity, width)] * (columns - 1) + [(capacity, width)] * (columns - 1)
    shapes += [(tokens, width)] * again
    outs = order.call(
        functools.partial(both_kernel, columns, capacity, again),
        [smem()] + [inside()] * 4,
        [place, x, scales, hits, d_rows],
        deps,
        out_specs=[inside()] * (len(shapes) + 2),
        out_shape=[jax.ShapeDtypeStruct(shape, BF16) for shape in shapes]
        + [
            jax.ShapeDtypeStruct((count, 128), F32),
            jax.ShapeDtypeStruct((count, tokens), BF16),
        ],
        name="select_both",
    )
    pairs, sends = outs[2 : columns + 1], outs[columns + 1 : 2 * columns]
    return outs[0], outs[1], pairs, sends, outs[-3], outs[-2], outs[-1]


def last_kernel(columns, scales_ref, hits_ref, d_ref, *out_refs):
    capacity = out_refs[0].shape[0]
    picked = jnp.dot(hits_ref[...], d_ref[...], preferred_element_type=F32)
    picked = (picked * scales_ref[:, 0:1]).astype(BF16)
    for d in range(columns):
        out_refs[d][...] = picked[d * capacity : (d + 1) * capacity, :]


def select_last(order, scales, hits, d_rows, columns, deps):
    width = d_rows.shape[1]
    capacity = hits.shape[0] // columns
    return order.call(
        functools.partial(last_kernel, columns),
        [inside()] * 3,
        [scales, hits, d_rows],
        deps,
        out_specs=[inside()] * columns,
        out_shape=[jax.ShapeDtypeStruct((capacity, width), BF16)] * columns,
        name="select_last",
    )


def place_all_kernel(experts, capacity, meta_ref, hits_ref):
    hits, _ = placing_of(0, 0, meta_ref[...], experts, capacity)
    hits_ref[...] = hits.astype(BF16)


def place_all(order, meta, experts, capacity):
    return order.call(
        functools.partial(place_all_kernel, experts, capacity),
        [inside()],
        [meta],
        out_specs=inside(),
        out_shape=jax.ShapeDtypeStruct((experts * capacity, meta.shape[1]), BF16),
        name="place_all",
    )


def merge_kernel(hits_ref, slots_ref, out_ref):
    out_ref[...] = lax.dot_general(
        hits_ref[...], slots_ref[...], (((0,), (0,)), ((), ())), preferred_element_type=F32
    ).astype(BF16)


def merge(order, hits, slots):
    return order.call(
        merge_kernel,
        [inside(), inside()],
        [hits, slots],
        out_shape=jax.ShapeDtypeStruct((hits.shape[1], slots.shape[1]), BF16),
        out_specs=inside(),
        name="merge",
    )


def start_rows(refs, target, sems):
    capacity = target.shape[0] // len(refs)
    copies = []
    for i, (ref, which) in enumerate(refs):
        source = ref if which is None else ref.at[which]
        rows = target.at[pl.ds(i * capacity, capacity)]
        copies.append(pltpu.make_async_copy(source, rows, sems.at[i]))
    for copy in copies:
        copy.start()
    return copies


def split_pieces(pieces):
    return [array for array, _ in pieces], [which for _, which in pieces]


def start_weights(w_ref, units, part, target, sem):
    width = target.shape[-1]
    copy = pltpu.make_async_copy(w_ref.at[0, units, pl.ds(part * width, width)], target, sem)
    copy.start()
    return copy


def gate_up_kernel(whiches, *refs):
    count = len(whiches)
    x_refs, w_ref, refs = refs[:count], refs[count], refs[count + 1 :]
    hid_ref, act_ref, slope_ref, x_all, x_turned, w_pair, sems, w_sems = refs
    half = hid_ref.shape[1]
    rows = start_rows(list(zip(x_refs, whiches)), x_all, sems)
    weights = []
    for t in range(2):
        for k in range(2):
            units = pl.ds(t * half, half)
            weights.append(start_weights(w_ref, units, k, w_pair.at[t, k], w_sems.at[2 * t + k]))
    for copy in rows:
        copy.wait()
    x_turned[...] = x_all[...].T
    for t in range(2):
        weights[2 * t].wait()
        gate = jnp.dot(w_pair[t, 0], x_turned[...], preferred_element_type=F32)
        weights[2 * t + 1].wait()
        up = jnp.dot(w_pair[t, 1], x_turned[...], preferred_element_type=F32)
        sig = jax.nn.sigmoid(gate)
        act = gate * sig
        hid_ref[t] = (act * up).astype(BF16)
        act_ref[t] = act
        slope_ref[t] = up * sig * (1.0 + gate * (1.0 - sig))


def gate_up(order, pieces, w_stack, capacity, deps=()):
    arrays, whiches = split_pieces(pieces)
    width = arrays[0].shape[-1]
    rows, hidden = len(pieces) * capacity, w_stack.shape[1]
    return order.call(
        functools.partial(gate_up_kernel, whiches),
        [anywhere()] * (len(pieces) + 1),
        [*arrays, w_stack],
        deps,
        out_specs=[inside()] * 3,
        out_shape=[
            jax.ShapeDtypeStruct((2, hidden // 2, rows), BF16),
            jax.ShapeDtypeStruct((2, hidden // 2, rows), F32),
            jax.ShapeDtypeStruct((2, hidden // 2, rows), F32),
        ],
        scratch_shapes=[
            pltpu.VMEM((rows, width), BF16),
            pltpu.VMEM((width, rows), BF16),
            pltpu.VMEM((2, 2, hidden // 2, width), BF16),
            pltpu.SemaphoreType.DMA((len(pieces),)),
            pltpu.SemaphoreType.DMA((4,)),
        ],
        name="gate_up",
    )


def backward_kernel(whiches, columns, first_step, place_ref, *refs):
    count = len(whiches)
    dy_refs, (act_ref, slope_ref, w_ref), refs = refs[:count], refs[count : count + 3], refs[count + 3 :]
    dx_ref, send_ref, keep_ref, dy_all, dy_turned, total, w_all, sems, w_sems, out_sems = refs[-10:]
    half = act_ref.shape[1]
    capacity = dx_ref.shape[1]
    rows = start_rows(list(zip(dy_refs, whiches)), dy_all, sems)
    halves = [jnp.bitwise_xor(place_ref[2], 1 - t) for t in range(2)]
    weights = []
    for t, which in enumerate(halves):
        units = pl.ds(pl.multiple_of(which * half, half), half)
        for k in (2, 0, 1):
            weights.append(start_weights(w_ref, units, k, w_all.at[t, k], w_sems.at[3 * t + k]))
    for copy in rows:
        copy.wait()
    dy_turned[...] = dy_all[...].T
    sums = None
    for t, which in enumerate(halves):
        weights[3 * t].wait()
        d_hidden = jnp.dot(w_all[t, 2], dy_turned[...], preferred_element_type=F32)
        d_up = (d_hidden * act_ref[which]).astype(BF16)
        d_gate = (d_hidden * slope_ref[which]).astype(BF16)
        out_ref = (send_ref, keep_ref)[t]
        out_ref[:half, :] = d_gate
        out_ref[half:, :] = d_up
        for k, factor in enumerate((d_gate, d_up)):
            weights[3 * t + 1 + k].wait()
            part = jnp.dot(factor.T, w_all[t, k], preferred_element_type=F32)
            sums = part if sums is None else sums + part
    total[...] = sums.astype(BF16)
    copies = []
    for i in range(count):
        block = place_ref[4 + first_step + i // columns] + jnp.bitwise_xor(
            place_ref[1], i % columns
        )
        copies.append(
            pltpu.make_async_copy(
                total.at[pl.ds(i * capacity, capacity)], dx_ref.at[block], out_sems.at[i]
            )
        )
    for copy in copies:
        copy.start()
    for copy in copies:
        copy.wait()


def backward(order, place, pieces, act, slope, w_stack, columns, first_step, dx, shape, deps):
    arrays, whiches = split_pieces(pieces)
    count = len(pieces)
    capacity, width = shape[1:]
    rows, hidden = count * capacity, w_stack.shape[1]
    operands = [place, *arrays, act, slope, w_stack]
    specs = [smem()] + [anywhere()] * count + [inside()] * 2 + [anywhere()]
    aliases = {}
    if dx is not None:
        aliases = {len(operands): 0}
        operands.append(dx)
        specs.append(anywhere())
    return order.call(
        functools.partial(backward_kernel, whiches, columns, first_step),
        specs,
        operands,
        deps,
        out_specs=[anywhere(), inside(), inside()],
        out_shape=[jax.ShapeDtypeStruct(shape, BF16)]
        + [jax.ShapeDtypeStruct((hidden, rows), BF16)] * 2,
        scratch_shapes=[
            pltpu.VMEM((rows, width), BF16),
            pltpu.VMEM((width, rows), BF16),
            pltpu.VMEM((rows, width), BF16),
            pltpu.VMEM((2, 3, hidden // 2, width), BF16),
            pltpu.SemaphoreType.DMA((count,)),
            pltpu.SemaphoreType.DMA((6,)),
            pltpu.SemaphoreType.DMA((count,)),
        ],
        input_output_aliases=aliases,
        name="backward",
    )


def side_by_side(refs, whiches, columns):
    return jnp.concatenate(
        [
            ref[:, columns] if which is None else ref[which, :, columns]
            for ref, which in zip(refs, whiches)
        ],
        axis=0,
    )


def grad_x_kernel(act_count, whiches, place_ref, *refs):
    acts, rows = refs[:act_count], refs[act_count:-2]
    send_ref, keep_ref = refs[-2:]
    own, width = send_ref.shape[1:]
    low = place_ref[3]
    lefts = []
    for who in (1 - low, low):
        for lead in range(2):
            start = pl.multiple_of((2 * lead + who) * own, own)
            lefts.append(jnp.concatenate([ref[pl.ds(start, own), :] for ref in acts], axis=1))
    left = jnp.concatenate(lefts, axis=0)
    tile = tile_of(width, 512)
    for n in range(0, width, tile):
        columns = slice(n, n + tile)
        right = side_by_side(rows, whiches, columns)
        total = jnp.dot(left, right, preferred_element_type=F32).astype(BF16)
        for lead in range(2):
            send_ref[lead, :, columns] = total[lead * own : (lead + 1) * own]
            keep_ref[lead, :, columns] = total[(2 + lead) * own : (3 + lead) * own]


def grad_x(order, place, acts, rows, width, deps):
    own = acts[0].shape[0] // 4
    arrays, whiches = split_pieces(rows)
    return order.call(
        functools.partial(grad_x_kernel, len(acts), whiches),
        [smem()] + [inside()] * (len(acts) + len(rows)),
        [place, *acts, *arrays],
        deps,
        out_specs=[inside()] * 2,
        out_shape=[jax.ShapeDtypeStruct((2, own, width), BF16)] * 2,
        name="grad_x",
    )


def grad_down_kernel(hid_count, whiches, place_ref, *refs):
    hids, rows, out_refs = refs[:hid_count], refs[hid_count:-4], refs[-4:]
    own, width = out_refs[0].shape
    high, low = place_ref[2], place_ref[3]
    lefts = []
    for lead in (1 - high, high):
        for who in (1 - low, low):
            start = pl.multiple_of(who * own, own)
            lefts.append(
                jnp.concatenate([ref[lead, pl.ds(start, own), :] for ref in hids], axis=1)
            )
    left = jnp.concatenate(lefts, axis=0)
    tile = tile_of(width, 512)
    for n in range(0, width, tile):
        columns = slice(n, n + tile)
        right = side_by_side(rows, whiches, columns)
        total = jnp.dot(left, right, preferred_element_type=F32).astype(BF16)
        for i in range(4):
            out_refs[i][:, columns] = total[i * own : (i + 1) * own]


def grad_down(order, place, hids, rows, width, deps):
    own = hids[0].shape[1] // 2
    arrays, whiches = split_pieces(rows)
    return order.call(
        functools.partial(grad_down_kernel, len(hids), whiches),
        [smem()] + [inside()] * (len(hids) + len(rows)),
        [place, *hids, *arrays],
        deps,
        out_specs=[inside()] * 4,
        out_shape=[jax.ShapeDtypeStruct((own, width), BF16)] * 4,
        name="grad_down",
    )


def sum_kernel(down_count, keep_ref, come_ref, *refs):
    downs, out_ref = refs[:down_count], refs[down_count]
    width = keep_ref.shape[2]
    for lead in range(2):
        total = keep_ref[lead].astype(F32) + come_ref[lead].astype(F32)
        out_ref[:, lead * width : (lead + 1) * width] = total.astype(BF16)
    total = downs[0][...].astype(F32)
    for ref in downs[1:]:
        total = total + ref[...].astype(F32)
    out_ref[:, 2 * width :] = total.astype(BF16)


def sum_all(order, keep, come, downs):
    _, own, width = keep.shape
    return order.call(
        functools.partial(sum_kernel, len(downs)),
        [inside()] * (2 + len(downs)),
        [keep, come, *downs],
        cost=pl.CostEstimate(flops=1024, bytes_accessed=1 << 26, transcendentals=0),
        out_specs=inside(),
        out_shape=jax.ShapeDtypeStruct((own, 3 * width), BF16),
        name="sum_all",
    )


def body(x_tokens, d_out, expert_ids, combine, w_stack):
    tokens, width = x_tokens.shape
    experts = lax.axis_size("expert")
    replicas = lax.axis_size("replica")
    planes = len(RING)
    columns = experts // planes
    capacity = 2 * tokens * expert_ids.shape[1] // experts

    position = lax.axis_index("expert")
    replica = lax.axis_index("replica")
    plane, column = position // columns, position % columns
    high, low = replica // 2, replica % 2
    ring_place = plane ^ (plane >> 1)
    sources = [(ring_place - s) & (planes - 1) for s in range(planes)]
    firsts = [(source ^ (source >> 1)) * columns for source in sources]
    place = jnp.stack([plane * columns, column, high, low, *firsts]).astype(jnp.int32)

    def along_ring(value):
        pairs = [
            (RING[i] * columns + c, RING[(i + 1) % planes] * columns + c)
            for i in range(planes)
            for c in range(columns)
        ]
        return lax.ppermute(value, "expert", pairs)

    def across(value, d, r):
        pairs = [
            ((p * columns + c) * replicas + k, (p * columns + (c ^ d)) * replicas + (k ^ r))
            for p in range(planes)
            for c in range(columns)
            for k in range(replicas)
        ]
        return lax.ppermute(value, ("expert", "replica"), pairs)

    def exchange(values, r):
        return [across(value, d + 1, r) for d, value in enumerate(values)]

    order = Order()
    meta = jnp.concatenate([expert_ids.T.astype(F32), combine.T], axis=0)

    x_0, picked, scales, hits = select_first(order, place, meta, x_tokens, columns, capacity)
    x_1 = along_ring(x_0)
    x_pieces = [(picked[0], None)] + [(value, None) for value in exchange(picked[1:], 0)]
    x_other = [(across(picked[0], 0, 2), None)] + [(v, None) for v in exchange(picked[1:], 2)]
    dy_pieces = []
    all_hits = place_all(order, meta, experts, capacity)
    x_block, d_block = x_1, d_out
    hids, acts_kept, acts_come = [], [], []
    dx = None
    dx_shape = (experts, capacity, width)
    factors = None
    for s in range(1, planes):
        x_next = along_ring(x_block) if s < planes - 1 else None
        waits = {
            1: [value for value, _ in x_pieces[1:] + x_other],
            2: [value for value, _ in x_other[columns:]],
            3: [],
        }[s]
        d_next = along_ring(d_block) if s > 1 else None
        keep_x, keep_d, pairs, sends, again, scales, hits = select_both(
            order, place, x_block, scales, hits, d_block, columns, s == 1, waits
        )
        if s == 1:
            d_next = along_ring(again)
        come = exchange(pairs, 0)
        x_pieces += [(keep_x, None)] + [(value, 0) for value in come]
        dy_pieces += [(keep_d, None)] + [(value, 1) for value in come]
        x_other += [(across(keep_x, 0, 2), None)] + [(v, None) for v in exchange(sends, 2)]
        x_block, d_block = x_next, d_next
        if s == 1:
            hid, *factors = gate_up(order, x_pieces[: 2 * columns], w_stack, capacity)
            hids.append(hid)
        if s == 2:
            dx, send, keep = backward(
                order, place, dy_pieces[: 2 * columns], *factors, w_stack, columns, 0, None,
                dx_shape, [value for value, _ in x_other[2 * columns : 3 * columns]],
            )
            acts_kept.append(keep)
            acts_come.append(across(send, 0, 2))
    picked = select_last(order, scales, hits, d_block, columns, [])
    dy_pieces += [(picked[0], None)] + [(value, None) for value in exchange(picked[1:], 0)]
    hid, *factors = gate_up(order, x_pieces[2 * columns :], w_stack, capacity)
    hids.append(hid)
    send_other, keep_other, send_own, down_own = grad_down(
        order, place, hids, dy_pieces, width,
        [acts_come[0]] + [value for value, _ in x_other[3 * columns :]],
    )
    dx, send, keep = backward(
        order, place, dy_pieces[2 * columns :], *factors, w_stack, columns, 2, dx, dx_shape, [],
    )
    acts_kept.append(keep)
    acts_come.append(across(send, 0, 2))
    returned = lax.all_to_all(dx, "expert", split_axis=0, concat_axis=0, tiled=True)
    summed = keep_other.astype(F32) + across(send_other, 0, 1).astype(F32)
    summed = summed.astype(BF16)
    down_y = across(summed, 0, 2)
    down_core = across(send_own, 0, 1)

    send, keep = grad_x(
        order, place, acts_kept + acts_come, x_pieces + x_other, width, [summed, down_core]
    )
    g_rows = sum_all(order, keep, across(send, 0, 1), [down_own, down_core, down_y])
    d_tokens = merge(order, all_hits, returned.reshape(experts * capacity, width))
    return d_tokens, g_rows[None]


def solution(mesh):
    return jax.shard_map(
        body,
        mesh=mesh,
        in_specs=(
            P(("expert", "replica"), None),
            P(("expert", "replica"), None),
            P(("expert", "replica"), None),
            P(("expert", "replica"), None),
            P("expert", None, None),
        ),
        out_specs=(P(("expert", "replica"), None), P("expert", "replica", None)),
        check_vma=False,
    )
```

```python
import functools

import jax
import jax.numpy as jnp
from jax import lax
from jax.experimental import pallas as pl
from jax.experimental.pallas import tpu as pltpu
from jax.sharding import PartitionSpec as P

BF16 = jnp.bfloat16
F32 = jnp.float32
RING = (0, 1, 3, 2)
VMEM_LIMIT = 44 * 1024 * 1024


def params():
    return pltpu.CompilerParams(vmem_limit_bytes=VMEM_LIMIT)


def smem():
    return pl.BlockSpec(memory_space=pltpu.SMEM)


def anywhere():
    return pl.BlockSpec(memory_space=pl.ANY)


def inside():
    return pl.BlockSpec(memory_space=pltpu.VMEM)


def small_cost():
    return pl.CostEstimate(flops=1024, bytes_accessed=1024, transcendentals=0)


def tile_of(width, most):
    return most if width % most == 0 else width


def large_cost():
    return pl.CostEstimate(flops=40 * 10**9, bytes_accessed=1 << 27, transcendentals=0)


class Order:
    def __init__(self):
        self.last = []

    def call(self, kernel, specs, operands, deps=(), cost=None, **options):
        extra = list(deps) + self.last
        count = len(operands)

        def body_of(*refs):
            kernel(*refs[:count], *refs[count + len(extra) :])

        outs = pl.pallas_call(
            body_of,
            in_specs=list(specs) + [anywhere()] * len(extra),
            compiler_params=params(),
            cost_estimate=cost or small_cost(),
            **options,
        )(*operands, *extra)
        self.last = [outs[-1] if isinstance(outs, (list, tuple)) else outs]
        return outs


def placing_of(base, own, meta, expert_count, capacity):
    tokens = meta.shape[1]
    id_first, id_second = meta[0:1, :], meta[1:2, :]
    scale_first, scale_second = meta[2:3, :], meta[3:4, :]
    row = lax.broadcasted_iota(jnp.int32, (max(16, expert_count), tokens), 0)
    expert = (base + jnp.bitwise_xor(row, own)).astype(F32)
    first = id_first == expert
    member = jnp.where(first | (id_second == expert), 1.0, 0.0)
    scale = jnp.where(first, scale_first, scale_second)
    earlier = lax.broadcasted_iota(jnp.int32, (tokens, tokens), 0)
    later = lax.broadcasted_iota(jnp.int32, (tokens, tokens), 1)
    before = jnp.where(earlier < later, 1.0, 0.0).astype(BF16)
    rank = jnp.dot(member.astype(BF16), before, preferred_element_type=F32)
    rank = jnp.where(member > 0.0, rank, -1.0)
    slot = lax.broadcasted_iota(jnp.int32, (capacity, tokens), 0).astype(F32)
    hits, scales = [], []
    for d in range(expert_count):
        hit = jnp.where(rank[d : d + 1, :] == slot, 1.0, 0.0)
        hits.append(hit)
        scales.append(jnp.sum(hit * scale[d : d + 1, :], axis=1, keepdims=True))
    return jnp.concatenate(hits, axis=0), jnp.concatenate(scales, axis=0)


def rounded(value):
    return value.astype(BF16).astype(F32)


def meta_columns(meta):
    scale = meta[2:4, :]
    top = rounded(scale)
    middle = rounded(scale - top)
    rest = scale - top - middle
    filler = jnp.zeros((120, meta.shape[1]), F32)
    return jnp.concatenate([meta[0:2, :], top, middle, rest, filler], axis=0).T.astype(BF16)


def meta_rows(columns):
    rows = columns.astype(F32).T
    scale = rows[2:4, :] + rows[4:6, :] + rows[6:8, :]
    return jnp.concatenate([rows[0:2, :], scale], axis=0)


def first_kernel(columns, capacity, place_ref, meta_ref, x_ref, *refs):
    x_out, keep_ref, send_refs = refs[0], refs[1], refs[2 : columns + 1]
    scales_ref, hits_ref = refs[columns + 1 :]
    width = x_ref.shape[1]
    meta = meta_ref[...]
    x = x_ref[...]
    x_out[:, :width] = x
    x_out[:, width:] = meta_columns(meta)
    hits, scales = placing_of(place_ref[0], place_ref[1], meta, columns, capacity)
    hits = hits.astype(BF16)
    hits_ref[...] = hits
    scales_ref[...] = jnp.broadcast_to(scales, scales_ref.shape)
    picked = jnp.dot(hits, x, preferred_element_type=F32).astype(BF16)
    keep_ref[...] = picked[:capacity, :]
    for d in range(1, columns):
        send_refs[d - 1][...] = picked[d * capacity : (d + 1) * capacity, :]


def select_first(order, place, meta, x, columns, capacity):
    tokens, width = x.shape
    count = columns * capacity
    outs = order.call(
        functools.partial(first_kernel, columns, capacity),
        [smem(), inside(), inside()],
        [place, meta, x],
        out_specs=[inside()] * (columns + 3),
        out_shape=[jax.ShapeDtypeStruct((tokens, width + 128), BF16)]
        + [jax.ShapeDtypeStruct((capacity, width), BF16)] * columns
        + [
            jax.ShapeDtypeStruct((count, 128), F32),
            jax.ShapeDtypeStruct((count, tokens), BF16),
        ],
        name="select_first",
    )
    return outs[0], outs[1:-2], outs[-2], outs[-1]


def both_kernel(columns, capacity, again, place_ref, x_ref, old_scales, old_hits, d_ref, *refs):
    keep_x, keep_d, refs = refs[0], refs[1], refs[2:]
    pair_refs, send_refs, refs = refs[: columns - 1], refs[columns - 1 : 2 * columns - 2], refs[2 * columns - 2 :]
    scales_ref, hits_ref = refs[-2:]
    width = d_ref.shape[1]
    rows = d_ref[...]
    if again:
        refs[0][...] = rows
    meta = meta_rows(x_ref[:, width:])
    hits, scales = placing_of(place_ref[0], place_ref[1], meta, columns, capacity)
    hits = hits.astype(BF16)
    hits_ref[...] = hits
    scales_ref[...] = jnp.broadcast_to(scales, scales_ref.shape)
    x = jnp.dot(hits, x_ref[:, :width], preferred_element_type=F32).astype(BF16)
    dy = jnp.dot(old_hits[...], rows, preferred_element_type=F32)
    dy = (dy * old_scales[:, 0:1]).astype(BF16)
    keep_x[...] = x[:capacity, :]
    keep_d[...] = dy[:capacity, :]
    for d in range(1, columns):
        part = slice(d * capacity, (d + 1) * capacity)
        pair_refs[d - 1][0] = x[part, :]
        pair_refs[d - 1][1] = dy[part, :]
        send_refs[d - 1][...] = x[part, :]


def select_both(order, place, x, scales, hits, d_rows, columns, again, deps):
    tokens, width = d_rows.shape
    count = hits.shape[0]
    capacity = count // columns
    shapes = [(capacity, width)] * 2
    shapes += [(2, capacity, width)] * (columns - 1) + [(capacity, width)] * (columns - 1)
    shapes += [(tokens, width)] * again
    outs = order.call(
        functools.partial(both_kernel, columns, capacity, again),
        [smem()] + [inside()] * 4,
        [place, x, scales, hits, d_rows],
        deps,
        out_specs=[inside()] * (len(shapes) + 2),
        out_shape=[jax.ShapeDtypeStruct(shape, BF16) for shape in shapes]
        + [
            jax.ShapeDtypeStruct((count, 128), F32),
            jax.ShapeDtypeStruct((count, tokens), BF16),
        ],
        name="select_both",
    )
    pairs, sends = outs[2 : columns + 1], outs[columns + 1 : 2 * columns]
    return outs[0], outs[1], pairs, sends, outs[-3], outs[-2], outs[-1]


def last_kernel(columns, scales_ref, hits_ref, d_ref, *out_refs):
    capacity = out_refs[0].shape[0]
    picked = jnp.dot(hits_ref[...], d_ref[...], preferred_element_type=F32)
    picked = (picked * scales_ref[:, 0:1]).astype(BF16)
    for d in range(columns):
        out_refs[d][...] = picked[d * capacity : (d + 1) * capacity, :]


def select_last(order, scales, hits, d_rows, columns, deps):
    width = d_rows.shape[1]
    capacity = hits.shape[0] // columns
    return order.call(
        functools.partial(last_kernel, columns),
        [inside()] * 3,
        [scales, hits, d_rows],
        deps,
        out_specs=[inside()] * columns,
        out_shape=[jax.ShapeDtypeStruct((capacity, width), BF16)] * columns,
        name="select_last",
    )


def place_all_kernel(experts, capacity, meta_ref, hits_ref):
    hits, _ = placing_of(0, 0, meta_ref[...], experts, capacity)
    hits_ref[...] = hits.astype(BF16)


def place_all(order, meta, experts, capacity):
    return order.call(
        functools.partial(place_all_kernel, experts, capacity),
        [inside()],
        [meta],
        out_specs=inside(),
        out_shape=jax.ShapeDtypeStruct((experts * capacity, meta.shape[1]), BF16),
        name="place_all",
    )


def merge_kernel(hits_ref, slots_ref, out_ref):
    out_ref[...] = lax.dot_general(
        hits_ref[...], slots_ref[...], (((0,), (0,)), ((), ())), preferred_element_type=F32
    ).astype(BF16)


def merge(order, hits, slots):
    return order.call(
        merge_kernel,
        [inside(), inside()],
        [hits, slots],
        out_shape=jax.ShapeDtypeStruct((hits.shape[1], slots.shape[1]), BF16),
        out_specs=inside(),
        name="merge",
    )


def start_rows(refs, target, sems):
    capacity = target.shape[0] // len(refs)
    copies = []
    for i, (ref, which) in enumerate(refs):
        source = ref if which is None else ref.at[which]
        rows = target.at[pl.ds(i * capacity, capacity)]
        copies.append(pltpu.make_async_copy(source, rows, sems.at[i]))
    for copy in copies:
        copy.start()
    return copies


def split_pieces(pieces):
    return [array for array, _ in pieces], [which for _, which in pieces]


def start_weights(w_ref, units, part, target, sem):
    width = target.shape[-1]
    copy = pltpu.make_async_copy(w_ref.at[0, units, pl.ds(part * width, width)], target, sem)
    copy.start()
    return copy


def gate_up_kernel(whiches, *refs):
    count = len(whiches)
    x_refs, w_ref, refs = refs[:count], refs[count], refs[count + 1 :]
    hid_ref, act_ref, slope_ref, x_all, x_turned, w_pair, sems, w_sems = refs
    half = hid_ref.shape[1]
    rows = start_rows(list(zip(x_refs, whiches)), x_all, sems)
    weights = []
    for t in range(2):
        for k in range(2):
            units = pl.ds(t * half, half)
            weights.append(start_weights(w_ref, units, k, w_pair.at[t, k], w_sems.at[2 * t + k]))
    for copy in rows:
        copy.wait()
    x_turned[...] = x_all[...].T
    for t in range(2):
        weights[2 * t].wait()
        gate = jnp.dot(w_pair[t, 0], x_turned[...], preferred_element_type=F32)
        weights[2 * t + 1].wait()
        up = jnp.dot(w_pair[t, 1], x_turned[...], preferred_element_type=F32)
        sig = jax.nn.sigmoid(gate)
        act = gate * sig
        hid_ref[t] = (act * up).astype(BF16)
        act_ref[t] = act
        slope_ref[t] = up * sig * (1.0 + gate * (1.0 - sig))


def gate_up(order, pieces, w_stack, capacity, cost=None):
    arrays, whiches = split_pieces(pieces)
    width = arrays[0].shape[-1]
    rows, hidden = len(pieces) * capacity, w_stack.shape[1]
    return order.call(
        functools.partial(gate_up_kernel, whiches),
        [anywhere()] * (len(pieces) + 1),
        [*arrays, w_stack],
        cost=cost,
        out_specs=[inside()] * 3,
        out_shape=[
            jax.ShapeDtypeStruct((2, hidden // 2, rows), BF16),
            jax.ShapeDtypeStruct((2, hidden // 2, rows), F32),
            jax.ShapeDtypeStruct((2, hidden // 2, rows), F32),
        ],
        scratch_shapes=[
            pltpu.VMEM((rows, width), BF16),
            pltpu.VMEM((width, rows), BF16),
            pltpu.VMEM((2, 2, hidden // 2, width), BF16),
            pltpu.SemaphoreType.DMA((len(pieces),)),
            pltpu.SemaphoreType.DMA((4,)),
        ],
        name="gate_up",
    )


def backward_kernel(whiches, columns, first_step, place_ref, *refs):
    count = len(whiches)
    dy_refs, (act_ref, slope_ref, w_ref), refs = refs[:count], refs[count : count + 3], refs[count + 3 :]
    dx_ref, send_ref, keep_ref, dy_all, dy_turned, total, w_all, sems, w_sems, out_sems = refs[-10:]
    half = act_ref.shape[1]
    capacity = dx_ref.shape[1]
    rows = start_rows(list(zip(dy_refs, whiches)), dy_all, sems)
    halves = [jnp.bitwise_xor(place_ref[2], 1 - t) for t in range(2)]
    weights = []
    for t, which in enumerate(halves):
        units = pl.ds(pl.multiple_of(which * half, half), half)
        for k in (2, 0, 1):
            weights.append(start_weights(w_ref, units, k, w_all.at[t, k], w_sems.at[3 * t + k]))
    for copy in rows:
        copy.wait()
    dy_turned[...] = dy_all[...].T
    sums = None
    for t, which in enumerate(halves):
        weights[3 * t].wait()
        d_hidden = jnp.dot(w_all[t, 2], dy_turned[...], preferred_element_type=F32)
        d_up = (d_hidden * act_ref[which]).astype(BF16)
        d_gate = (d_hidden * slope_ref[which]).astype(BF16)
        out_ref = (send_ref, keep_ref)[t]
        out_ref[:half, :] = d_gate
        out_ref[half:, :] = d_up
        for k, factor in enumerate((d_gate, d_up)):
            weights[3 * t + 1 + k].wait()
            part = jnp.dot(factor.T, w_all[t, k], preferred_element_type=F32)
            sums = part if sums is None else sums + part
    total[...] = sums.astype(BF16)
    copies = []
    for i in range(count):
        block = place_ref[4 + first_step + i // columns] + jnp.bitwise_xor(
            place_ref[1], i % columns
        )
        copies.append(
            pltpu.make_async_copy(
                total.at[pl.ds(i * capacity, capacity)], dx_ref.at[block], out_sems.at[i]
            )
        )
    for copy in copies:
        copy.start()
    for copy in copies:
        copy.wait()


def backward(order, place, pieces, act, slope, w_stack, columns, first_step, dx, shape, deps):
    arrays, whiches = split_pieces(pieces)
    count = len(pieces)
    capacity, width = shape[1:]
    rows, hidden = count * capacity, w_stack.shape[1]
    operands = [place, *arrays, act, slope, w_stack]
    specs = [smem()] + [anywhere()] * count + [inside()] * 2 + [anywhere()]
    aliases = {}
    if dx is not None:
        aliases = {len(operands): 0}
        operands.append(dx)
        specs.append(anywhere())
    return order.call(
        functools.partial(backward_kernel, whiches, columns, first_step),
        specs,
        operands,
        deps,
        None if dx is None else large_cost(),
        out_specs=[anywhere(), inside(), inside()],
        out_shape=[jax.ShapeDtypeStruct(shape, BF16)]
        + [jax.ShapeDtypeStruct((hidden, rows), BF16)] * 2,
        scratch_shapes=[
            pltpu.VMEM((rows, width), BF16),
            pltpu.VMEM((width, rows), BF16),
            pltpu.VMEM((rows, width), BF16),
            pltpu.VMEM((2, 3, hidden // 2, width), BF16),
            pltpu.SemaphoreType.DMA((count,)),
            pltpu.SemaphoreType.DMA((6,)),
            pltpu.SemaphoreType.DMA((count,)),
        ],
        input_output_aliases=aliases,
        name="backward",
    )


def side_by_side(refs, whiches, columns):
    return jnp.concatenate(
        [
            ref[:, columns] if which is None else ref[which, :, columns]
            for ref, which in zip(refs, whiches)
        ],
        axis=0,
    )


def grad_x_kernel(act_count, whiches, place_ref, *refs):
    acts, rows = refs[:act_count], refs[act_count:-4]
    send_ref, keep_ref, right, sems = refs[-4:]
    copies = start_rows(list(zip(rows, whiches)), right, sems)
    own, width = send_ref.shape[1:]
    low = place_ref[3]
    lefts = []
    for who in (1 - low, low):
        for lead in range(2):
            start = pl.multiple_of((2 * lead + who) * own, own)
            lefts.append(jnp.concatenate([ref[pl.ds(start, own), :] for ref in acts], axis=1))
    left = jnp.concatenate(lefts, axis=0)
    for copy in copies:
        copy.wait()
    tile = tile_of(width, 512)
    for n in range(0, width, tile):
        columns = slice(n, n + tile)
        total = jnp.dot(left, right[:, columns], preferred_element_type=F32).astype(BF16)
        for lead in range(2):
            send_ref[lead, :, columns] = total[lead * own : (lead + 1) * own]
            keep_ref[lead, :, columns] = total[(2 + lead) * own : (3 + lead) * own]


def grad_x(order, place, acts, rows, width, deps):
    own = acts[0].shape[0] // 4
    arrays, whiches = split_pieces(rows)
    return order.call(
        functools.partial(grad_x_kernel, len(acts), whiches),
        [smem()] + [inside()] * len(acts) + [anywhere()] * len(rows),
        [place, *acts, *arrays],
        deps,
        large_cost(),
        scratch_shapes=[
            pltpu.VMEM((sum(act.shape[1] for act in acts), width), BF16),
            pltpu.SemaphoreType.DMA((len(rows),)),
        ],
        out_specs=[inside()] * 2,
        out_shape=[jax.ShapeDtypeStruct((2, own, width), BF16)] * 2,
        name="grad_x",
    )


def grad_down_kernel(hid_count, whiches, place_ref, *refs):
    hids, rows, out_refs = refs[:hid_count], refs[hid_count:-4], refs[-4:]
    own, width = out_refs[0].shape
    high, low = place_ref[2], place_ref[3]
    lefts = []
    for lead in (1 - high, high):
        for who in (1 - low, low):
            start = pl.multiple_of(who * own, own)
            lefts.append(
                jnp.concatenate([ref[lead, pl.ds(start, own), :] for ref in hids], axis=1)
            )
    left = jnp.concatenate(lefts, axis=0)
    tile = tile_of(width, 512)
    for n in range(0, width, tile):
        columns = slice(n, n + tile)
        right = side_by_side(rows, whiches, columns)
        total = jnp.dot(left, right, preferred_element_type=F32).astype(BF16)
        for i in range(4):
            out_refs[i][:, columns] = total[i * own : (i + 1) * own]


def grad_down(order, place, hids, rows, width, deps):
    own = hids[0].shape[1] // 2
    arrays, whiches = split_pieces(rows)
    return order.call(
        functools.partial(grad_down_kernel, len(hids), whiches),
        [smem()] + [inside()] * (len(hids) + len(rows)),
        [place, *hids, *arrays],
        deps,
        out_specs=[inside()] * 4,
        out_shape=[jax.ShapeDtypeStruct((own, width), BF16)] * 4,
        name="grad_down",
    )


def sum_down_kernel(*refs):
    total = refs[0][...].astype(F32)
    for ref in refs[1:-1]:
        total = total + ref[...].astype(F32)
    refs[-1][...] = total.astype(BF16)


def sum_down(order, terms):
    return order.call(
        sum_down_kernel,
        [inside()] * len(terms),
        terms,
        cost=large_cost(),
        out_specs=inside(),
        out_shape=jax.ShapeDtypeStruct(terms[0].shape, BF16),
        name="sum_down",
    )


def sum_kernel(keep_ref, come_ref, down_ref, out_ref):
    width = keep_ref.shape[2]
    for lead in range(2):
        total = keep_ref[lead].astype(F32) + come_ref[lead].astype(F32)
        out_ref[:, lead * width : (lead + 1) * width] = total.astype(BF16)
    out_ref[:, 2 * width :] = down_ref[...]


def sum_all(order, keep, come, down):
    _, own, width = keep.shape
    return order.call(
        sum_kernel,
        [inside()] * 3,
        [keep, come, down],
        out_specs=inside(),
        out_shape=jax.ShapeDtypeStruct((own, 3 * width), BF16),
        name="sum_all",
    )


def body(x_tokens, d_out, expert_ids, combine, w_stack):
    tokens, width = x_tokens.shape
    experts = lax.axis_size("expert")
    replicas = lax.axis_size("replica")
    planes = len(RING)
    columns = experts // planes
    capacity = 2 * tokens * expert_ids.shape[1] // experts

    position = lax.axis_index("expert")
    replica = lax.axis_index("replica")
    plane, column = position // columns, position % columns
    high, low = replica // 2, replica % 2
    ring_place = plane ^ (plane >> 1)
    sources = [(ring_place - s) & (planes - 1) for s in range(planes)]
    firsts = [(source ^ (source >> 1)) * columns for source in sources]
    place = jnp.stack([plane * columns, column, high, low, *firsts]).astype(jnp.int32)

    def along_ring(value):
        pairs = [
            (RING[i] * columns + c, RING[(i + 1) % planes] * columns + c)
            for i in range(planes)
            for c in range(columns)
        ]
        return lax.ppermute(value, "expert", pairs)

    def across(value, d, r):
        pairs = [
            ((p * columns + c) * replicas + k, (p * columns + (c ^ d)) * replicas + (k ^ r))
            for p in range(planes)
            for c in range(columns)
            for k in range(replicas)
        ]
        return lax.ppermute(value, ("expert", "replica"), pairs)

    def exchange(values, r):
        return [across(value, d + 1, r) for d, value in enumerate(values)]

    order = Order()
    meta = jnp.concatenate([expert_ids.T.astype(F32), combine.T], axis=0)

    x_0, picked, scales, hits = select_first(order, place, meta, x_tokens, columns, capacity)
    x_1 = along_ring(x_0)
    x_pieces = [(picked[0], None)] + [(value, None) for value in exchange(picked[1:], 0)]
    x_other = [(across(picked[0], 0, 2), None)] + [(v, None) for v in exchange(picked[1:], 2)]
    dy_pieces = []
    all_hits = place_all(order, meta, experts, capacity)
    x_block, d_block = x_1, d_out
    hids, acts_kept, acts_come = [], [], []
    dx = None
    dx_shape = (experts, capacity, width)
    factors = None
    for s in range(1, planes):
        x_next = along_ring(x_block) if s < planes - 1 else None
        waits = {
            1: [value for value, _ in x_pieces[1:] + x_other],
            2: [value for value, _ in x_other[columns:]],
            3: [value for value, _ in x_other[2 * columns :]],
        }[s]
        d_next = along_ring(d_block) if s > 1 else None
        keep_x, keep_d, pairs, sends, again, scales, hits = select_both(
            order, place, x_block, scales, hits, d_block, columns, s == 1, waits
        )
        if s == 1:
            d_next = along_ring(again)
        come = exchange(pairs, 0)
        x_pieces += [(keep_x, None)] + [(value, 0) for value in come]
        dy_pieces += [(keep_d, None)] + [(value, 1) for value in come]
        x_other += [(across(keep_x, 0, 2), None)] + [(v, None) for v in exchange(sends, 2)]
        x_block, d_block = x_next, d_next
        if s == 1:
            hid, *factors = gate_up(order, x_pieces[: 2 * columns], w_stack, capacity)
            hids.append(hid)
        if s == 3:
            dx, send, keep = backward(
                order, place, dy_pieces[: 2 * columns], *factors, w_stack, columns, 0, None,
                dx_shape, [],
            )
            acts_kept.append(keep)
            acts_come.append(across(send, 0, 2))
    picked = select_last(order, scales, hits, d_block, columns, [])
    dy_pieces += [(picked[0], None)] + [(value, None) for value in exchange(picked[1:], 0)]
    hid, *factors = gate_up(order, x_pieces[2 * columns :], w_stack, capacity, large_cost())
    hids.append(hid)
    send_other, keep_other, send_own, down_own = grad_down(
        order, place, hids, dy_pieces, width, []
    )
    dx, send, keep = backward(
        order, place, dy_pieces[2 * columns :], *factors, w_stack, columns, 2, dx, dx_shape,
        [value for value, _ in x_other[3 * columns :]],
    )
    acts_kept.append(keep)
    acts_come.append(across(send, 0, 2))
    returned = lax.all_to_all(dx, "expert", split_axis=0, concat_axis=0, tiled=True)
    summed = keep_other.astype(F32) + across(send_other, 0, 1).astype(F32)
    summed = summed.astype(BF16)
    down_y = across(summed, 0, 2)
    down_core = across(send_own, 0, 1)

    send, keep = grad_x(
        order, place, acts_kept + acts_come, x_pieces + x_other, width, [summed, down_core]
    )
    down = sum_down(order, [down_own, down_core, down_y])
    g_rows = sum_all(order, keep, across(send, 0, 1), down)
    d_tokens = merge(order, all_hits, returned.reshape(experts * capacity, width))
    return d_tokens, g_rows[None]


def solution(mesh):
    return jax.shard_map(
        body,
        mesh=mesh,
        in_specs=(
            P(("expert", "replica"), None),
            P(("expert", "replica"), None),
            P(("expert", "replica"), None),
            P(("expert", "replica"), None),
            P("expert", None, None),
        ),
        out_specs=(P(("expert", "replica"), None), P("expert", "replica", None)),
        check_vma=False,
    )
```

```python
import functools

import jax
import jax.numpy as jnp
from jax import lax
from jax.experimental import pallas as pl
from jax.experimental.pallas import tpu as pltpu
from jax.sharding import PartitionSpec as P

BF16 = jnp.bfloat16
F32 = jnp.float32
RING = (0, 1, 3, 2)
VMEM_LIMIT = 44 * 1024 * 1024


def params():
    return pltpu.CompilerParams(vmem_limit_bytes=VMEM_LIMIT)


def smem():
    return pl.BlockSpec(memory_space=pltpu.SMEM)


def anywhere():
    return pl.BlockSpec(memory_space=pl.ANY)


def inside():
    return pl.BlockSpec(memory_space=pltpu.VMEM)


def small_cost():
    return pl.CostEstimate(flops=1024, bytes_accessed=1024, transcendentals=0)


def tile_of(width, most):
    return most if width % most == 0 else width


def large_cost():
    return pl.CostEstimate(flops=40 * 10**9, bytes_accessed=1 << 27, transcendentals=0)


class Order:
    def __init__(self):
        self.last = []

    def call(self, kernel, specs, operands, deps=(), cost=None, **options):
        extra = list(deps) + self.last
        count = len(operands)

        def body_of(*refs):
            kernel(*refs[:count], *refs[count + len(extra) :])

        outs = pl.pallas_call(
            body_of,
            in_specs=list(specs) + [anywhere()] * len(extra),
            compiler_params=params(),
            cost_estimate=cost or small_cost(),
            **options,
        )(*operands, *extra)
        self.last = [outs[-1] if isinstance(outs, (list, tuple)) else outs]
        return outs


def placing_of(base, own, meta, expert_count, capacity):
    tokens = meta.shape[1]
    id_first, id_second = meta[0:1, :], meta[1:2, :]
    scale_first, scale_second = meta[2:3, :], meta[3:4, :]
    row = lax.broadcasted_iota(jnp.int32, (max(16, expert_count), tokens), 0)
    expert = (base + jnp.bitwise_xor(row, own)).astype(F32)
    first = id_first == expert
    member = jnp.where(first | (id_second == expert), 1.0, 0.0)
    scale = jnp.where(first, scale_first, scale_second)
    earlier = lax.broadcasted_iota(jnp.int32, (tokens, tokens), 0)
    later = lax.broadcasted_iota(jnp.int32, (tokens, tokens), 1)
    before = jnp.where(earlier < later, 1.0, 0.0).astype(BF16)
    rank = jnp.dot(member.astype(BF16), before, preferred_element_type=F32)
    rank = jnp.where(member > 0.0, rank, -1.0)
    slot = lax.broadcasted_iota(jnp.int32, (capacity, tokens), 0).astype(F32)
    hits, scales = [], []
    for d in range(expert_count):
        hit = jnp.where(rank[d : d + 1, :] == slot, 1.0, 0.0)
        hits.append(hit)
        scales.append(jnp.sum(hit * scale[d : d + 1, :], axis=1, keepdims=True))
    return jnp.concatenate(hits, axis=0), jnp.concatenate(scales, axis=0)


def rounded(value):
    return value.astype(BF16).astype(F32)


def meta_columns(meta):
    scale = meta[2:4, :]
    top = rounded(scale)
    middle = rounded(scale - top)
    rest = scale - top - middle
    filler = jnp.zeros((120, meta.shape[1]), F32)
    return jnp.concatenate([meta[0:2, :], top, middle, rest, filler], axis=0).T.astype(BF16)


def meta_rows(columns):
    rows = columns.astype(F32).T
    scale = rows[2:4, :] + rows[4:6, :] + rows[6:8, :]
    return jnp.concatenate([rows[0:2, :], scale], axis=0)


def first_kernel(columns, capacity, place_ref, meta_ref, x_ref, *refs):
    x_out, keep_ref, send_refs = refs[0], refs[1], refs[2 : columns + 1]
    scales_ref, hits_ref = refs[columns + 1 :]
    width = x_ref.shape[1]
    meta = meta_ref[...]
    x = x_ref[...]
    x_out[:, :width] = x
    x_out[:, width:] = meta_columns(meta)
    hits, scales = placing_of(place_ref[0], place_ref[1], meta, columns, capacity)
    hits = hits.astype(BF16)
    hits_ref[...] = hits
    scales_ref[...] = jnp.broadcast_to(scales, scales_ref.shape)
    picked = jnp.dot(hits, x, preferred_element_type=F32).astype(BF16)
    keep_ref[...] = picked[:capacity, :]
    for d in range(1, columns):
        send_refs[d - 1][...] = picked[d * capacity : (d + 1) * capacity, :]


def select_first(order, place, meta, x, columns, capacity):
    tokens, width = x.shape
    count = columns * capacity
    outs = order.call(
        functools.partial(first_kernel, columns, capacity),
        [smem(), inside(), inside()],
        [place, meta, x],
        out_specs=[inside()] * (columns + 3),
        out_shape=[jax.ShapeDtypeStruct((tokens, width + 128), BF16)]
        + [jax.ShapeDtypeStruct((capacity, width), BF16)] * columns
        + [
            jax.ShapeDtypeStruct((count, 128), F32),
            jax.ShapeDtypeStruct((count, tokens), BF16),
        ],
        name="select_first",
    )
    return outs[0], outs[1:-2], outs[-2], outs[-1]


def both_kernel(columns, capacity, again, place_ref, x_ref, old_scales, old_hits, d_ref, *refs):
    keep_x, keep_d, refs = refs[0], refs[1], refs[2:]
    pair_refs, send_refs, refs = refs[: columns - 1], refs[columns - 1 : 2 * columns - 2], refs[2 * columns - 2 :]
    scales_ref, hits_ref = refs[-2:]
    width = d_ref.shape[1]
    rows = d_ref[...]
    if again:
        refs[0][...] = rows
    meta = meta_rows(x_ref[:, width:])
    hits, scales = placing_of(place_ref[0], place_ref[1], meta, columns, capacity)
    hits = hits.astype(BF16)
    hits_ref[...] = hits
    scales_ref[...] = jnp.broadcast_to(scales, scales_ref.shape)
    x = jnp.dot(hits, x_ref[:, :width], preferred_element_type=F32).astype(BF16)
    dy = jnp.dot(old_hits[...], rows, preferred_element_type=F32)
    dy = (dy * old_scales[:, 0:1]).astype(BF16)
    keep_x[...] = x[:capacity, :]
    keep_d[...] = dy[:capacity, :]
    for d in range(1, columns):
        part = slice(d * capacity, (d + 1) * capacity)
        pair_refs[d - 1][0] = x[part, :]
        pair_refs[d - 1][1] = dy[part, :]
        send_refs[d - 1][...] = x[part, :]


def select_both(order, place, x, scales, hits, d_rows, columns, again, deps):
    tokens, width = d_rows.shape
    count = hits.shape[0]
    capacity = count // columns
    shapes = [(capacity, width)] * 2
    shapes += [(2, capacity, width)] * (columns - 1) + [(capacity, width)] * (columns - 1)
    shapes += [(tokens, width)] * again
    outs = order.call(
        functools.partial(both_kernel, columns, capacity, again),
        [smem()] + [inside()] * 4,
        [place, x, scales, hits, d_rows],
        deps,
        out_specs=[inside()] * (len(shapes) + 2),
        out_shape=[jax.ShapeDtypeStruct(shape, BF16) for shape in shapes]
        + [
            jax.ShapeDtypeStruct((count, 128), F32),
            jax.ShapeDtypeStruct((count, tokens), BF16),
        ],
        name="select_both",
    )
    pairs, sends = outs[2 : columns + 1], outs[columns + 1 : 2 * columns]
    return outs[0], outs[1], pairs, sends, outs[-3], outs[-2], outs[-1]


def last_kernel(columns, scales_ref, hits_ref, d_ref, *out_refs):
    capacity = out_refs[0].shape[0]
    picked = jnp.dot(hits_ref[...], d_ref[...], preferred_element_type=F32)
    picked = (picked * scales_ref[:, 0:1]).astype(BF16)
    for d in range(columns):
        out_refs[d][...] = picked[d * capacity : (d + 1) * capacity, :]


def select_last(order, scales, hits, d_rows, columns, deps):
    width = d_rows.shape[1]
    capacity = hits.shape[0] // columns
    return order.call(
        functools.partial(last_kernel, columns),
        [inside()] * 3,
        [scales, hits, d_rows],
        deps,
        out_specs=[inside()] * columns,
        out_shape=[jax.ShapeDtypeStruct((capacity, width), BF16)] * columns,
        name="select_last",
    )


def place_all_kernel(experts, capacity, meta_ref, hits_ref):
    hits, _ = placing_of(0, 0, meta_ref[...], experts, capacity)
    hits_ref[...] = hits.astype(BF16)


def place_all(order, meta, experts, capacity):
    return order.call(
        functools.partial(place_all_kernel, experts, capacity),
        [inside()],
        [meta],
        out_specs=inside(),
        out_shape=jax.ShapeDtypeStruct((experts * capacity, meta.shape[1]), BF16),
        name="place_all",
    )


def merge_kernel(hits_ref, slots_ref, out_ref):
    out_ref[...] = lax.dot_general(
        hits_ref[...], slots_ref[...], (((0,), (0,)), ((), ())), preferred_element_type=F32
    ).astype(BF16)


def merge(order, hits, slots):
    return order.call(
        merge_kernel,
        [inside(), inside()],
        [hits, slots],
        out_shape=jax.ShapeDtypeStruct((hits.shape[1], slots.shape[1]), BF16),
        out_specs=inside(),
        name="merge",
    )


def start_rows(refs, target, sems):
    capacity = target.shape[0] // len(refs)
    copies = []
    for i, (ref, which) in enumerate(refs):
        source = ref if which is None else ref.at[which]
        rows = target.at[pl.ds(i * capacity, capacity)]
        copies.append(pltpu.make_async_copy(source, rows, sems.at[i]))
    for copy in copies:
        copy.start()
    return copies


def split_pieces(pieces):
    return [array for array, _ in pieces], [which for _, which in pieces]


def start_weights(w_ref, units, part, target, sem):
    width = target.shape[-1]
    copy = pltpu.make_async_copy(w_ref.at[0, units, pl.ds(part * width, width)], target, sem)
    copy.start()
    return copy


def gate_up_kernel(whiches, *refs):
    count = len(whiches)
    x_refs, w_ref, refs = refs[:count], refs[count], refs[count + 1 :]
    hid_ref, act_ref, slope_ref, x_all, x_turned, w_pair, sems, w_sems = refs
    half = hid_ref.shape[1]
    rows = start_rows(list(zip(x_refs, whiches)), x_all, sems)
    weights = []
    for t in range(2):
        for k in range(2):
            units = pl.ds(t * half, half)
            weights.append(start_weights(w_ref, units, k, w_pair.at[t, k], w_sems.at[2 * t + k]))
    for copy in rows:
        copy.wait()
    x_turned[...] = x_all[...].T
    for t in range(2):
        weights[2 * t].wait()
        gate = jnp.dot(w_pair[t, 0], x_turned[...], preferred_element_type=F32)
        weights[2 * t + 1].wait()
        up = jnp.dot(w_pair[t, 1], x_turned[...], preferred_element_type=F32)
        sig = jax.nn.sigmoid(gate)
        act = gate * sig
        hid_ref[t] = (act * up).astype(BF16)
        act_ref[t] = act
        slope_ref[t] = up * sig * (1.0 + gate * (1.0 - sig))


def gate_up(order, pieces, w_stack, capacity, cost=None):
    arrays, whiches = split_pieces(pieces)
    width = arrays[0].shape[-1]
    rows, hidden = len(pieces) * capacity, w_stack.shape[1]
    return order.call(
        functools.partial(gate_up_kernel, whiches),
        [anywhere()] * (len(pieces) + 1),
        [*arrays, w_stack],
        cost=cost,
        out_specs=[inside()] * 3,
        out_shape=[
            jax.ShapeDtypeStruct((2, hidden // 2, rows), BF16),
            jax.ShapeDtypeStruct((2, hidden // 2, rows), F32),
            jax.ShapeDtypeStruct((2, hidden // 2, rows), F32),
        ],
        scratch_shapes=[
            pltpu.VMEM((rows, width), BF16),
            pltpu.VMEM((width, rows), BF16),
            pltpu.VMEM((2, 2, hidden // 2, width), BF16),
            pltpu.SemaphoreType.DMA((len(pieces),)),
            pltpu.SemaphoreType.DMA((4,)),
        ],
        name="gate_up",
    )


def backward_kernel(whiches, columns, first_step, place_ref, *refs):
    count = len(whiches)
    dy_refs, (act_ref, slope_ref, w_ref), refs = refs[:count], refs[count : count + 3], refs[count + 3 :]
    dx_ref, send_ref, keep_ref, dy_all, dy_turned, total, w_all, sems, w_sems, out_sems = refs[-10:]
    half = act_ref.shape[1]
    capacity = dx_ref.shape[1]
    rows = start_rows(list(zip(dy_refs, whiches)), dy_all, sems)
    halves = [jnp.bitwise_xor(place_ref[2], 1 - t) for t in range(2)]
    weights = []
    for t, which in enumerate(halves):
        units = pl.ds(pl.multiple_of(which * half, half), half)
        for k in (2, 0, 1):
            weights.append(start_weights(w_ref, units, k, w_all.at[t, k], w_sems.at[3 * t + k]))
    for copy in rows:
        copy.wait()
    dy_turned[...] = dy_all[...].T
    sums = None
    for t, which in enumerate(halves):
        weights[3 * t].wait()
        d_hidden = jnp.dot(w_all[t, 2], dy_turned[...], preferred_element_type=F32)
        d_up = (d_hidden * act_ref[which]).astype(BF16)
        d_gate = (d_hidden * slope_ref[which]).astype(BF16)
        out_ref = (send_ref, keep_ref)[t]
        out_ref[:half, :] = d_gate
        out_ref[half:, :] = d_up
        for k, factor in enumerate((d_gate, d_up)):
            weights[3 * t + 1 + k].wait()
            part = jnp.dot(factor.T, w_all[t, k], preferred_element_type=F32)
            sums = part if sums is None else sums + part
    total[...] = sums.astype(BF16)
    copies = []
    for i in range(count):
        block = place_ref[4 + first_step + i // columns] + jnp.bitwise_xor(
            place_ref[1], i % columns
        )
        copies.append(
            pltpu.make_async_copy(
                total.at[pl.ds(i * capacity, capacity)], dx_ref.at[block], out_sems.at[i]
            )
        )
    for copy in copies:
        copy.start()
    for copy in copies:
        copy.wait()


def backward(order, place, pieces, act, slope, w_stack, columns, first_step, dx, shape, deps):
    arrays, whiches = split_pieces(pieces)
    count = len(pieces)
    capacity, width = shape[1:]
    rows, hidden = count * capacity, w_stack.shape[1]
    operands = [place, *arrays, act, slope, w_stack]
    specs = [smem()] + [anywhere()] * count + [inside()] * 2 + [anywhere()]
    aliases = {}
    if dx is not None:
        aliases = {len(operands): 0}
        operands.append(dx)
        specs.append(anywhere())
    return order.call(
        functools.partial(backward_kernel, whiches, columns, first_step),
        specs,
        operands,
        deps,
        None if dx is None else large_cost(),
        out_specs=[anywhere(), inside(), inside()],
        out_shape=[jax.ShapeDtypeStruct(shape, BF16)]
        + [jax.ShapeDtypeStruct((hidden, rows), BF16)] * 2,
        scratch_shapes=[
            pltpu.VMEM((rows, width), BF16),
            pltpu.VMEM((width, rows), BF16),
            pltpu.VMEM((rows, width), BF16),
            pltpu.VMEM((2, 3, hidden // 2, width), BF16),
            pltpu.SemaphoreType.DMA((count,)),
            pltpu.SemaphoreType.DMA((6,)),
            pltpu.SemaphoreType.DMA((count,)),
        ],
        input_output_aliases=aliases,
        name="backward",
    )


def side_by_side(refs, whiches, columns):
    return jnp.concatenate(
        [
            ref[:, columns] if which is None else ref[which, :, columns]
            for ref, which in zip(refs, whiches)
        ],
        axis=0,
    )


def grad_x_kernel(act_count, whiches, place_ref, *refs):
    acts, rows = refs[:act_count], refs[act_count:-4]
    send_ref, keep_ref, right, sems = refs[-4:]
    copies = start_rows(list(zip(rows, whiches)), right, sems)
    own, width = send_ref.shape[1:]
    low = place_ref[3]
    lefts = []
    for who in (1 - low, low):
        for lead in range(2):
            start = pl.multiple_of((2 * lead + who) * own, own)
            lefts.append(jnp.concatenate([ref[pl.ds(start, own), :] for ref in acts], axis=1))
    left = jnp.concatenate(lefts, axis=0)
    for copy in copies:
        copy.wait()
    tile = tile_of(width, 512)
    for n in range(0, width, tile):
        columns = slice(n, n + tile)
        total = jnp.dot(left, right[:, columns], preferred_element_type=F32).astype(BF16)
        for lead in range(2):
            send_ref[lead, :, columns] = total[lead * own : (lead + 1) * own]
            keep_ref[lead, :, columns] = total[(2 + lead) * own : (3 + lead) * own]


def grad_x(order, place, acts, rows, width, deps):
    own = acts[0].shape[0] // 4
    arrays, whiches = split_pieces(rows)
    return order.call(
        functools.partial(grad_x_kernel, len(acts), whiches),
        [smem()] + [inside()] * len(acts) + [anywhere()] * len(rows),
        [place, *acts, *arrays],
        deps,
        large_cost(),
        scratch_shapes=[
            pltpu.VMEM((sum(act.shape[1] for act in acts), width), BF16),
            pltpu.SemaphoreType.DMA((len(rows),)),
        ],
        out_specs=[inside()] * 2,
        out_shape=[jax.ShapeDtypeStruct((2, own, width), BF16)] * 2,
        name="grad_x",
    )


def grad_down_kernel(hid_count, whiches, place_ref, *refs):
    hids, rows, out_refs = refs[:hid_count], refs[hid_count:-4], refs[-4:]
    own, width = out_refs[0].shape
    high, low = place_ref[2], place_ref[3]
    lefts = []
    for lead in (1 - high, high):
        for who in (1 - low, low):
            start = pl.multiple_of(who * own, own)
            lefts.append(
                jnp.concatenate([ref[lead, pl.ds(start, own), :] for ref in hids], axis=1)
            )
    left = jnp.concatenate(lefts, axis=0)
    tile = tile_of(width, 512)
    for n in range(0, width, tile):
        columns = slice(n, n + tile)
        right = side_by_side(rows, whiches, columns)
        total = jnp.dot(left, right, preferred_element_type=F32).astype(BF16)
        for i in range(4):
            out_refs[i][:, columns] = total[i * own : (i + 1) * own]


def grad_down(order, place, hids, rows, width, deps):
    own = hids[0].shape[1] // 2
    arrays, whiches = split_pieces(rows)
    return order.call(
        functools.partial(grad_down_kernel, len(hids), whiches),
        [smem()] + [inside()] * (len(hids) + len(rows)),
        [place, *hids, *arrays],
        deps,
        out_specs=[inside()] * 4,
        out_shape=[jax.ShapeDtypeStruct((own, width), BF16)] * 4,
        name="grad_down",
    )


def arrive_kernel(*refs):
    refs[-1][...] = jnp.zeros_like(refs[-1])


def arrive(order, value):
    return order.call(
        arrive_kernel,
        [],
        [],
        [value],
        large_cost(),
        out_specs=inside(),
        out_shape=jax.ShapeDtypeStruct((8, 128), F32),
        name="arrive",
    )


def sum_kernel(keep_ref, come_ref, *refs):
    down_refs, (out_ref, downs, total, sems, out_sems) = refs[:-5], refs[-5:]
    width = keep_ref.shape[2]
    copies = [
        pltpu.make_async_copy(ref, downs.at[i], sems.at[i]) for i, ref in enumerate(down_refs)
    ]
    for copy in copies:
        copy.start()
    outs = []
    for part in range(3):
        columns = pl.ds(part * width, width)
        if part < 2:
            value = keep_ref[part].astype(F32) + come_ref[part].astype(F32)
        else:
            for copy in copies:
                copy.wait()
            value = downs[0].astype(F32)
            for i in range(1, len(down_refs)):
                value = value + downs[i].astype(F32)
        total[part] = value.astype(BF16)
        outs.append(
            pltpu.make_async_copy(total.at[part], out_ref.at[:, columns], out_sems.at[part])
        )
        outs[-1].start()
    for copy in outs:
        copy.wait()


def sum_all(order, keep, come, downs):
    _, own, width = keep.shape
    return order.call(
        sum_kernel,
        [inside()] * 2 + [anywhere()] * len(downs),
        [keep, come, *downs],
        out_specs=anywhere(),
        out_shape=jax.ShapeDtypeStruct((own, 3 * width), BF16),
        scratch_shapes=[
            pltpu.VMEM((len(downs), own, width), BF16),
            pltpu.VMEM((3, own, width), BF16),
            pltpu.SemaphoreType.DMA((len(downs),)),
            pltpu.SemaphoreType.DMA((3,)),
        ],
        name="sum_all",
    )


def body(x_tokens, d_out, expert_ids, combine, w_stack):
    tokens, width = x_tokens.shape
    experts = lax.axis_size("expert")
    replicas = lax.axis_size("replica")
    planes = len(RING)
    columns = experts // planes
    capacity = 2 * tokens * expert_ids.shape[1] // experts

    position = lax.axis_index("expert")
    replica = lax.axis_index("replica")
    plane, column = position // columns, position % columns
    high, low = replica // 2, replica % 2
    ring_place = plane ^ (plane >> 1)
    sources = [(ring_place - s) & (planes - 1) for s in range(planes)]
    firsts = [(source ^ (source >> 1)) * columns for source in sources]
    place = jnp.stack([plane * columns, column, high, low, *firsts]).astype(jnp.int32)

    def along_ring(value):
        pairs = [
            (RING[i] * columns + c, RING[(i + 1) % planes] * columns + c)
            for i in range(planes)
            for c in range(columns)
        ]
        return lax.ppermute(value, "expert", pairs)

    def across(value, d, r):
        pairs = [
            ((p * columns + c) * replicas + k, (p * columns + (c ^ d)) * replicas + (k ^ r))
            for p in range(planes)
            for c in range(columns)
            for k in range(replicas)
        ]
        return lax.ppermute(value, ("expert", "replica"), pairs)

    def exchange(values, r):
        return [across(value, d + 1, r) for d, value in enumerate(values)]

    order = Order()
    meta = jnp.concatenate([expert_ids.T.astype(F32), combine.T], axis=0)

    x_0, picked, scales, hits = select_first(order, place, meta, x_tokens, columns, capacity)
    x_1 = along_ring(x_0)
    x_pieces = [(picked[0], None)] + [(value, None) for value in exchange(picked[1:], 0)]
    x_other = [(across(picked[0], 0, 2), None)] + [(v, None) for v in exchange(picked[1:], 2)]
    dy_pieces = []
    all_hits = place_all(order, meta, experts, capacity)
    x_block, d_block = x_1, d_out
    hids, acts_kept, acts_come = [], [], []
    dx = None
    dx_shape = (experts, capacity, width)
    factors = None
    for s in range(1, planes):
        x_next = along_ring(x_block) if s < planes - 1 else None
        waits = {
            1: [value for value, _ in x_pieces[1:] + x_other],
            2: [value for value, _ in x_other[columns:]],
            3: [value for value, _ in x_other[2 * columns :]],
        }[s]
        d_next = along_ring(d_block) if s > 2 else None
        keep_x, keep_d, pairs, sends, again, scales, hits = select_both(
            order, place, x_block, scales, hits, d_block, columns, s < 3, waits
        )
        if s < 3:
            d_next = along_ring(again)
        come = exchange(pairs, 0)
        x_pieces += [(keep_x, None)] + [(value, 0) for value in come]
        dy_pieces += [(keep_d, None)] + [(value, 1) for value in come]
        x_other += [(across(keep_x, 0, 2), None)] + [(v, None) for v in exchange(sends, 2)]
        x_block, d_block = x_next, d_next
        if s == 1:
            hid, *factors = gate_up(order, x_pieces[: 2 * columns], w_stack, capacity)
            hids.append(hid)
        if s == 3:
            dx, send, keep = backward(
                order, place, dy_pieces[: 2 * columns], *factors, w_stack, columns, 0, None,
                dx_shape, [],
            )
            acts_kept.append(keep)
            acts_come.append(across(send, 0, 2))
    picked = select_last(order, scales, hits, d_block, columns, [])
    dy_pieces += [(picked[0], None)] + [(value, None) for value in exchange(picked[1:], 0)]
    hid, *factors = gate_up(order, x_pieces[2 * columns :], w_stack, capacity, large_cost())
    hids.append(hid)
    send_other, keep_other, send_own, down_own = grad_down(
        order, place, hids, dy_pieces, width, []
    )
    dx, send, keep = backward(
        order, place, dy_pieces[2 * columns :], *factors, w_stack, columns, 2, dx, dx_shape,
        [value for value, _ in x_other[3 * columns :]],
    )
    acts_kept.append(keep)
    acts_come.append(across(send, 0, 2))
    returned = lax.all_to_all(dx, "expert", split_axis=0, concat_axis=0, tiled=True)
    summed = keep_other.astype(F32) + across(send_other, 0, 1).astype(F32)
    summed = summed.astype(BF16)
    down_y = across(summed, 0, 2)
    down_core = across(send_own, 0, 1)

    send, keep = grad_x(
        order, place, acts_kept + acts_come, x_pieces + x_other, width, [summed, down_core]
    )
    arrive(order, down_y)
    g_rows = sum_all(order, keep, across(send, 0, 1), [down_own, down_core, down_y])
    d_tokens = merge(order, all_hits, returned.reshape(experts * capacity, width))
    return d_tokens, g_rows[None]


def solution(mesh):
    return jax.shard_map(
        body,
        mesh=mesh,
        in_specs=(
            P(("expert", "replica"), None),
            P(("expert", "replica"), None),
            P(("expert", "replica"), None),
            P(("expert", "replica"), None),
            P("expert", None, None),
        ),
        out_specs=(P(("expert", "replica"), None), P("expert", "replica", None)),
        check_vma=False,
    )
```

```python
import functools

import jax
import jax.numpy as jnp
from jax import lax
from jax.experimental import pallas as pl
from jax.experimental.pallas import tpu as pltpu
from jax.sharding import PartitionSpec as P

BF16 = jnp.bfloat16
F32 = jnp.float32
RING = (0, 1, 3, 2)
VMEM_LIMIT = 44 * 1024 * 1024


def params():
    return pltpu.CompilerParams(vmem_limit_bytes=VMEM_LIMIT)


def smem():
    return pl.BlockSpec(memory_space=pltpu.SMEM)


def anywhere():
    return pl.BlockSpec(memory_space=pl.ANY)


def inside():
    return pl.BlockSpec(memory_space=pltpu.VMEM)


def small_cost():
    return pl.CostEstimate(flops=1024, bytes_accessed=1024, transcendentals=0)


def tile_of(width, most):
    return most if width % most == 0 else width


def large_cost():
    return pl.CostEstimate(flops=40 * 10**9, bytes_accessed=1 << 27, transcendentals=0)


class Order:
    def __init__(self):
        self.last = []

    def call(self, kernel, specs, operands, deps=(), cost=None, **options):
        extra = list(deps) + self.last
        count = len(operands)

        def body_of(*refs):
            kernel(*refs[:count], *refs[count + len(extra) :])

        outs = pl.pallas_call(
            body_of,
            in_specs=list(specs) + [anywhere()] * len(extra),
            compiler_params=params(),
            cost_estimate=cost or small_cost(),
            **options,
        )(*operands, *extra)
        self.last = [outs[-1] if isinstance(outs, (list, tuple)) else outs]
        return outs


def placing_of(base, own, meta, expert_count, capacity):
    tokens = meta.shape[1]
    id_first, id_second = meta[0:1, :], meta[1:2, :]
    scale_first, scale_second = meta[2:3, :], meta[3:4, :]
    row = lax.broadcasted_iota(jnp.int32, (max(16, expert_count), tokens), 0)
    expert = (base + jnp.bitwise_xor(row, own)).astype(F32)
    first = id_first == expert
    member = jnp.where(first | (id_second == expert), 1.0, 0.0)
    scale = jnp.where(first, scale_first, scale_second)
    earlier = lax.broadcasted_iota(jnp.int32, (tokens, tokens), 0)
    later = lax.broadcasted_iota(jnp.int32, (tokens, tokens), 1)
    before = jnp.where(earlier < later, 1.0, 0.0).astype(BF16)
    rank = jnp.dot(member.astype(BF16), before, preferred_element_type=F32)
    rank = jnp.where(member > 0.0, rank, -1.0)
    slot = lax.broadcasted_iota(jnp.int32, (capacity, tokens), 0).astype(F32)
    hits, scales = [], []
    for d in range(expert_count):
        hit = jnp.where(rank[d : d + 1, :] == slot, 1.0, 0.0)
        hits.append(hit)
        scales.append(jnp.sum(hit * scale[d : d + 1, :], axis=1, keepdims=True))
    return jnp.concatenate(hits, axis=0), jnp.concatenate(scales, axis=0)


def rounded(value):
    return value.astype(BF16).astype(F32)


def meta_columns(meta):
    scale = meta[2:4, :]
    top = rounded(scale)
    middle = rounded(scale - top)
    rest = scale - top - middle
    filler = jnp.zeros((120, meta.shape[1]), F32)
    return jnp.concatenate([meta[0:2, :], top, middle, rest, filler], axis=0).T.astype(BF16)


def meta_rows(columns):
    rows = columns.astype(F32).T
    scale = rows[2:4, :] + rows[4:6, :] + rows[6:8, :]
    return jnp.concatenate([rows[0:2, :], scale], axis=0)


def first_kernel(columns, capacity, place_ref, meta_ref, x_ref, *refs):
    x_out, keep_ref, send_refs = refs[0], refs[1], refs[2 : columns + 1]
    scales_ref, hits_ref = refs[columns + 1 :]
    width = x_ref.shape[1]
    meta = meta_ref[...]
    x = x_ref[...]
    x_out[:, :width] = x
    x_out[:, width:] = meta_columns(meta)
    hits, scales = placing_of(place_ref[0], place_ref[1], meta, columns, capacity)
    hits = hits.astype(BF16)
    hits_ref[...] = hits
    scales_ref[...] = jnp.broadcast_to(scales, scales_ref.shape)
    picked = jnp.dot(hits, x, preferred_element_type=F32).astype(BF16)
    keep_ref[...] = picked[:capacity, :]
    for d in range(1, columns):
        send_refs[d - 1][...] = picked[d * capacity : (d + 1) * capacity, :]


def select_first(order, place, meta, x, columns, capacity):
    tokens, width = x.shape
    count = columns * capacity
    outs = order.call(
        functools.partial(first_kernel, columns, capacity),
        [smem(), inside(), inside()],
        [place, meta, x],
        out_specs=[inside()] * (columns + 3),
        out_shape=[jax.ShapeDtypeStruct((tokens, width + 128), BF16)]
        + [jax.ShapeDtypeStruct((capacity, width), BF16)] * columns
        + [
            jax.ShapeDtypeStruct((count, 128), F32),
            jax.ShapeDtypeStruct((count, tokens), BF16),
        ],
        name="select_first",
    )
    return outs[0], outs[1:-2], outs[-2], outs[-1]


def both_kernel(columns, capacity, again, place_ref, x_ref, old_scales, old_hits, d_ref, *refs):
    keep_x, keep_d, refs = refs[0], refs[1], refs[2:]
    pair_refs, send_refs, refs = refs[: columns - 1], refs[columns - 1 : 2 * columns - 2], refs[2 * columns - 2 :]
    scales_ref, hits_ref = refs[-2:]
    width = d_ref.shape[1]
    rows = d_ref[...]
    if again:
        refs[0][...] = rows
    meta = meta_rows(x_ref[:, width:])
    hits, scales = placing_of(place_ref[0], place_ref[1], meta, columns, capacity)
    hits = hits.astype(BF16)
    hits_ref[...] = hits
    scales_ref[...] = jnp.broadcast_to(scales, scales_ref.shape)
    x = jnp.dot(hits, x_ref[:, :width], preferred_element_type=F32).astype(BF16)
    dy = jnp.dot(old_hits[...], rows, preferred_element_type=F32)
    dy = (dy * old_scales[:, 0:1]).astype(BF16)
    keep_x[...] = x[:capacity, :]
    keep_d[...] = dy[:capacity, :]
    for d in range(1, columns):
        part = slice(d * capacity, (d + 1) * capacity)
        pair_refs[d - 1][0] = x[part, :]
        pair_refs[d - 1][1] = dy[part, :]
        send_refs[d - 1][...] = x[part, :]


def select_both(order, place, x, scales, hits, d_rows, columns, again, deps):
    tokens, width = d_rows.shape
    count = hits.shape[0]
    capacity = count // columns
    shapes = [(capacity, width)] * 2
    shapes += [(2, capacity, width)] * (columns - 1) + [(capacity, width)] * (columns - 1)
    shapes += [(tokens, width)] * again
    outs = order.call(
        functools.partial(both_kernel, columns, capacity, again),
        [smem()] + [inside()] * 4,
        [place, x, scales, hits, d_rows],
        deps,
        out_specs=[inside()] * (len(shapes) + 2),
        out_shape=[jax.ShapeDtypeStruct(shape, BF16) for shape in shapes]
        + [
            jax.ShapeDtypeStruct((count, 128), F32),
            jax.ShapeDtypeStruct((count, tokens), BF16),
        ],
        name="select_both",
    )
    pairs, sends = outs[2 : columns + 1], outs[columns + 1 : 2 * columns]
    return outs[0], outs[1], pairs, sends, outs[-3], outs[-2], outs[-1]


def last_kernel(columns, scales_ref, hits_ref, d_ref, *out_refs):
    capacity = out_refs[0].shape[0]
    picked = jnp.dot(hits_ref[...], d_ref[...], preferred_element_type=F32)
    picked = (picked * scales_ref[:, 0:1]).astype(BF16)
    for d in range(columns):
        out_refs[d][...] = picked[d * capacity : (d + 1) * capacity, :]


def select_last(order, scales, hits, d_rows, columns, deps):
    width = d_rows.shape[1]
    capacity = hits.shape[0] // columns
    return order.call(
        functools.partial(last_kernel, columns),
        [inside()] * 3,
        [scales, hits, d_rows],
        deps,
        out_specs=[inside()] * columns,
        out_shape=[jax.ShapeDtypeStruct((capacity, width), BF16)] * columns,
        name="select_last",
    )


def place_all_kernel(experts, capacity, meta_ref, hits_ref):
    hits, _ = placing_of(0, 0, meta_ref[...], experts, capacity)
    hits_ref[...] = hits.astype(BF16)


def place_all(order, meta, experts, capacity):
    return order.call(
        functools.partial(place_all_kernel, experts, capacity),
        [inside()],
        [meta],
        out_specs=inside(),
        out_shape=jax.ShapeDtypeStruct((experts * capacity, meta.shape[1]), BF16),
        name="place_all",
    )


def merge_kernel(hits_ref, slots_ref, out_ref):
    out_ref[...] = lax.dot_general(
        hits_ref[...], slots_ref[...], (((0,), (0,)), ((), ())), preferred_element_type=F32
    ).astype(BF16)


def merge(order, hits, slots):
    return order.call(
        merge_kernel,
        [inside(), inside()],
        [hits, slots],
        out_shape=jax.ShapeDtypeStruct((hits.shape[1], slots.shape[1]), BF16),
        out_specs=inside(),
        name="merge",
    )


def start_rows(refs, target, sems):
    capacity = target.shape[0] // len(refs)
    copies = []
    for i, (ref, which) in enumerate(refs):
        source = ref if which is None else ref.at[which]
        rows = target.at[pl.ds(i * capacity, capacity)]
        copies.append(pltpu.make_async_copy(source, rows, sems.at[i]))
    for copy in copies:
        copy.start()
    return copies


def split_pieces(pieces):
    return [array for array, _ in pieces], [which for _, which in pieces]


def start_weights(w_ref, units, part, target, sem):
    width = target.shape[-1]
    copy = pltpu.make_async_copy(w_ref.at[0, units, pl.ds(part * width, width)], target, sem)
    copy.start()
    return copy


def gate_up_kernel(whiches, *refs):
    count = len(whiches)
    x_refs, w_ref, refs = refs[:count], refs[count], refs[count + 1 :]
    hid_ref, act_ref, slope_ref, x_all, x_turned, w_pair, sems, w_sems = refs
    half = hid_ref.shape[1]
    rows = start_rows(list(zip(x_refs, whiches)), x_all, sems)
    weights = []
    for t in range(2):
        for k in range(2):
            units = pl.ds(t * half, half)
            weights.append(start_weights(w_ref, units, k, w_pair.at[t, k], w_sems.at[2 * t + k]))
    for copy in rows:
        copy.wait()
    x_turned[...] = x_all[...].T
    for t in range(2):
        weights[2 * t].wait()
        gate = jnp.dot(w_pair[t, 0], x_turned[...], preferred_element_type=F32)
        weights[2 * t + 1].wait()
        up = jnp.dot(w_pair[t, 1], x_turned[...], preferred_element_type=F32)
        sig = jax.nn.sigmoid(gate)
        act = gate * sig
        hid_ref[t] = (act * up).astype(BF16)
        act_ref[t] = act
        slope_ref[t] = up * sig * (1.0 + gate * (1.0 - sig))


def gate_up(order, pieces, w_stack, capacity, cost=None):
    arrays, whiches = split_pieces(pieces)
    width = arrays[0].shape[-1]
    rows, hidden = len(pieces) * capacity, w_stack.shape[1]
    return order.call(
        functools.partial(gate_up_kernel, whiches),
        [anywhere()] * (len(pieces) + 1),
        [*arrays, w_stack],
        cost=cost,
        out_specs=[inside()] * 3,
        out_shape=[
            jax.ShapeDtypeStruct((2, hidden // 2, rows), BF16),
            jax.ShapeDtypeStruct((2, hidden // 2, rows), F32),
            jax.ShapeDtypeStruct((2, hidden // 2, rows), F32),
        ],
        scratch_shapes=[
            pltpu.VMEM((rows, width), BF16),
            pltpu.VMEM((width, rows), BF16),
            pltpu.VMEM((2, 2, hidden // 2, width), BF16),
            pltpu.SemaphoreType.DMA((len(pieces),)),
            pltpu.SemaphoreType.DMA((4,)),
        ],
        name="gate_up",
    )


def backward_kernel(whiches, columns, first_step, place_ref, *refs):
    count = len(whiches)
    dy_refs, (act_ref, slope_ref, w_ref), refs = refs[:count], refs[count : count + 3], refs[count + 3 :]
    dx_ref, send_ref, keep_ref, dy_all, dy_turned, total, w_all, sems, w_sems, out_sems = refs[-10:]
    half = act_ref.shape[1]
    capacity = dx_ref.shape[1]
    rows = start_rows(list(zip(dy_refs, whiches)), dy_all, sems)
    halves = [jnp.bitwise_xor(place_ref[2], 1 - t) for t in range(2)]
    weights = []
    for t, which in enumerate(halves):
        units = pl.ds(pl.multiple_of(which * half, half), half)
        for k in (2, 0, 1):
            weights.append(start_weights(w_ref, units, k, w_all.at[t, k], w_sems.at[3 * t + k]))
    for copy in rows:
        copy.wait()
    dy_turned[...] = dy_all[...].T
    sums = None
    for t, which in enumerate(halves):
        weights[3 * t].wait()
        d_hidden = jnp.dot(w_all[t, 2], dy_turned[...], preferred_element_type=F32)
        d_up = (d_hidden * act_ref[which]).astype(BF16)
        d_gate = (d_hidden * slope_ref[which]).astype(BF16)
        out_ref = (send_ref, keep_ref)[t]
        out_ref[:half, :] = d_gate
        out_ref[half:, :] = d_up
        for k, factor in enumerate((d_gate, d_up)):
            weights[3 * t + 1 + k].wait()
            part = jnp.dot(factor.T, w_all[t, k], preferred_element_type=F32)
            sums = part if sums is None else sums + part
    total[...] = sums.astype(BF16)
    copies = []
    for i in range(count):
        block = place_ref[4 + first_step + i // columns] + jnp.bitwise_xor(
            place_ref[1], i % columns
        )
        copies.append(
            pltpu.make_async_copy(
                total.at[pl.ds(i * capacity, capacity)], dx_ref.at[block], out_sems.at[i]
            )
        )
    for copy in copies:
        copy.start()
    for copy in copies:
        copy.wait()


def backward(order, place, pieces, act, slope, w_stack, columns, first_step, dx, shape, deps):
    arrays, whiches = split_pieces(pieces)
    count = len(pieces)
    capacity, width = shape[1:]
    rows, hidden = count * capacity, w_stack.shape[1]
    operands = [place, *arrays, act, slope, w_stack]
    specs = [smem()] + [anywhere()] * count + [inside()] * 2 + [anywhere()]
    aliases = {}
    if dx is not None:
        aliases = {len(operands): 0}
        operands.append(dx)
        specs.append(pl.BlockSpec(memory_space=pltpu.HBM))
    return order.call(
        functools.partial(backward_kernel, whiches, columns, first_step),
        specs,
        operands,
        deps,
        None if dx is None else large_cost(),
        out_specs=[pl.BlockSpec(memory_space=pltpu.HBM), inside(), inside()],
        out_shape=[jax.ShapeDtypeStruct(shape, BF16)]
        + [jax.ShapeDtypeStruct((hidden, rows), BF16)] * 2,
        scratch_shapes=[
            pltpu.VMEM((rows, width), BF16),
            pltpu.VMEM((width, rows), BF16),
            pltpu.VMEM((rows, width), BF16),
            pltpu.VMEM((2, 3, hidden // 2, width), BF16),
            pltpu.SemaphoreType.DMA((count,)),
            pltpu.SemaphoreType.DMA((6,)),
            pltpu.SemaphoreType.DMA((count,)),
        ],
        input_output_aliases=aliases,
        name="backward",
    )


def side_by_side(refs, whiches, columns):
    return jnp.concatenate(
        [
            ref[:, columns] if which is None else ref[which, :, columns]
            for ref, which in zip(refs, whiches)
        ],
        axis=0,
    )


def grad_x_kernel(act_count, whiches, place_ref, *refs):
    acts, rows = refs[:act_count], refs[act_count:-4]
    send_ref, keep_ref, right, sems = refs[-4:]
    copies = start_rows(list(zip(rows, whiches)), right, sems)
    own, width = send_ref.shape[1:]
    low = place_ref[3]
    lefts = []
    for who in (1 - low, low):
        for lead in range(2):
            start = pl.multiple_of((2 * lead + who) * own, own)
            lefts.append(jnp.concatenate([ref[pl.ds(start, own), :] for ref in acts], axis=1))
    left = jnp.concatenate(lefts, axis=0)
    for copy in copies:
        copy.wait()
    tile = tile_of(width, 512)
    for n in range(0, width, tile):
        columns = slice(n, n + tile)
        total = jnp.dot(left, right[:, columns], preferred_element_type=F32).astype(BF16)
        for lead in range(2):
            send_ref[lead, :, columns] = total[lead * own : (lead + 1) * own]
            keep_ref[lead, :, columns] = total[(2 + lead) * own : (3 + lead) * own]


def grad_x(order, place, acts, rows, width, deps):
    own = acts[0].shape[0] // 4
    arrays, whiches = split_pieces(rows)
    return order.call(
        functools.partial(grad_x_kernel, len(acts), whiches),
        [smem()] + [inside()] * len(acts) + [anywhere()] * len(rows),
        [place, *acts, *arrays],
        deps,
        large_cost(),
        scratch_shapes=[
            pltpu.VMEM((sum(act.shape[1] for act in acts), width), BF16),
            pltpu.SemaphoreType.DMA((len(rows),)),
        ],
        out_specs=[inside()] * 2,
        out_shape=[jax.ShapeDtypeStruct((2, own, width), BF16)] * 2,
        name="grad_x",
    )


def grad_down_kernel(hid_count, whiches, place_ref, *refs):
    hids, rows, out_refs = refs[:hid_count], refs[hid_count:-4], refs[-4:]
    own, width = out_refs[0].shape
    high, low = place_ref[2], place_ref[3]
    lefts = []
    for lead in (1 - high, high):
        for who in (1 - low, low):
            start = pl.multiple_of(who * own, own)
            lefts.append(
                jnp.concatenate([ref[lead, pl.ds(start, own), :] for ref in hids], axis=1)
            )
    left = jnp.concatenate(lefts, axis=0)
    tile = tile_of(width, 512)
    for n in range(0, width, tile):
        columns = slice(n, n + tile)
        right = side_by_side(rows, whiches, columns)
        total = jnp.dot(left, right, preferred_element_type=F32).astype(BF16)
        for i in range(4):
            out_refs[i][:, columns] = total[i * own : (i + 1) * own]


def grad_down(order, place, hids, rows, width, deps):
    own = hids[0].shape[1] // 2
    arrays, whiches = split_pieces(rows)
    return order.call(
        functools.partial(grad_down_kernel, len(hids), whiches),
        [smem()] + [inside()] * (len(hids) + len(rows)),
        [place, *hids, *arrays],
        deps,
        out_specs=[inside()] * 4,
        out_shape=[jax.ShapeDtypeStruct((own, width), BF16)] * 4,
        name="grad_down",
    )


def arrive_kernel(*refs):
    refs[-1][...] = jnp.zeros_like(refs[-1])


def arrive(order, value):
    return order.call(
        arrive_kernel,
        [],
        [],
        [value],
        large_cost(),
        out_specs=inside(),
        out_shape=jax.ShapeDtypeStruct((8, 128), F32),
        name="arrive",
    )


def sum_kernel(keep_ref, come_ref, *refs):
    down_refs, (out_ref, stage, total, sems, out_sems) = refs[:-5], refs[-5:]
    width = keep_ref.shape[2]
    sources = [[ref.at[part] for ref in (keep_ref, come_ref)] for part in range(2)]
    sources.append(down_refs)
    copies, spots = [], []
    for terms in sources:
        spots.append([])
        for ref in terms:
            spot = len(copies)
            spots[-1].append(spot)
            copies.append(pltpu.make_async_copy(ref, stage.at[spot], sems.at[spot]))
            copies[-1].start()
    outs = []
    for part, places in enumerate(spots):
        value = None
        for spot in places:
            copies[spot].wait()
            term = stage[spot].astype(F32)
            value = term if value is None else value + term
        total[part] = value.astype(BF16)
        columns = pl.ds(part * width, width)
        outs.append(
            pltpu.make_async_copy(total.at[part], out_ref.at[:, columns], out_sems.at[part])
        )
        outs[-1].start()
    for copy in outs:
        copy.wait()


def sum_all(order, keep, come, downs):
    _, own, width = keep.shape
    count = 4 + len(downs)
    return order.call(
        sum_kernel,
        [anywhere()] * (2 + len(downs)),
        [keep, come, *downs],
        out_specs=pl.BlockSpec(memory_space=pltpu.HBM),
        out_shape=jax.ShapeDtypeStruct((own, 3 * width), BF16),
        scratch_shapes=[
            pltpu.VMEM((count, own, width), BF16),
            pltpu.VMEM((3, own, width), BF16),
            pltpu.SemaphoreType.DMA((count,)),
            pltpu.SemaphoreType.DMA((3,)),
        ],
        name="sum_all",
    )


def body(x_tokens, d_out, expert_ids, combine, w_stack):
    tokens, width = x_tokens.shape
    experts = lax.axis_size("expert")
    replicas = lax.axis_size("replica")
    planes = len(RING)
    columns = experts // planes
    capacity = 2 * tokens * expert_ids.shape[1] // experts

    position = lax.axis_index("expert")
    replica = lax.axis_index("replica")
    plane, column = position // columns, position % columns
    high, low = replica // 2, replica % 2
    ring_place = plane ^ (plane >> 1)
    sources = [(ring_place - s) & (planes - 1) for s in range(planes)]
    firsts = [(source ^ (source >> 1)) * columns for source in sources]
    place = jnp.stack([plane * columns, column, high, low, *firsts]).astype(jnp.int32)

    def along_ring(value):
        pairs = [
            (RING[i] * columns + c, RING[(i + 1) % planes] * columns + c)
            for i in range(planes)
            for c in range(columns)
        ]
        return lax.ppermute(value, "expert", pairs)

    def across(value, d, r):
        pairs = [
            ((p * columns + c) * replicas + k, (p * columns + (c ^ d)) * replicas + (k ^ r))
            for p in range(planes)
            for c in range(columns)
            for k in range(replicas)
        ]
        return lax.ppermute(value, ("expert", "replica"), pairs)

    def exchange(values, r):
        return [across(value, d + 1, r) for d, value in enumerate(values)]

    order = Order()
    meta = jnp.concatenate([expert_ids.T.astype(F32), combine.T], axis=0)

    x_0, picked, scales, hits = select_first(order, place, meta, x_tokens, columns, capacity)
    x_1 = along_ring(x_0)
    x_pieces = [(picked[0], None)] + [(value, None) for value in exchange(picked[1:], 0)]
    x_other = [(across(picked[0], 0, 2), None)] + [(v, None) for v in exchange(picked[1:], 2)]
    dy_pieces = []
    all_hits = place_all(order, meta, experts, capacity)
    x_block, d_block = x_1, d_out
    hids, acts_kept, acts_come = [], [], []
    dx = None
    dx_shape = (experts, capacity, width)
    factors = None
    for s in range(1, planes):
        x_next = along_ring(x_block) if s < planes - 1 else None
        waits = {
            1: [value for value, _ in x_pieces[1:] + x_other],
            2: [value for value, _ in x_other[columns:]],
            3: [value for value, _ in x_other[2 * columns :]],
        }[s]
        d_next = along_ring(d_block) if s > 2 else None
        keep_x, keep_d, pairs, sends, again, scales, hits = select_both(
            order, place, x_block, scales, hits, d_block, columns, s < 3, waits
        )
        if s < 3:
            d_next = along_ring(again)
        come = exchange(pairs, 0)
        x_pieces += [(keep_x, None)] + [(value, 0) for value in come]
        dy_pieces += [(keep_d, None)] + [(value, 1) for value in come]
        x_other += [(across(keep_x, 0, 2), None)] + [(v, None) for v in exchange(sends, 2)]
        x_block, d_block = x_next, d_next
        if s == 1:
            hid, *factors = gate_up(order, x_pieces[: 2 * columns], w_stack, capacity)
            hids.append(hid)
        if s == 3:
            dx, send, keep = backward(
                order, place, dy_pieces[: 2 * columns], *factors, w_stack, columns, 0, None,
                dx_shape, [],
            )
            acts_kept.append(keep)
            acts_come.append(across(send, 0, 2))
    picked = select_last(order, scales, hits, d_block, columns, [])
    dy_pieces += [(picked[0], None)] + [(value, None) for value in exchange(picked[1:], 0)]
    hid, *factors = gate_up(order, x_pieces[2 * columns :], w_stack, capacity, large_cost())
    hids.append(hid)
    send_other, keep_other, send_own, down_own = grad_down(
        order, place, hids, dy_pieces, width, []
    )
    dx, send, keep = backward(
        order, place, dy_pieces[2 * columns :], *factors, w_stack, columns, 2, dx, dx_shape,
        [value for value, _ in x_other[3 * columns :]],
    )
    acts_kept.append(keep)
    acts_come.append(across(send, 0, 2))
    returned = lax.all_to_all(dx, "expert", split_axis=0, concat_axis=0, tiled=True)
    summed = keep_other.astype(F32) + across(send_other, 0, 1).astype(F32)
    summed = summed.astype(BF16)
    down_y = across(summed, 0, 2)
    down_core = across(send_own, 0, 1)

    send, keep = grad_x(
        order, place, acts_kept + acts_come, x_pieces + x_other, width, [summed, down_core]
    )
    arrive(order, down_y)
    g_rows = sum_all(order, keep, across(send, 0, 1), [down_own, down_core, down_y])
    d_tokens = merge(order, all_hits, returned.reshape(experts * capacity, width))
    return d_tokens, g_rows[None]


def solution(mesh):
    return jax.shard_map(
        body,
        mesh=mesh,
        in_specs=(
            P(("expert", "replica"), None),
            P(("expert", "replica"), None),
            P(("expert", "replica"), None),
            P(("expert", "replica"), None),
            P("expert", None, None),
        ),
        out_specs=(P(("expert", "replica"), None), P("expert", "replica", None)),
        check_vma=False,
    )
```

```python
import functools

import jax
import jax.numpy as jnp
from jax import lax
from jax.experimental import pallas as pl
from jax.experimental.pallas import tpu as pltpu
from jax.sharding import PartitionSpec as P

BF16 = jnp.bfloat16
F32 = jnp.float32
RING = (0, 1, 3, 2)
VMEM_LIMIT = 44 * 1024 * 1024


def params():
    return pltpu.CompilerParams(vmem_limit_bytes=VMEM_LIMIT)


def smem():
    return pl.BlockSpec(memory_space=pltpu.SMEM)


def anywhere():
    return pl.BlockSpec(memory_space=pl.ANY)


def inside():
    return pl.BlockSpec(memory_space=pltpu.VMEM)


def small_cost():
    return pl.CostEstimate(flops=1024, bytes_accessed=1024, transcendentals=0)


def tile_of(width, most):
    return most if width % most == 0 else width


def large_cost():
    return pl.CostEstimate(flops=40 * 10**9, bytes_accessed=1 << 27, transcendentals=0)


class Order:
    def __init__(self):
        self.last = []

    def call(self, kernel, specs, operands, deps=(), cost=None, **options):
        extra = list(deps) + self.last
        count = len(operands)

        def body_of(*refs):
            kernel(*refs[:count], *refs[count + len(extra) :])

        outs = pl.pallas_call(
            body_of,
            in_specs=list(specs) + [anywhere()] * len(extra),
            compiler_params=params(),
            cost_estimate=cost or small_cost(),
            **options,
        )(*operands, *extra)
        self.last = [outs[-1] if isinstance(outs, (list, tuple)) else outs]
        return outs


def placing_of(base, own, meta, expert_count, capacity):
    tokens = meta.shape[1]
    id_first, id_second = meta[0:1, :], meta[1:2, :]
    scale_first, scale_second = meta[2:3, :], meta[3:4, :]
    row = lax.broadcasted_iota(jnp.int32, (max(16, expert_count), tokens), 0)
    expert = (base + jnp.bitwise_xor(row, own)).astype(F32)
    first = id_first == expert
    member = jnp.where(first | (id_second == expert), 1.0, 0.0)
    scale = jnp.where(first, scale_first, scale_second)
    earlier = lax.broadcasted_iota(jnp.int32, (tokens, tokens), 0)
    later = lax.broadcasted_iota(jnp.int32, (tokens, tokens), 1)
    before = jnp.where(earlier < later, 1.0, 0.0).astype(BF16)
    rank = jnp.dot(member.astype(BF16), before, preferred_element_type=F32)
    rank = jnp.where(member > 0.0, rank, -1.0)
    slot = lax.broadcasted_iota(jnp.int32, (capacity, tokens), 0).astype(F32)
    hits, scales = [], []
    for d in range(expert_count):
        hit = jnp.where(rank[d : d + 1, :] == slot, 1.0, 0.0)
        hits.append(hit)
        scales.append(jnp.sum(hit * scale[d : d + 1, :], axis=1, keepdims=True))
    return jnp.concatenate(hits, axis=0), jnp.concatenate(scales, axis=0)


def rounded(value):
    return value.astype(BF16).astype(F32)


def meta_columns(meta):
    scale = meta[2:4, :]
    top = rounded(scale)
    middle = rounded(scale - top)
    rest = scale - top - middle
    filler = jnp.zeros((120, meta.shape[1]), F32)
    return jnp.concatenate([meta[0:2, :], top, middle, rest, filler], axis=0).T.astype(BF16)


def meta_rows(columns):
    rows = columns.astype(F32).T
    scale = rows[2:4, :] + rows[4:6, :] + rows[6:8, :]
    return jnp.concatenate([rows[0:2, :], scale], axis=0)


def first_kernel(columns, capacity, place_ref, meta_ref, x_ref, *refs):
    x_out, keep_ref, send_refs = refs[0], refs[1], refs[2 : columns + 1]
    scales_ref, hits_ref = refs[columns + 1 :]
    width = x_ref.shape[1]
    meta = meta_ref[...]
    x = x_ref[...]
    x_out[:, :width] = x
    x_out[:, width:] = meta_columns(meta)
    hits, scales = placing_of(place_ref[0], place_ref[1], meta, columns, capacity)
    hits = hits.astype(BF16)
    hits_ref[...] = hits
    scales_ref[...] = jnp.broadcast_to(scales, scales_ref.shape)
    picked = jnp.dot(hits, x, preferred_element_type=F32).astype(BF16)
    keep_ref[...] = picked[:capacity, :]
    for d in range(1, columns):
        send_refs[d - 1][...] = picked[d * capacity : (d + 1) * capacity, :]


def select_first(order, place, meta, x, columns, capacity):
    tokens, width = x.shape
    count = columns * capacity
    outs = order.call(
        functools.partial(first_kernel, columns, capacity),
        [smem(), inside(), inside()],
        [place, meta, x],
        out_specs=[inside()] * (columns + 3),
        out_shape=[jax.ShapeDtypeStruct((tokens, width + 128), BF16)]
        + [jax.ShapeDtypeStruct((capacity, width), BF16)] * columns
        + [
            jax.ShapeDtypeStruct((count, 128), F32),
            jax.ShapeDtypeStruct((count, tokens), BF16),
        ],
        name="select_first",
    )
    return outs[0], outs[1:-2], outs[-2], outs[-1]


def both_kernel(columns, capacity, again, place_ref, x_ref, old_scales, old_hits, d_ref, *refs):
    keep_x, keep_d, refs = refs[0], refs[1], refs[2:]
    pair_refs, send_refs, refs = refs[: columns - 1], refs[columns - 1 : 2 * columns - 2], refs[2 * columns - 2 :]
    scales_ref, hits_ref = refs[-2:]
    width = d_ref.shape[1]
    rows = d_ref[...]
    if again:
        refs[0][...] = rows
    meta = meta_rows(x_ref[:, width:])
    hits, scales = placing_of(place_ref[0], place_ref[1], meta, columns, capacity)
    hits = hits.astype(BF16)
    hits_ref[...] = hits
    scales_ref[...] = jnp.broadcast_to(scales, scales_ref.shape)
    x = jnp.dot(hits, x_ref[:, :width], preferred_element_type=F32).astype(BF16)
    dy = jnp.dot(old_hits[...], rows, preferred_element_type=F32)
    dy = (dy * old_scales[:, 0:1]).astype(BF16)
    keep_x[...] = x[:capacity, :]
    keep_d[...] = dy[:capacity, :]
    for d in range(1, columns):
        part = slice(d * capacity, (d + 1) * capacity)
        pair_refs[d - 1][0] = x[part, :]
        pair_refs[d - 1][1] = dy[part, :]
        send_refs[d - 1][...] = x[part, :]


def select_both(order, place, x, scales, hits, d_rows, columns, again, deps):
    tokens, width = d_rows.shape
    count = hits.shape[0]
    capacity = count // columns
    shapes = [(capacity, width)] * 2
    shapes += [(2, capacity, width)] * (columns - 1) + [(capacity, width)] * (columns - 1)
    shapes += [(tokens, width)] * again
    outs = order.call(
        functools.partial(both_kernel, columns, capacity, again),
        [smem()] + [inside()] * 4,
        [place, x, scales, hits, d_rows],
        deps,
        out_specs=[inside()] * (len(shapes) + 2),
        out_shape=[jax.ShapeDtypeStruct(shape, BF16) for shape in shapes]
        + [
            jax.ShapeDtypeStruct((count, 128), F32),
            jax.ShapeDtypeStruct((count, tokens), BF16),
        ],
        name="select_both",
    )
    pairs, sends = outs[2 : columns + 1], outs[columns + 1 : 2 * columns]
    return outs[0], outs[1], pairs, sends, outs[-3], outs[-2], outs[-1]


def last_kernel(columns, scales_ref, hits_ref, d_ref, *out_refs):
    capacity = out_refs[0].shape[0]
    picked = jnp.dot(hits_ref[...], d_ref[...], preferred_element_type=F32)
    picked = (picked * scales_ref[:, 0:1]).astype(BF16)
    for d in range(columns):
        out_refs[d][...] = picked[d * capacity : (d + 1) * capacity, :]


def select_last(order, scales, hits, d_rows, columns, deps):
    width = d_rows.shape[1]
    capacity = hits.shape[0] // columns
    return order.call(
        functools.partial(last_kernel, columns),
        [inside()] * 3,
        [scales, hits, d_rows],
        deps,
        out_specs=[inside()] * columns,
        out_shape=[jax.ShapeDtypeStruct((capacity, width), BF16)] * columns,
        name="select_last",
    )


def place_all_kernel(experts, capacity, meta_ref, hits_ref):
    hits, _ = placing_of(0, 0, meta_ref[...], experts, capacity)
    hits_ref[...] = hits.astype(BF16)


def place_all(order, meta, experts, capacity):
    return order.call(
        functools.partial(place_all_kernel, experts, capacity),
        [inside()],
        [meta],
        out_specs=inside(),
        out_shape=jax.ShapeDtypeStruct((experts * capacity, meta.shape[1]), BF16),
        name="place_all",
    )


def merge_kernel(hits_ref, slots_ref, out_ref):
    out_ref[...] = lax.dot_general(
        hits_ref[...], slots_ref[...], (((0,), (0,)), ((), ())), preferred_element_type=F32
    ).astype(BF16)


def merge(order, hits, slots):
    return order.call(
        merge_kernel,
        [inside(), inside()],
        [hits, slots],
        out_shape=jax.ShapeDtypeStruct((hits.shape[1], slots.shape[1]), BF16),
        out_specs=inside(),
        name="merge",
    )


def start_rows(refs, target, sems):
    capacity = target.shape[0] // len(refs)
    copies = []
    for i, (ref, which) in enumerate(refs):
        source = ref if which is None else ref.at[which]
        rows = target.at[pl.ds(i * capacity, capacity)]
        copies.append(pltpu.make_async_copy(source, rows, sems.at[i]))
    for copy in copies:
        copy.start()
    return copies


def split_pieces(pieces):
    return [array for array, _ in pieces], [which for _, which in pieces]


def start_weights(w_ref, units, part, target, sem):
    width = target.shape[-1]
    copy = pltpu.make_async_copy(w_ref.at[0, units, pl.ds(part * width, width)], target, sem)
    copy.start()
    return copy


def gate_up_kernel(whiches, *refs):
    count = len(whiches)
    x_refs, w_ref, refs = refs[:count], refs[count], refs[count + 1 :]
    hid_ref, act_ref, slope_ref, x_all, x_turned, w_pair, sems, w_sems = refs
    half = hid_ref.shape[1]
    rows = start_rows(list(zip(x_refs, whiches)), x_all, sems)
    weights = []
    for t in range(2):
        for k in range(2):
            units = pl.ds(t * half, half)
            weights.append(start_weights(w_ref, units, k, w_pair.at[t, k], w_sems.at[2 * t + k]))
    for copy in rows:
        copy.wait()
    x_turned[...] = x_all[...].T
    for t in range(2):
        weights[2 * t].wait()
        gate = jnp.dot(w_pair[t, 0], x_turned[...], preferred_element_type=F32)
        weights[2 * t + 1].wait()
        up = jnp.dot(w_pair[t, 1], x_turned[...], preferred_element_type=F32)
        sig = jax.nn.sigmoid(gate)
        act = gate * sig
        hid_ref[t] = (act * up).astype(BF16)
        act_ref[t] = act
        slope_ref[t] = up * sig * (1.0 + gate * (1.0 - sig))


def gate_up(order, pieces, w_stack, capacity, cost=None):
    arrays, whiches = split_pieces(pieces)
    width = arrays[0].shape[-1]
    rows, hidden = len(pieces) * capacity, w_stack.shape[1]
    return order.call(
        functools.partial(gate_up_kernel, whiches),
        [anywhere()] * (len(pieces) + 1),
        [*arrays, w_stack],
        cost=cost,
        out_specs=[inside()] * 3,
        out_shape=[
            jax.ShapeDtypeStruct((2, hidden // 2, rows), BF16),
            jax.ShapeDtypeStruct((2, hidden // 2, rows), F32),
            jax.ShapeDtypeStruct((2, hidden // 2, rows), F32),
        ],
        scratch_shapes=[
            pltpu.VMEM((rows, width), BF16),
            pltpu.VMEM((width, rows), BF16),
            pltpu.VMEM((2, 2, hidden // 2, width), BF16),
            pltpu.SemaphoreType.DMA((len(pieces),)),
            pltpu.SemaphoreType.DMA((4,)),
        ],
        name="gate_up",
    )


def backward_kernel(whiches, columns, first_step, place_ref, *refs):
    count = len(whiches)
    dy_refs, (act_ref, slope_ref, w_ref), refs = refs[:count], refs[count : count + 3], refs[count + 3 :]
    dx_ref, send_ref, keep_ref, dy_all, dy_turned, total, w_all, sems, w_sems, out_sems = refs[-10:]
    half = act_ref.shape[1]
    capacity = dx_ref.shape[1]
    rows = start_rows(list(zip(dy_refs, whiches)), dy_all, sems)
    halves = [jnp.bitwise_xor(place_ref[2], 1 - t) for t in range(2)]
    weights = []
    for t, which in enumerate(halves):
        units = pl.ds(pl.multiple_of(which * half, half), half)
        for k in (2, 0, 1):
            weights.append(start_weights(w_ref, units, k, w_all.at[t, k], w_sems.at[3 * t + k]))
    for copy in rows:
        copy.wait()
    dy_turned[...] = dy_all[...].T
    sums = None
    for t, which in enumerate(halves):
        weights[3 * t].wait()
        d_hidden = jnp.dot(w_all[t, 2], dy_turned[...], preferred_element_type=F32)
        d_up = (d_hidden * act_ref[which]).astype(BF16)
        d_gate = (d_hidden * slope_ref[which]).astype(BF16)
        out_ref = (send_ref, keep_ref)[t]
        out_ref[:half, :] = d_gate
        out_ref[half:, :] = d_up
        for k, factor in enumerate((d_gate, d_up)):
            weights[3 * t + 1 + k].wait()
            part = jnp.dot(factor.T, w_all[t, k], preferred_element_type=F32)
            sums = part if sums is None else sums + part
    total[...] = sums.astype(BF16)
    copies = []
    for i in range(count):
        block = place_ref[4 + first_step + i // columns] + jnp.bitwise_xor(
            place_ref[1], i % columns
        )
        copies.append(
            pltpu.make_async_copy(
                total.at[pl.ds(i * capacity, capacity)], dx_ref.at[block], out_sems.at[i]
            )
        )
    for copy in copies:
        copy.start()
    for copy in copies:
        copy.wait()


def backward(order, place, pieces, act, slope, w_stack, columns, first_step, dx, shape, deps):
    arrays, whiches = split_pieces(pieces)
    count = len(pieces)
    capacity, width = shape[1:]
    rows, hidden = count * capacity, w_stack.shape[1]
    operands = [place, *arrays, act, slope, w_stack]
    specs = [smem()] + [anywhere()] * count + [inside()] * 2 + [anywhere()]
    aliases = {}
    if dx is not None:
        aliases = {len(operands): 0}
        operands.append(dx)
        specs.append(anywhere())
    return order.call(
        functools.partial(backward_kernel, whiches, columns, first_step),
        specs,
        operands,
        deps,
        None if dx is None else large_cost(),
        out_specs=[anywhere(), inside(), inside()],
        out_shape=[jax.ShapeDtypeStruct(shape, BF16)]
        + [jax.ShapeDtypeStruct((hidden, rows), BF16)] * 2,
        scratch_shapes=[
            pltpu.VMEM((rows, width), BF16),
            pltpu.VMEM((width, rows), BF16),
            pltpu.VMEM((rows, width), BF16),
            pltpu.VMEM((2, 3, hidden // 2, width), BF16),
            pltpu.SemaphoreType.DMA((count,)),
            pltpu.SemaphoreType.DMA((6,)),
            pltpu.SemaphoreType.DMA((count,)),
        ],
        input_output_aliases=aliases,
        name="backward",
    )


def side_by_side(refs, whiches, columns):
    return jnp.concatenate(
        [
            ref[:, columns] if which is None else ref[which, :, columns]
            for ref, which in zip(refs, whiches)
        ],
        axis=0,
    )


def grad_x_kernel(act_count, whiches, place_ref, *refs):
    acts, rows = refs[:act_count], refs[act_count:-4]
    send_ref, keep_ref, right, sems = refs[-4:]
    copies = start_rows(list(zip(rows, whiches)), right, sems)
    own, width = send_ref.shape[1:]
    low = place_ref[3]
    lefts = []
    for who in (1 - low, low):
        for lead in range(2):
            start = pl.multiple_of((2 * lead + who) * own, own)
            lefts.append(jnp.concatenate([ref[pl.ds(start, own), :] for ref in acts], axis=1))
    left = jnp.concatenate(lefts, axis=0)
    for copy in copies:
        copy.wait()
    tile = tile_of(width, 512)
    for n in range(0, width, tile):
        columns = slice(n, n + tile)
        total = jnp.dot(left, right[:, columns], preferred_element_type=F32).astype(BF16)
        for lead in range(2):
            send_ref[lead, :, columns] = total[lead * own : (lead + 1) * own]
            keep_ref[lead, :, columns] = total[(2 + lead) * own : (3 + lead) * own]


def grad_x(order, place, acts, rows, width, deps):
    own = acts[0].shape[0] // 4
    arrays, whiches = split_pieces(rows)
    return order.call(
        functools.partial(grad_x_kernel, len(acts), whiches),
        [smem()] + [inside()] * len(acts) + [anywhere()] * len(rows),
        [place, *acts, *arrays],
        deps,
        large_cost(),
        scratch_shapes=[
            pltpu.VMEM((sum(act.shape[1] for act in acts), width), BF16),
            pltpu.SemaphoreType.DMA((len(rows),)),
        ],
        out_specs=[inside()] * 2,
        out_shape=[jax.ShapeDtypeStruct((2, own, width), BF16)] * 2,
        name="grad_x",
    )


def grad_down_kernel(hid_count, whiches, place_ref, *refs):
    hids, rows, out_refs = refs[:hid_count], refs[hid_count:-4], refs[-4:]
    own, width = out_refs[0].shape
    high, low = place_ref[2], place_ref[3]
    lefts = []
    for lead in (1 - high, high):
        for who in (1 - low, low):
            start = pl.multiple_of(who * own, own)
            lefts.append(
                jnp.concatenate([ref[lead, pl.ds(start, own), :] for ref in hids], axis=1)
            )
    left = jnp.concatenate(lefts, axis=0)
    tile = tile_of(width, 512)
    for n in range(0, width, tile):
        columns = slice(n, n + tile)
        right = side_by_side(rows, whiches, columns)
        total = jnp.dot(left, right, preferred_element_type=F32).astype(BF16)
        for i in range(4):
            out_refs[i][:, columns] = total[i * own : (i + 1) * own]


def grad_down(order, place, hids, rows, width, deps):
    own = hids[0].shape[1] // 2
    arrays, whiches = split_pieces(rows)
    return order.call(
        functools.partial(grad_down_kernel, len(hids), whiches),
        [smem()] + [inside()] * (len(hids) + len(rows)),
        [place, *hids, *arrays],
        deps,
        out_specs=[inside()] * 4,
        out_shape=[jax.ShapeDtypeStruct((own, width), BF16)] * 4,
        name="grad_down",
    )


def arrive_kernel(*refs):
    refs[-1][...] = jnp.zeros_like(refs[-1])


def arrive(order, value):
    return order.call(
        arrive_kernel,
        [],
        [],
        [value],
        large_cost(),
        out_specs=inside(),
        out_shape=jax.ShapeDtypeStruct((8, 128), F32),
        name="arrive",
    )


def sum_kernel(keep_ref, come_ref, *refs):
    down_refs, (out_ref, downs, total, sems, out_sems) = refs[:-5], refs[-5:]
    width = keep_ref.shape[2]
    copies = [
        pltpu.make_async_copy(ref, downs.at[i], sems.at[i]) for i, ref in enumerate(down_refs)
    ]
    for copy in copies:
        copy.start()
    outs = []
    for part in range(3):
        columns = pl.ds(part * width, width)
        if part < 2:
            value = keep_ref[part].astype(F32) + come_ref[part].astype(F32)
        else:
            for copy in copies:
                copy.wait()
            value = downs[0].astype(F32)
            for i in range(1, len(down_refs)):
                value = value + downs[i].astype(F32)
        total[part] = value.astype(BF16)
        outs.append(
            pltpu.make_async_copy(total.at[part], out_ref.at[:, columns], out_sems.at[part])
        )
        outs[-1].start()
    for copy in outs:
        copy.wait()


def sum_all(order, keep, come, downs):
    _, own, width = keep.shape
    return order.call(
        sum_kernel,
        [inside()] * 2 + [anywhere()] * len(downs),
        [keep, come, *downs],
        out_specs=anywhere(),
        out_shape=jax.ShapeDtypeStruct((own, 3 * width), BF16),
        scratch_shapes=[
            pltpu.VMEM((len(downs), own, width), BF16),
            pltpu.VMEM((3, own, width), BF16),
            pltpu.SemaphoreType.DMA((len(downs),)),
            pltpu.SemaphoreType.DMA((3,)),
        ],
        name="sum_all",
    )


def body(x_tokens, d_out, expert_ids, combine, w_stack):
    tokens, width = x_tokens.shape
    experts = lax.axis_size("expert")
    replicas = lax.axis_size("replica")
    planes = len(RING)
    columns = experts // planes
    capacity = 2 * tokens * expert_ids.shape[1] // experts

    position = lax.axis_index("expert")
    replica = lax.axis_index("replica")
    plane, column = position // columns, position % columns
    high, low = replica // 2, replica % 2
    ring_place = plane ^ (plane >> 1)
    sources = [(ring_place - s) & (planes - 1) for s in range(planes)]
    firsts = [(source ^ (source >> 1)) * columns for source in sources]
    place = jnp.stack([plane * columns, column, high, low, *firsts]).astype(jnp.int32)

    def along_ring(value):
        pairs = [
            (RING[i] * columns + c, RING[(i + 1) % planes] * columns + c)
            for i in range(planes)
            for c in range(columns)
        ]
        return lax.ppermute(value, "expert", pairs)

    def across(value, d, r):
        pairs = [
            ((p * columns + c) * replicas + k, (p * columns + (c ^ d)) * replicas + (k ^ r))
            for p in range(planes)
            for c in range(columns)
            for k in range(replicas)
        ]
        return lax.ppermute(value, ("expert", "replica"), pairs)

    def exchange(values, r):
        return [across(value, d + 1, r) for d, value in enumerate(values)]

    order = Order()
    meta = jnp.concatenate([expert_ids.T.astype(F32), combine.T], axis=0)

    x_0, picked, scales, hits = select_first(order, place, meta, x_tokens, columns, capacity)
    x_1 = along_ring(x_0)
    x_pieces = [(picked[0], None)] + [(value, None) for value in exchange(picked[1:], 0)]
    x_other = [(across(picked[0], 0, 2), None)] + [(v, None) for v in exchange(picked[1:], 2)]
    dy_pieces = []
    all_hits = place_all(order, meta, experts, capacity)
    x_block, d_block = x_1, d_out
    hids, acts_kept, acts_come = [], [], []
    dx = None
    dx_shape = (experts, capacity, width)
    factors = None
    for s in range(1, planes):
        x_next = along_ring(x_block) if s < planes - 1 else None
        waits = {
            1: [value for value, _ in x_pieces[1:] + x_other],
            2: [value for value, _ in x_other[columns:]],
            3: [value for value, _ in x_other[2 * columns :]],
        }[s]
        d_next = along_ring(d_block) if s > 2 else None
        keep_x, keep_d, pairs, sends, again, scales, hits = select_both(
            order, place, x_block, scales, hits, d_block, columns, s < 3, waits
        )
        if s < 3:
            d_next = along_ring(again)
        come = exchange(pairs, 0)
        x_pieces += [(keep_x, None)] + [(value, 0) for value in come]
        dy_pieces += [(keep_d, None)] + [(value, 1) for value in come]
        x_other += [(across(keep_x, 0, 2), None)] + [(v, None) for v in exchange(sends, 2)]
        x_block, d_block = x_next, d_next
        if s == 1:
            hid, *factors = gate_up(order, x_pieces[: 2 * columns], w_stack, capacity)
            hids.append(hid)
        if s == 3:
            dx, send, keep = backward(
                order, place, dy_pieces[: 2 * columns], *factors, w_stack, columns, 0, None,
                dx_shape, [],
            )
            acts_kept.append(keep)
            acts_come.append(across(send, 0, 2))
    picked = select_last(order, scales, hits, d_block, columns, [])
    dy_pieces += [(picked[0], None)] + [(value, None) for value in exchange(picked[1:], 0)]
    hid, *factors = gate_up(order, x_pieces[2 * columns :], w_stack, capacity, large_cost())
    hids.append(hid)
    send_other, keep_other, send_own, down_own = grad_down(
        order, place, hids, dy_pieces, width, []
    )
    dx, send, keep = backward(
        order, place, dy_pieces[2 * columns :], *factors, w_stack, columns, 2, dx, dx_shape,
        [value for value, _ in x_other[3 * columns :]],
    )
    acts_kept.append(keep)
    acts_come.append(across(send, 0, 2))
    returned = lax.all_to_all(dx, "expert", split_axis=0, concat_axis=0, tiled=True)
    summed = keep_other.astype(F32) + across(send_other, 0, 1).astype(F32)
    summed = summed.astype(BF16)
    down_y = across(summed, 0, 2)
    down_core = across(send_own, 0, 1)

    send, keep = grad_x(
        order, place, acts_kept + acts_come, x_pieces + x_other, width, [summed, down_core]
    )
    d_tokens = merge(order, all_hits, returned.reshape(experts * capacity, width))
    arrive(order, down_y)
    g_rows = sum_all(order, keep, across(send, 0, 1), [down_own, down_core, down_y])
    return d_tokens, g_rows[None]


def solution(mesh):
    return jax.shard_map(
        body,
        mesh=mesh,
        in_specs=(
            P(("expert", "replica"), None),
            P(("expert", "replica"), None),
            P(("expert", "replica"), None),
            P(("expert", "replica"), None),
            P("expert", None, None),
        ),
        out_specs=(P(("expert", "replica"), None), P("expert", "replica", None)),
        check_vma=False,
    )
```

```python
import functools

import jax
import jax.numpy as jnp
from jax import lax
from jax.experimental import pallas as pl
from jax.experimental.pallas import tpu as pltpu
from jax.sharding import PartitionSpec as P

BF16 = jnp.bfloat16
F32 = jnp.float32
RING = (0, 1, 3, 2)
VMEM_LIMIT = 44 * 1024 * 1024


def params():
    return pltpu.CompilerParams(vmem_limit_bytes=VMEM_LIMIT)


def smem():
    return pl.BlockSpec(memory_space=pltpu.SMEM)


def anywhere():
    return pl.BlockSpec(memory_space=pl.ANY)


def inside():
    return pl.BlockSpec(memory_space=pltpu.VMEM)


def small_cost():
    return pl.CostEstimate(flops=1024, bytes_accessed=1024, transcendentals=0)


def tile_of(width, most):
    return most if width % most == 0 else width


def large_cost():
    return pl.CostEstimate(flops=40 * 10**9, bytes_accessed=1 << 27, transcendentals=0)


class Order:
    def __init__(self):
        self.last = []

    def call(self, kernel, specs, operands, deps=(), cost=None, **options):
        extra = list(deps) + self.last
        count = len(operands)

        def body_of(*refs):
            kernel(*refs[:count], *refs[count + len(extra) :])

        outs = pl.pallas_call(
            body_of,
            in_specs=list(specs) + [anywhere()] * len(extra),
            compiler_params=params(),
            cost_estimate=cost or small_cost(),
            **options,
        )(*operands, *extra)
        self.last = [outs[-1] if isinstance(outs, (list, tuple)) else outs]
        return outs


def placing_of(base, own, meta, expert_count, capacity):
    tokens = meta.shape[1]
    id_first, id_second = meta[0:1, :], meta[1:2, :]
    scale_first, scale_second = meta[2:3, :], meta[3:4, :]
    row = lax.broadcasted_iota(jnp.int32, (max(16, expert_count), tokens), 0)
    expert = (base + jnp.bitwise_xor(row, own)).astype(F32)
    first = id_first == expert
    member = jnp.where(first | (id_second == expert), 1.0, 0.0)
    scale = jnp.where(first, scale_first, scale_second)
    earlier = lax.broadcasted_iota(jnp.int32, (tokens, tokens), 0)
    later = lax.broadcasted_iota(jnp.int32, (tokens, tokens), 1)
    before = jnp.where(earlier < later, 1.0, 0.0).astype(BF16)
    rank = jnp.dot(member.astype(BF16), before, preferred_element_type=F32)
    rank = jnp.where(member > 0.0, rank, -1.0)
    slot = lax.broadcasted_iota(jnp.int32, (capacity, tokens), 0).astype(F32)
    hits, scales = [], []
    for d in range(expert_count):
        hit = jnp.where(rank[d : d + 1, :] == slot, 1.0, 0.0)
        hits.append(hit)
        scales.append(jnp.sum(hit * scale[d : d + 1, :], axis=1, keepdims=True))
    return jnp.concatenate(hits, axis=0), jnp.concatenate(scales, axis=0)


def rounded(value):
    return value.astype(BF16).astype(F32)


def meta_columns(meta):
    scale = meta[2:4, :]
    top = rounded(scale)
    middle = rounded(scale - top)
    rest = scale - top - middle
    filler = jnp.zeros((120, meta.shape[1]), F32)
    return jnp.concatenate([meta[0:2, :], top, middle, rest, filler], axis=0).T.astype(BF16)


def meta_rows(columns):
    rows = columns.astype(F32).T
    scale = rows[2:4, :] + rows[4:6, :] + rows[6:8, :]
    return jnp.concatenate([rows[0:2, :], scale], axis=0)


def first_kernel(columns, capacity, place_ref, meta_ref, x_ref, *refs):
    x_out, keep_ref, send_refs = refs[0], refs[1], refs[2 : columns + 1]
    scales_ref, hits_ref = refs[columns + 1 :]
    width = x_ref.shape[1]
    meta = meta_ref[...]
    x = x_ref[...]
    x_out[:, :width] = x
    x_out[:, width:] = meta_columns(meta)
    hits, scales = placing_of(place_ref[0], place_ref[1], meta, columns, capacity)
    hits = hits.astype(BF16)
    hits_ref[...] = hits
    scales_ref[...] = jnp.broadcast_to(scales, scales_ref.shape)
    picked = jnp.dot(hits, x, preferred_element_type=F32).astype(BF16)
    keep_ref[...] = picked[:capacity, :]
    for d in range(1, columns):
        send_refs[d - 1][...] = picked[d * capacity : (d + 1) * capacity, :]


def select_first(order, place, meta, x, columns, capacity):
    tokens, width = x.shape
    count = columns * capacity
    outs = order.call(
        functools.partial(first_kernel, columns, capacity),
        [smem(), inside(), inside()],
        [place, meta, x],
        out_specs=[inside()] * (columns + 3),
        out_shape=[jax.ShapeDtypeStruct((tokens, width + 128), BF16)]
        + [jax.ShapeDtypeStruct((capacity, width), BF16)] * columns
        + [
            jax.ShapeDtypeStruct((count, 128), F32),
            jax.ShapeDtypeStruct((count, tokens), BF16),
        ],
        name="select_first",
    )
    return outs[0], outs[1:-2], outs[-2], outs[-1]


def both_kernel(columns, capacity, again, place_ref, x_ref, old_scales, old_hits, d_ref, *refs):
    keep_x, keep_d, refs = refs[0], refs[1], refs[2:]
    pair_refs, send_refs, refs = refs[: columns - 1], refs[columns - 1 : 2 * columns - 2], refs[2 * columns - 2 :]
    scales_ref, hits_ref = refs[-2:]
    width = d_ref.shape[1]
    rows = d_ref[...]
    if again:
        refs[0][...] = rows
    meta = meta_rows(x_ref[:, width:])
    hits, scales = placing_of(place_ref[0], place_ref[1], meta, columns, capacity)
    hits = hits.astype(BF16)
    hits_ref[...] = hits
    scales_ref[...] = jnp.broadcast_to(scales, scales_ref.shape)
    x = jnp.dot(hits, x_ref[:, :width], preferred_element_type=F32).astype(BF16)
    dy = jnp.dot(old_hits[...], rows, preferred_element_type=F32)
    dy = (dy * old_scales[:, 0:1]).astype(BF16)
    keep_x[...] = x[:capacity, :]
    keep_d[...] = dy[:capacity, :]
    for d in range(1, columns):
        part = slice(d * capacity, (d + 1) * capacity)
        pair_refs[d - 1][0] = x[part, :]
        pair_refs[d - 1][1] = dy[part, :]
        send_refs[d - 1][...] = x[part, :]


def select_both(order, place, x, scales, hits, d_rows, columns, again, deps):
    tokens, width = d_rows.shape
    count = hits.shape[0]
    capacity = count // columns
    shapes = [(capacity, width)] * 2
    shapes += [(2, capacity, width)] * (columns - 1) + [(capacity, width)] * (columns - 1)
    shapes += [(tokens, width)] * again
    outs = order.call(
        functools.partial(both_kernel, columns, capacity, again),
        [smem()] + [inside()] * 4,
        [place, x, scales, hits, d_rows],
        deps,
        out_specs=[inside()] * (len(shapes) + 2),
        out_shape=[jax.ShapeDtypeStruct(shape, BF16) for shape in shapes]
        + [
            jax.ShapeDtypeStruct((count, 128), F32),
            jax.ShapeDtypeStruct((count, tokens), BF16),
        ],
        name="select_both",
    )
    pairs, sends = outs[2 : columns + 1], outs[columns + 1 : 2 * columns]
    return outs[0], outs[1], pairs, sends, outs[-3], outs[-2], outs[-1]


def last_kernel(columns, scales_ref, hits_ref, d_ref, *out_refs):
    capacity = out_refs[0].shape[0]
    picked = jnp.dot(hits_ref[...], d_ref[...], preferred_element_type=F32)
    picked = (picked * scales_ref[:, 0:1]).astype(BF16)
    for d in range(columns):
        out_refs[d][...] = picked[d * capacity : (d + 1) * capacity, :]


def select_last(order, scales, hits, d_rows, columns, deps):
    width = d_rows.shape[1]
    capacity = hits.shape[0] // columns
    return order.call(
        functools.partial(last_kernel, columns),
        [inside()] * 3,
        [scales, hits, d_rows],
        deps,
        out_specs=[inside()] * columns,
        out_shape=[jax.ShapeDtypeStruct((capacity, width), BF16)] * columns,
        name="select_last",
    )


def place_all_kernel(experts, capacity, meta_ref, hits_ref):
    hits, _ = placing_of(0, 0, meta_ref[...], experts, capacity)
    hits_ref[...] = hits.astype(BF16)


def place_all(order, meta, experts, capacity):
    return order.call(
        functools.partial(place_all_kernel, experts, capacity),
        [inside()],
        [meta],
        out_specs=inside(),
        out_shape=jax.ShapeDtypeStruct((experts * capacity, meta.shape[1]), BF16),
        name="place_all",
    )


def merge_kernel(hits_ref, slots_ref, out_ref):
    out_ref[...] = lax.dot_general(
        hits_ref[...], slots_ref[...], (((0,), (0,)), ((), ())), preferred_element_type=F32
    ).astype(BF16)


def merge(order, hits, slots):
    return order.call(
        merge_kernel,
        [inside(), inside()],
        [hits, slots],
        out_shape=jax.ShapeDtypeStruct((hits.shape[1], slots.shape[1]), BF16),
        out_specs=inside(),
        name="merge",
    )


def start_rows(refs, target, sems):
    capacity = target.shape[0] // len(refs)
    copies = []
    for i, (ref, which) in enumerate(refs):
        source = ref if which is None else ref.at[which]
        rows = target.at[pl.ds(i * capacity, capacity)]
        copies.append(pltpu.make_async_copy(source, rows, sems.at[i]))
    for copy in copies:
        copy.start()
    return copies


def split_pieces(pieces):
    return [array for array, _ in pieces], [which for _, which in pieces]


def start_weights(w_ref, units, part, target, sem):
    width = target.shape[-1]
    copy = pltpu.make_async_copy(w_ref.at[0, units, pl.ds(part * width, width)], target, sem)
    copy.start()
    return copy


def gate_up_kernel(whiches, *refs):
    count = len(whiches)
    x_refs, w_ref, refs = refs[:count], refs[count], refs[count + 1 :]
    hid_ref, act_ref, slope_ref, x_all, x_turned, w_pair, sems, w_sems = refs
    half = hid_ref.shape[1]
    rows = start_rows(list(zip(x_refs, whiches)), x_all, sems)
    weights = []
    for t in range(2):
        for k in range(2):
            units = pl.ds(t * half, half)
            weights.append(start_weights(w_ref, units, k, w_pair.at[t, k], w_sems.at[2 * t + k]))
    for copy in rows:
        copy.wait()
    x_turned[...] = x_all[...].T
    for t in range(2):
        weights[2 * t].wait()
        gate = jnp.dot(w_pair[t, 0], x_turned[...], preferred_element_type=F32)
        weights[2 * t + 1].wait()
        up = jnp.dot(w_pair[t, 1], x_turned[...], preferred_element_type=F32)
        sig = jax.nn.sigmoid(gate)
        act = gate * sig
        hid_ref[t] = (act * up).astype(BF16)
        act_ref[t] = act
        slope_ref[t] = up * sig * (1.0 + gate * (1.0 - sig))


def gate_up(order, pieces, w_stack, capacity, cost=None):
    arrays, whiches = split_pieces(pieces)
    width = arrays[0].shape[-1]
    rows, hidden = len(pieces) * capacity, w_stack.shape[1]
    return order.call(
        functools.partial(gate_up_kernel, whiches),
        [anywhere()] * (len(pieces) + 1),
        [*arrays, w_stack],
        cost=cost,
        out_specs=[inside()] * 3,
        out_shape=[
            jax.ShapeDtypeStruct((2, hidden // 2, rows), BF16),
            jax.ShapeDtypeStruct((2, hidden // 2, rows), F32),
            jax.ShapeDtypeStruct((2, hidden // 2, rows), F32),
        ],
        scratch_shapes=[
            pltpu.VMEM((rows, width), BF16),
            pltpu.VMEM((width, rows), BF16),
            pltpu.VMEM((2, 2, hidden // 2, width), BF16),
            pltpu.SemaphoreType.DMA((len(pieces),)),
            pltpu.SemaphoreType.DMA((4,)),
        ],
        name="gate_up",
    )


def backward_kernel(whiches, columns, first_step, place_ref, *refs):
    count = len(whiches)
    dy_refs, (act_ref, slope_ref, w_ref), refs = refs[:count], refs[count : count + 3], refs[count + 3 :]
    dx_ref, send_ref, keep_ref, dy_all, dy_turned, total, w_all, sems, w_sems, out_sems = refs[-10:]
    half = act_ref.shape[1]
    capacity = dx_ref.shape[1]
    rows = start_rows(list(zip(dy_refs, whiches)), dy_all, sems)
    halves = [jnp.bitwise_xor(place_ref[2], 1 - t) for t in range(2)]
    weights = []
    for t, which in enumerate(halves):
        units = pl.ds(pl.multiple_of(which * half, half), half)
        for k in (2, 0, 1):
            weights.append(start_weights(w_ref, units, k, w_all.at[t, k], w_sems.at[3 * t + k]))
    for copy in rows:
        copy.wait()
    dy_turned[...] = dy_all[...].T
    sums = None
    for t, which in enumerate(halves):
        weights[3 * t].wait()
        d_hidden = jnp.dot(w_all[t, 2], dy_turned[...], preferred_element_type=F32)
        d_up = (d_hidden * act_ref[which]).astype(BF16)
        d_gate = (d_hidden * slope_ref[which]).astype(BF16)
        out_ref = (send_ref, keep_ref)[t]
        out_ref[:half, :] = d_gate
        out_ref[half:, :] = d_up
        for k, factor in enumerate((d_gate, d_up)):
            weights[3 * t + 1 + k].wait()
            part = jnp.dot(factor.T, w_all[t, k], preferred_element_type=F32)
            sums = part if sums is None else sums + part
    total[...] = sums.astype(BF16)
    copies = []
    for i in range(count):
        block = place_ref[4 + first_step + i // columns] + jnp.bitwise_xor(
            place_ref[1], i % columns
        )
        copies.append(
            pltpu.make_async_copy(
                total.at[pl.ds(i * capacity, capacity)], dx_ref.at[block], out_sems.at[i]
            )
        )
    for copy in copies:
        copy.start()
    for copy in copies:
        copy.wait()


def backward(order, place, pieces, act, slope, w_stack, columns, first_step, dx, shape, deps):
    arrays, whiches = split_pieces(pieces)
    count = len(pieces)
    capacity, width = shape[1:]
    rows, hidden = count * capacity, w_stack.shape[1]
    operands = [place, *arrays, act, slope, w_stack]
    specs = [smem()] + [anywhere()] * count + [inside()] * 2 + [anywhere()]
    aliases = {}
    if dx is not None:
        aliases = {len(operands): 0}
        operands.append(dx)
        specs.append(anywhere())
    return order.call(
        functools.partial(backward_kernel, whiches, columns, first_step),
        specs,
        operands,
        deps,
        None if dx is None else large_cost(),
        out_specs=[anywhere(), inside(), inside()],
        out_shape=[jax.ShapeDtypeStruct(shape, BF16)]
        + [jax.ShapeDtypeStruct((hidden, rows), BF16)] * 2,
        scratch_shapes=[
            pltpu.VMEM((rows, width), BF16),
            pltpu.VMEM((width, rows), BF16),
            pltpu.VMEM((rows, width), BF16),
            pltpu.VMEM((2, 3, hidden // 2, width), BF16),
            pltpu.SemaphoreType.DMA((count,)),
            pltpu.SemaphoreType.DMA((6,)),
            pltpu.SemaphoreType.DMA((count,)),
        ],
        input_output_aliases=aliases,
        name="backward",
    )


def side_by_side(refs, whiches, columns):
    return jnp.concatenate(
        [
            ref[:, columns] if which is None else ref[which, :, columns]
            for ref, which in zip(refs, whiches)
        ],
        axis=0,
    )


def grad_x_kernel(act_count, whiches, place_ref, *refs):
    acts, rows = refs[:act_count], refs[act_count:-4]
    send_ref, keep_ref, right, sems = refs[-4:]
    copies = start_rows(list(zip(rows, whiches)), right, sems)
    own, width = send_ref.shape[1:]
    low = place_ref[3]
    lefts = []
    for who in (1 - low, low):
        for lead in range(2):
            start = pl.multiple_of((2 * lead + who) * own, own)
            lefts.append(jnp.concatenate([ref[pl.ds(start, own), :] for ref in acts], axis=1))
    left = jnp.concatenate(lefts, axis=0)
    for copy in copies:
        copy.wait()
    tile = tile_of(width, 1024)
    for n in range(0, width, tile):
        columns = slice(n, n + tile)
        total = jnp.dot(left, right[:, columns], preferred_element_type=F32).astype(BF16)
        for lead in range(2):
            send_ref[lead, :, columns] = total[lead * own : (lead + 1) * own]
            keep_ref[lead, :, columns] = total[(2 + lead) * own : (3 + lead) * own]


def grad_x(order, place, acts, rows, width, deps):
    own = acts[0].shape[0] // 4
    arrays, whiches = split_pieces(rows)
    return order.call(
        functools.partial(grad_x_kernel, len(acts), whiches),
        [smem()] + [inside()] * len(acts) + [anywhere()] * len(rows),
        [place, *acts, *arrays],
        deps,
        large_cost(),
        scratch_shapes=[
            pltpu.VMEM((sum(act.shape[1] for act in acts), width), BF16),
            pltpu.SemaphoreType.DMA((len(rows),)),
        ],
        out_specs=[inside()] * 2,
        out_shape=[jax.ShapeDtypeStruct((2, own, width), BF16)] * 2,
        name="grad_x",
    )


def grad_down_kernel(hid_count, whiches, place_ref, *refs):
    hids, rows, out_refs = refs[:hid_count], refs[hid_count:-4], refs[-4:]
    own, width = out_refs[0].shape
    high, low = place_ref[2], place_ref[3]
    lefts = []
    for lead in (1 - high, high):
        for who in (1 - low, low):
            start = pl.multiple_of(who * own, own)
            lefts.append(
                jnp.concatenate([ref[lead, pl.ds(start, own), :] for ref in hids], axis=1)
            )
    left = jnp.concatenate(lefts, axis=0)
    tile = tile_of(width, 1024)
    for n in range(0, width, tile):
        columns = slice(n, n + tile)
        right = side_by_side(rows, whiches, columns)
        total = jnp.dot(left, right, preferred_element_type=F32).astype(BF16)
        for i in range(4):
            out_refs[i][:, columns] = total[i * own : (i + 1) * own]


def grad_down(order, place, hids, rows, width, deps):
    own = hids[0].shape[1] // 2
    arrays, whiches = split_pieces(rows)
    return order.call(
        functools.partial(grad_down_kernel, len(hids), whiches),
        [smem()] + [inside()] * (len(hids) + len(rows)),
        [place, *hids, *arrays],
        deps,
        out_specs=[inside()] * 4,
        out_shape=[jax.ShapeDtypeStruct((own, width), BF16)] * 4,
        name="grad_down",
    )


def arrive_kernel(*refs):
    refs[-1][...] = jnp.zeros_like(refs[-1])


def arrive(order, value):
    return order.call(
        arrive_kernel,
        [],
        [],
        [value],
        large_cost(),
        out_specs=inside(),
        out_shape=jax.ShapeDtypeStruct((8, 128), F32),
        name="arrive",
    )


def sum_kernel(keep_ref, come_ref, *refs):
    down_refs, (out_ref, downs, total, sems, out_sems) = refs[:-5], refs[-5:]
    width = keep_ref.shape[2]
    copies = [
        pltpu.make_async_copy(ref, downs.at[i], sems.at[i]) for i, ref in enumerate(down_refs)
    ]
    for copy in copies:
        copy.start()
    outs = []
    for part in range(3):
        columns = pl.ds(part * width, width)
        if part < 2:
            value = keep_ref[part].astype(F32) + come_ref[part].astype(F32)
        else:
            for copy in copies:
                copy.wait()
            value = downs[0].astype(F32)
            for i in range(1, len(down_refs)):
                value = value + downs[i].astype(F32)
        total[part] = value.astype(BF16)
        outs.append(
            pltpu.make_async_copy(total.at[part], out_ref.at[:, columns], out_sems.at[part])
        )
        outs[-1].start()
    for copy in outs:
        copy.wait()


def sum_all(order, keep, come, downs):
    _, own, width = keep.shape
    return order.call(
        sum_kernel,
        [inside()] * 2 + [anywhere()] * len(downs),
        [keep, come, *downs],
        out_specs=anywhere(),
        out_shape=jax.ShapeDtypeStruct((own, 3 * width), BF16),
        scratch_shapes=[
            pltpu.VMEM((len(downs), own, width), BF16),
            pltpu.VMEM((3, own, width), BF16),
            pltpu.SemaphoreType.DMA((len(downs),)),
            pltpu.SemaphoreType.DMA((3,)),
        ],
        name="sum_all",
    )


def body(x_tokens, d_out, expert_ids, combine, w_stack):
    tokens, width = x_tokens.shape
    experts = lax.axis_size("expert")
    replicas = lax.axis_size("replica")
    planes = len(RING)
    columns = experts // planes
    capacity = 2 * tokens * expert_ids.shape[1] // experts

    position = lax.axis_index("expert")
    replica = lax.axis_index("replica")
    plane, column = position // columns, position % columns
    high, low = replica // 2, replica % 2
    ring_place = plane ^ (plane >> 1)
    sources = [(ring_place - s) & (planes - 1) for s in range(planes)]
    firsts = [(source ^ (source >> 1)) * columns for source in sources]
    place = jnp.stack([plane * columns, column, high, low, *firsts]).astype(jnp.int32)

    def along_ring(value):
        pairs = [
            (RING[i] * columns + c, RING[(i + 1) % planes] * columns + c)
            for i in range(planes)
            for c in range(columns)
        ]
        return lax.ppermute(value, "expert", pairs)

    def across(value, d, r):
        pairs = [
            ((p * columns + c) * replicas + k, (p * columns + (c ^ d)) * replicas + (k ^ r))
            for p in range(planes)
            for c in range(columns)
            for k in range(replicas)
        ]
        return lax.ppermute(value, ("expert", "replica"), pairs)

    def exchange(values, r):
        return [across(value, d + 1, r) for d, value in enumerate(values)]

    order = Order()
    meta = jnp.concatenate([expert_ids.T.astype(F32), combine.T], axis=0)

    x_0, picked, scales, hits = select_first(order, place, meta, x_tokens, columns, capacity)
    x_1 = along_ring(x_0)
    x_pieces = [(picked[0], None)] + [(value, None) for value in exchange(picked[1:], 0)]
    x_other = [(across(picked[0], 0, 2), None)] + [(v, None) for v in exchange(picked[1:], 2)]
    dy_pieces = []
    all_hits = place_all(order, meta, experts, capacity)
    x_block, d_block = x_1, d_out
    hids, acts_kept, acts_come = [], [], []
    dx = None
    dx_shape = (experts, capacity, width)
    factors = None
    for s in range(1, planes):
        x_next = along_ring(x_block) if s < planes - 1 else None
        waits = {
            1: [value for value, _ in x_pieces[1:] + x_other],
            2: [value for value, _ in x_other[columns:]],
            3: [value for value, _ in x_other[2 * columns :]],
        }[s]
        d_next = along_ring(d_block) if s > 2 else None
        keep_x, keep_d, pairs, sends, again, scales, hits = select_both(
            order, place, x_block, scales, hits, d_block, columns, s < 3, waits
        )
        if s < 3:
            d_next = along_ring(again)
        come = exchange(pairs, 0)
        x_pieces += [(keep_x, None)] + [(value, 0) for value in come]
        dy_pieces += [(keep_d, None)] + [(value, 1) for value in come]
        x_other += [(across(keep_x, 0, 2), None)] + [(v, None) for v in exchange(sends, 2)]
        x_block, d_block = x_next, d_next
        if s == 1:
            hid, *factors = gate_up(order, x_pieces[: 2 * columns], w_stack, capacity)
            hids.append(hid)
        if s == 3:
            dx, send, keep = backward(
                order, place, dy_pieces[: 2 * columns], *factors, w_stack, columns, 0, None,
                dx_shape, [],
            )
            acts_kept.append(keep)
            acts_come.append(across(send, 0, 2))
    picked = select_last(order, scales, hits, d_block, columns, [])
    dy_pieces += [(picked[0], None)] + [(value, None) for value in exchange(picked[1:], 0)]
    hid, *factors = gate_up(order, x_pieces[2 * columns :], w_stack, capacity, large_cost())
    hids.append(hid)
    send_other, keep_other, send_own, down_own = grad_down(
        order, place, hids, dy_pieces, width, []
    )
    dx, send, keep = backward(
        order, place, dy_pieces[2 * columns :], *factors, w_stack, columns, 2, dx, dx_shape,
        [value for value, _ in x_other[3 * columns :]],
    )
    acts_kept.append(keep)
    acts_come.append(across(send, 0, 2))
    returned = lax.all_to_all(dx, "expert", split_axis=0, concat_axis=0, tiled=True)
    summed = keep_other.astype(F32) + across(send_other, 0, 1).astype(F32)
    summed = summed.astype(BF16)
    down_y = across(summed, 0, 2)
    down_core = across(send_own, 0, 1)

    send, keep = grad_x(
        order, place, acts_kept + acts_come, x_pieces + x_other, width, [summed, down_core]
    )
    arrive(order, down_y)
    g_rows = sum_all(order, keep, across(send, 0, 1), [down_own, down_core, down_y])
    d_tokens = merge(order, all_hits, returned.reshape(experts * capacity, width))
    return d_tokens, g_rows[None]


def solution(mesh):
    return jax.shard_map(
        body,
        mesh=mesh,
        in_specs=(
            P(("expert", "replica"), None),
            P(("expert", "replica"), None),
            P(("expert", "replica"), None),
            P(("expert", "replica"), None),
            P("expert", None, None),
        ),
        out_specs=(P(("expert", "replica"), None), P("expert", "replica", None)),
        check_vma=False,
    )
```
